32 devices in a mesh: tok: 4 (over y, x), blk: 8 (over z, core).
Axes of the slice: x: 2, y: 2, z: 4, core: 2. Of those that a mesh axis runs over, the one named last changes fastest.
Arguments:
- states: bfloat16 [24, 512, 1024], P('blk', 'tok'), may hold values from -6 to 6
- gain_attn: bfloat16 [1024], replicated, may hold values from 0.099609375 to 1.8984375
- w_qkv: bfloat16 [1024, 3072], replicated, may hold values from -4 to 4
- w_out: bfloat16 [1024, 1024], replicated, may hold values from -0.1875 to 0.1875
- cache_prev: bfloat16 [24, 1536, 2, 1024], P('blk', 'tok'), may hold values from -6 to 6
- cached_blocks: int32 [24], P('blk'), may hold values from 0 to 12, as said below
- gain_moe: bfloat16 [1024], replicated, may hold values from 0.099609375 to 1.8984375
- w_router: bfloat16 [1024, 8], replicated, may hold values from -0.1875 to 0.1875
- routes: int32 [4, 24, 128, 2], P('tok', 'blk'), may hold values from 0 to 7, all different within a row; in each aligned block of 384 rows (0 to 383, 384 to 767, ..., all dimensions but the last counted through in order) at most 120 rows name the same one
- w_gate_up: bfloat16 [8, 2, 1024, 2816], P('blk', None, None, 'tok'), may hold values from -0.1875 to 0.1875
- w_down: bfloat16 [8, 2816, 1024], P('blk', 'tok'), may hold values from -0.109375 to 0.109375
Outputs:
- out_hidden: bfloat16 [24, 512, 1024], P('blk', 'tok')
- decode_cache: bfloat16 [24, 2048, 2, 1024], P('blk', None, None, 'tok')
The draws below stay inside these ranges and needn't reach their ends.
Inputs may be any that keep to these rules, and one draw needn't show every extreme that they name: `cached_blocks`: some request holds all 12 blocks. `routes`: among the 384 tokens of one device, no expert is named more than 120 times.
All inputs are finite; a program needn't handle non-finite values.
Results may differ from the reference program's by a relative error of at most 0.0065.
Values may be sent and summed in bfloat16 or wider, within the bound.
No kernel may reach another device: no remote copies, remote signals or barrier semaphores. Data moves between devices by JAX's collectives and lax.ppermute only.
A program may use at most 192 MiB of HBM per device.

```python
import math
import jax
import jax.numpy as jnp
import numpy as np
from jax import lax

D = 1024
HEADS = 16
HEAD_DIM = 64
FF = 2816
EXPERTS = 8
TOP = 2
BLOCK = 128
GROUP = 512
CACHE_BLOCKS = 12
REQS = 24
GROUP_DEV = 128
TOK_DEV = 384
CACHE_LEN = 1536
CAPACITY = 120
N_TOK = 4
N_BLK = 8


def draw_w_qkv(key, part):
    base = jax.random.normal(key, (D, 3 * D), jnp.float32) * D ** (-0.5)
    return jnp.clip(base, -4.0, 4.0).astype(jnp.bfloat16)


def draw_cached_blocks(key, part):
    first_key = jax.random.fold_in(key, 11)
    second_key = jax.random.fold_in(key, 23)
    counts = jax.random.randint(first_key, (REQS,), 0, CACHE_BLOCKS + 1)
    picked = jax.random.randint(second_key, (), 0, REQS)
    return jnp.where(jnp.arange(REQS) == picked, CACHE_BLOCKS, counts).astype(jnp.int32)


def block_scale(key, shape, cuts, least, largest):
    loudness, own = 1.0, jax.random.fold_in(key, 6)
    for axis_at, shards_of in cuts:
        heights = jnp.exp(jax.random.uniform(jax.random.fold_in(own, axis_at), (shards_of,), jnp.float32, least / len(cuts), largest / len(cuts)))
        loudness = loudness * jnp.repeat(heights, shape[axis_at] // shards_of).reshape([-1 if axis == axis_at else 1 for axis in range(len(shape))])
    return loudness


def shared_out(key, own, number, rows, count, top, reach, slope):
    order = jax.random.permutation(key, count)
    crowded, common = shares(count, rows * top, reach, slope, True), shares(count, rows * top, reach, slope, False)
    places = jnp.arange(count)

    def named(sizes, rotation):
        used = int((sizes > 0).sum())
        fixed = max(1, used // 4)
        passed = fixed + (places - fixed + rotation * (used - fixed)) % max(1, count - fixed)
        return jnp.zeros((count,), jnp.int32).at[order[jnp.where(places < fixed, places, passed)]].set(jnp.asarray(sizes, jnp.int32))

    sizes = jnp.where(number % 4 == 0, named(crowded, number // 4), named(common, number - number // 4 - 1))
    mixed = jax.random.permutation(jax.random.fold_in(own, 3), count)
    source_of, sink = mixed[0:count // 2 * 2:2], mixed[1:count // 2 * 2:2]
    room = jnp.minimum(sizes[source_of] - 1, reach - sizes[sink]) // 2
    room = jnp.where((source_of == order[0]) | (sink == order[0]) | (sizes[sink] == 0), 0, jnp.maximum(room, 0))
    passed = jax.random.randint(jax.random.fold_in(own, 4), (count // 2,), 0, 1 << 20) % (room + 1)
    sizes = sizes.at[source_of].add(-passed).at[sink].add(passed)
    members = jnp.searchsorted(jnp.cumsum(sizes), jnp.arange(rows * top), side="right").astype(jnp.int32)
    table = members.reshape(top, rows).T
    table = table[jax.random.permutation(jax.random.fold_in(own, 1), rows)]
    rotation = jax.random.randint(jax.random.fold_in(own, 2), (rows, 1), 0, top)
    return jnp.take_along_axis(table, (jnp.arange(top)[None, :] + rotation) % top, axis=1)


def shares(amount, total, bound, skew, full):
    portions = [(1 << 20) // math.isqrt(standing ** skew) + 1 for standing in range(1, amount + 1)]
    largest = bound if full else min(bound, max(-(-total // amount), total * portions[0] // sum(portions)))
    least = 1 if total - largest >= amount - 1 else 0
    given, rest = [largest] + [least] * (amount - 1), total - largest - least * (amount - 1)
    while rest > 0:
        candidates = [i for i in range(1, amount) if given[i] < largest] or [i for i in range(1, amount) if given[i] < bound]
        mass, budget = sum([portions[i] for i in candidates]), rest
        for i in candidates:
            more = min(bound - given[i], max(1, budget * portions[i] // mass), rest)
            given[i] = given[i] + more
            rest = rest - more
    return np.array(given)


def scatter_about(key, extent, deviation, most, pieces=(), held_as=jnp.bfloat16):
    values = jax.random.normal(key, extent, jnp.float32) * deviation
    if len(pieces) > 0:
        values = block_scale(key, extent, pieces, -0.22, 0.18) * values
    return jnp.clip(values, min=-most, max=most).astype(held_as)


def setup_inputs(seed: int = 0) -> dict:
    keys = jax.random.split(jax.random.key(seed), 12)
    states = scatter_about(keys[0], (REQS, GROUP, D), 1.0, 6.0, ((0, 8), (1, 4)))
    gain_attn = jnp.clip(1.0 + 0.18 * jax.random.normal(keys[1], (D,), jnp.float32), 0.099609375, 1.8984375).astype(jnp.bfloat16)
    w_qkv = draw_w_qkv(jax.random.fold_in(keys[11], 71), 0)
    w_out = scatter_about(keys[3], (D, D), D ** -0.5, 0.1875)
    cache_prev = scatter_about(keys[4], (REQS, CACHE_LEN, 2, D), 1.0, 6.0, ((0, 8), (1, 4)))
    cached_blocks = draw_cached_blocks(jax.random.fold_in(keys[11], 71), 0)
    gain_moe = jnp.clip(1.0 + 0.18 * jax.random.normal(keys[6], (D,), jnp.float32), 0.099609375, 1.8984375).astype(jnp.bfloat16)
    w_router = scatter_about(keys[7], (D, EXPERTS), D ** -0.5, 0.1875)
    routes_keys = jax.random.split(jax.random.fold_in(keys[8], 1), N_TOK * REQS * GROUP_DEV // TOK_DEV)
    routes_turns = jax.random.permutation(jax.random.fold_in(keys[8], 3), N_TOK * REQS * GROUP_DEV // TOK_DEV)
    routes = jax.vmap(lambda own, number: shared_out(jax.random.fold_in(keys[8], 2), own, number, TOK_DEV, EXPERTS, TOP, CAPACITY, 2))(routes_keys, routes_turns).reshape((N_TOK, REQS, GROUP_DEV, TOP))
    w_gate_up = scatter_about(keys[9], (EXPERTS, 2, D, FF), D ** -0.5, 0.1875, ((0, 8), (3, 4)))
    w_down = scatter_about(keys[10], (EXPERTS, FF, D), FF ** -0.5, 0.109375, ((0, 8), (1, 4)))
    return {"states": states, "gain_attn": gain_attn, "w_qkv": w_qkv, "w_out": w_out, "cache_prev": cache_prev, "cached_blocks": cached_blocks, "gain_moe": gain_moe, "w_router": w_router, "routes": routes, "w_gate_up": w_gate_up, "w_down": w_down}


def normalize(values, gain):
    return values * lax.rsqrt(lax.optimization_barrier(jnp.mean(values * values, -1, keepdims=True)) + 1e-06) * gain.astype(jnp.float32)

def reference(states, gain_attn, w_qkv, w_out, cache_prev, cached_blocks, gain_moe, w_router, routes, w_gate_up, w_down):
    flat_states = states.reshape(REQS * GROUP, D).astype(jnp.float32)
    normed = normalize(flat_states, gain_attn).astype(jnp.bfloat16)
    projected = jnp.dot(normed, w_qkv, preferred_element_type=jnp.float32).astype(jnp.bfloat16)
    projected = projected.reshape(REQS, GROUP, 3, HEADS, HEAD_DIM)
    lengths = (cached_blocks * BLOCK).astype(jnp.int32)

    def one_request(inputs):
        fresh, cached, length = inputs
        old_heads = cached.reshape(CACHE_LEN, 2, HEADS, HEAD_DIM)
        query = fresh[:, 0].astype(jnp.float32)
        key_all = jnp.concatenate([old_heads[:, 0], fresh[:, 1]], axis=0).astype(jnp.float32)
        value_all = jnp.concatenate([old_heads[:, 1], fresh[:, 2]], axis=0).astype(jnp.float32)
        scores = jnp.einsum('qhd,khd->hqk', query, key_all) * HEAD_DIM ** (-0.5)
        key_pos = jnp.arange(CACHE_LEN + GROUP)
        query_pos = jnp.arange(GROUP)
        valid = jnp.where(key_pos[None, :] < CACHE_LEN, key_pos[None, :] < length, key_pos[None, :] - CACHE_LEN <= query_pos[:, None])
        scores = jnp.where(valid[None], scores, -1e+30)
        highest = lax.optimization_barrier(jnp.max(scores, axis=-1, keepdims=True))
        weights = jnp.exp(scores - highest)
        weights = (weights / lax.optimization_barrier(jnp.sum(weights, axis=-1, keepdims=True))).astype(jnp.bfloat16)
        attended = jnp.einsum('hqk,khd->qhd', weights.astype(jnp.float32), value_all).astype(jnp.bfloat16).reshape(GROUP, D)
        keep = jnp.arange(CACHE_LEN)[:, None, None] < length
        base = jnp.concatenate([jnp.where(keep, cached, jnp.zeros((), jnp.bfloat16)), jnp.zeros((GROUP, 2, D), jnp.bfloat16)], axis=0)
        new_rows = fresh[:, 1:3].reshape(GROUP, 2, D)
        cache_out = lax.dynamic_update_slice(base, new_rows, (length, length * 0, length * 0))
        return (attended, cache_out)
    attended, decode_cache = lax.map(one_request, (projected, cache_prev, lengths))
    residual = flat_states + jnp.dot(attended.reshape(REQS * GROUP, D), w_out, preferred_element_type=jnp.float32)
    normed_moe = normalize(residual, gain_moe).astype(jnp.bfloat16)
    logits = jnp.dot(normed_moe, w_router, preferred_element_type=jnp.float32)
    route_full = jnp.transpose(routes, (1, 0, 2, 3)).reshape(REQS * GROUP, TOP)
    chosen = lax.optimization_barrier(jnp.sum(jnp.where(route_full[:, :, None] == jnp.arange(EXPERTS)[None, None, :], logits[:, None, :], 0.0), axis=-1))
    gates = jax.nn.sigmoid(chosen)
    assigned = route_full.reshape(-1)
    total_rows = REQS * GROUP * TOP
    padded = jnp.concatenate([normed_moe, jnp.zeros((1, D), jnp.bfloat16)], axis=0)
    slot_rows = N_TOK * N_BLK * CAPACITY

    def one_expert(collected, expert):
        chosen_rows = jnp.nonzero(assigned == expert, size=slot_rows, fill_value=total_rows)[0].astype(jnp.int32)
        token_rows = jnp.where(chosen_rows < total_rows, chosen_rows // TOP, REQS * GROUP).astype(jnp.int32)
        rows_in = padded[token_rows]
        gate_part = jnp.dot(rows_in, w_gate_up[expert, 0], preferred_element_type=jnp.float32)
        up_part = jnp.dot(rows_in, w_gate_up[expert, 1], preferred_element_type=jnp.float32)
        hidden = (jax.nn.gelu(gate_part, approximate=True) * up_part).astype(jnp.bfloat16)
        result = jnp.dot(hidden, w_down[expert], preferred_element_type=jnp.float32).astype(jnp.bfloat16)
        return (collected.at[chosen_rows].set(result, mode='drop'), None)
    collected = lax.scan(one_expert, jnp.zeros((total_rows, D), jnp.bfloat16), jnp.arange(EXPERTS, dtype=jnp.int32))[0]
    mixed = lax.optimization_barrier(jnp.sum(collected.reshape(REQS * GROUP, TOP, D).astype(jnp.float32) * gates[:, :, None], axis=1))
    out_hidden = (residual + mixed).astype(jnp.bfloat16).reshape(REQS, GROUP, D)
    return (out_hidden, decode_cache)
```

```python
import functools
import math

import jax
import jax.numpy as jnp
from jax import lax
from jax.experimental import pallas as pl
from jax.experimental.pallas import tpu as pltpu
from jax.sharding import PartitionSpec as P

HEAD_DIM = 64
TOP = 2
BLOCK = 128
CHUNK = 256
LANES = 128
HIDDEN_SCORE = -1e30
EPS = 1e-06
VMEM_BYTES = 56 * 1024 * 1024
ANY = pl.BlockSpec(memory_space=pl.ANY)


def normalize(values, gain):
    return (
        values
        * lax.rsqrt(jnp.mean(values * values, -1, keepdims=True) + EPS)
        * gain.astype(jnp.float32)
    )


def after(value, *others):
    return lax.optimization_barrier((value, others))[0]


def dot(left, right):
    return jnp.dot(left, right, preferred_element_type=jnp.float32)


def dot_nt(left, right):
    return lax.dot_general(left, right, (((1,), (1,)), ((), ())), preferred_element_type=jnp.float32)


def iota(shape, dim):
    return lax.broadcasted_iota(jnp.int32, shape, dim)


def attention_kernel(parts, first, chained, info, *refs):
    fresh_in, cached_in, refs = refs[:parts], refs[parts : 2 * parts], refs[2 * parts :]
    if chained:
        refs = refs[1:]
    outs, cache_out, refs = refs[:parts], refs[parts], refs[parts + 1 :]
    q_s, k_s, v_s, s_s, m_s, l_s, acc_s, o_s, fresh_s, zero_s, fresh_sem, old_sem = refs
    per, width = outs[0].shape
    group = per * parts
    held = cached_in[0].shape[1]
    unit = zero_s.shape[0]
    heads = width // HEAD_DIM
    me = info[0]
    req = first + pl.program_id(0)
    length = info[1 + req] * BLOCK
    zero_s[...] = jnp.zeros_like(zero_s)
    pick_row = iota((unit, 2 * unit), 0) * 2
    pick_col = iota((unit, 2 * unit), 1)
    pick_k = (pick_col == pick_row).astype(jnp.bfloat16)
    pick_v = (pick_col == pick_row + 1).astype(jnp.bfloat16)

    for d in range(parts):
        row = pl.multiple_of((me ^ d) * per, per)
        key, value = fresh_in[d][:, width : 2 * width], fresh_in[d][:, 2 * width :]
        q_s[pl.ds(row, per), :] = fresh_in[d][:, :width]
        k_s[pl.ds(row, per), :] = key
        v_s[pl.ds(row, per), :] = value
        fresh_s[d] = jnp.stack([key, value], axis=1)
        pltpu.make_async_copy(
            fresh_s.at[d], cache_out.at[req, pl.ds(length + row, per)], fresh_sem.at[d]
        ).start()
        for i in range(held // unit):
            at = pl.multiple_of((me ^ d) * held + i * unit, unit)
            block = cached_in[d].at[0, pl.ds(i * unit, unit)]
            sem = old_sem.at[d * (held // unit) + i]

            @pl.when(at < length)
            def _():
                pltpu.make_async_copy(block, cache_out.at[req, pl.ds(at, unit)], sem).start()
                pairs = block[...].reshape(2 * unit, width)
                k_s[pl.ds(group + at, unit), :] = dot(pick_k, pairs).astype(jnp.bfloat16)
                v_s[pl.ds(group + at, unit), :] = dot(pick_v, pairs).astype(jnp.bfloat16)

            @pl.when(at >= length)
            def _():
                pltpu.make_async_copy(
                    zero_s, cache_out.at[req, pl.ds(at + group, unit)], sem
                ).start()

    tail = pl.ds(pl.multiple_of(group + length, BLOCK), BLOCK)
    k_s[tail, :] = jnp.zeros((BLOCK, width), jnp.bfloat16)
    v_s[tail, :] = jnp.zeros((BLOCK, width), jnp.bfloat16)
    chunks = (length + CHUNK - 1) // CHUNK
    own = group // CHUNK
    scale = HEAD_DIM ** (-0.5) * math.log2(math.e)

    def fold(values):
        folded = values[:, :LANES]
        for at in range(LANES, CHUNK, LANES):
            folded = jnp.maximum(folded, values[:, at : at + LANES])
        return folded

    def one_head(h, carry):
        lane_head = iota((group, width), 1) // HEAD_DIM
        query = jnp.where(lane_head == h, q_s[...], jnp.zeros((), jnp.bfloat16))
        m_s[...] = jnp.full(m_s.shape, HIDDEN_SCORE, jnp.float32)
        for c in range(own):
            top = c * CHUNK
            scores = dot_nt(query[top:], k_s[top : top + CHUNK, :])
            rows = group - top
            visible = iota((rows, CHUNK), 1) <= iota((rows, CHUNK), 0)
            scores = jnp.where(visible, scores, HIDDEN_SCORE)
            s_s[c, top:, :] = scores
            m_s[top:, :] = jnp.maximum(m_s[top:, :], fold(scores))

        def score_chunk(c, carry):
            start = pl.multiple_of(c * CHUNK, CHUNK)
            scores = dot_nt(query, k_s[pl.ds(group + start, CHUNK), :])
            scores = jnp.where(iota((1, CHUNK), 1) + start < length, scores, HIDDEN_SCORE)
            s_s[own + c] = scores
            m_s[...] = jnp.maximum(m_s[...], fold(scores))
            return carry

        lax.fori_loop(0, chunks, score_chunk, 0)
        highest = jnp.max(m_s[...], axis=-1, keepdims=True) * scale
        m_s[...] = jnp.broadcast_to(highest, m_s.shape)

        def weigh(scores, rows):
            highest = m_s[rows:, :]
            parts_ = [
                jnp.exp2(scores[:, at : at + LANES] * scale - highest)
                for at in range(0, CHUNK, LANES)
            ]
            total = parts_[0]
            for part in parts_[1:]:
                total = total + part
            return jnp.concatenate([p.astype(jnp.bfloat16) for p in parts_], axis=1), total

        for c in range(own):
            top = c * CHUNK
            weights, total = weigh(s_s[c, top:, :], top)
            product = dot(weights, v_s[top : top + CHUNK, :])
            if c == 0:
                l_s[...] = total
                acc_s[...] = product
            else:
                l_s[top:, :] += total
                acc_s[top:, :] += product

        def value_chunk(c, carry):
            start = pl.multiple_of(c * CHUNK, CHUNK)
            weights, total = weigh(s_s[own + c], 0)
            l_s[...] += total
            acc_s[...] += dot(weights, v_s[pl.ds(group + start, CHUNK), :])
            return carry

        lax.fori_loop(0, chunks, value_chunk, 0)
        result = acc_s[...] / jnp.sum(l_s[...], axis=-1, keepdims=True)
        o_s[...] = jnp.where(lane_head == h, result, o_s[...])
        return carry

    o_s[...] = jnp.zeros_like(o_s)
    lax.fori_loop(0, heads, one_head, 0)
    for d in range(parts):
        row = pl.multiple_of((me ^ d) * per, per)
        outs[d][...] = o_s[pl.ds(row, per), :].astype(jnp.bfloat16)
    for d in range(parts):
        pltpu.make_async_copy(
            fresh_s.at[d], cache_out.at[req, pl.ds(length, per)], fresh_sem.at[d]
        ).wait()
        for i in range(held // unit):
            pltpu.make_async_copy(
                zero_s, cache_out.at[req, pl.ds(0, unit)], old_sem.at[d * (held // unit) + i]
            ).wait()


def attend(info, fresh, cached, first, cache_so_far, requests):
    parts = len(fresh)
    count, held, _, width = cached[0].shape
    per = fresh[0].shape[1]
    group, cache_full = per * parts, held * parts
    unit = math.gcd(held, BLOCK)
    heads = width // HEAD_DIM
    chained = cache_so_far is not None
    slots = (group + cache_full) // CHUNK
    rows = group + cache_full + BLOCK
    in_specs = [pl.BlockSpec((None, per, 3 * width), lambda r, _: (first + r, 0, 0))] * parts
    in_specs += [pl.BlockSpec((1, held, 2, width), lambda r, _: (r, 0, 0, 0))] * parts
    operands = [info, *fresh, *cached]
    aliases = {}
    if chained:
        in_specs.append(ANY)
        aliases = {len(operands): parts}
        operands.append(cache_so_far)
    out = pl.pallas_call(
        functools.partial(attention_kernel, parts, first, chained),
        grid_spec=pltpu.PrefetchScalarGridSpec(
            num_scalar_prefetch=1,
            grid=(count,),
            in_specs=in_specs,
            out_specs=[pl.BlockSpec((None, per, width), lambda r, _: (r, 0, 0))] * parts + [ANY],
            scratch_shapes=[
                pltpu.VMEM((group, width), jnp.bfloat16),
                pltpu.VMEM((rows, width), jnp.bfloat16),
                pltpu.VMEM((rows, width), jnp.bfloat16),
                pltpu.VMEM((slots, group, CHUNK), jnp.float32),
                pltpu.VMEM((group, LANES), jnp.float32),
                pltpu.VMEM((group, LANES), jnp.float32),
                pltpu.VMEM((group, width), jnp.float32),
                pltpu.VMEM((group, width), jnp.float32),
                pltpu.VMEM((parts, per, 2, width), jnp.bfloat16),
                pltpu.VMEM((unit, 2, width), jnp.bfloat16),
                pltpu.SemaphoreType.DMA((parts,)),
                pltpu.SemaphoreType.DMA((cache_full // unit,)),
            ],
        ),
        out_shape=[jax.ShapeDtypeStruct((count, per, width), jnp.bfloat16)] * parts
        + [jax.ShapeDtypeStruct((requests, cache_full + group, 2, width), jnp.bfloat16)],
        input_output_aliases=aliases,
        cost_estimate=pl.CostEstimate(
            flops=count * heads * group * (cache_full + group) * width * 4,
            bytes_accessed=count * (cache_full + group) * width * 8,
            transcendentals=count * heads * group * (cache_full + group),
        ),
        compiler_params=pltpu.CompilerParams(vmem_limit_bytes=VMEM_BYTES),
        name="attention",
    )(*operands)
    return list(out[:parts]), out[parts]


def project_kernel(groups, parts, info, states, w_out, gain, w_router, slots, *refs):
    pieces, refs = refs[: groups * parts], refs[groups * parts :]
    residual_ref, scores_ref, outgoing = refs[0], refs[1], refs[2:]
    me = info[0]
    width = pieces[0].shape[-1]
    per = pieces[0].shape[-2]
    tokens = states.shape[0]
    capacity = outgoing[0].shape[0]
    total = []
    for g in range(groups):
        rows = pieces[g * parts].shape[0] * per
        value = None
        for d in range(parts):
            piece = pieces[g * parts + d][...].reshape(rows, width)
            term = dot(piece, w_out[pl.ds(pl.multiple_of((me ^ d) * width, width), width), :])
            value = term if value is None else value + term
        total.append(value)
    residual = states[...].astype(jnp.float32) + jnp.concatenate(total, axis=0)
    residual_ref[...] = residual
    normed = normalize(residual, gain[...]).astype(jnp.bfloat16)
    scores_ref[...] = jax.nn.sigmoid(dot(normed, w_router[...]))
    for e in range(len(outgoing)):
        row = iota((capacity, tokens), 0) + e * capacity
        chosen = (row == slots[0:1, :]) | (row == slots[1:2, :])
        outgoing[e][...] = dot(chosen.astype(jnp.bfloat16), normed).astype(jnp.bfloat16)


def project(info, states, w_out, gain, w_router, slots, pieces, capacity):
    groups, parts = len(pieces), len(pieces[0])
    tokens, width = states.shape
    experts = w_router.shape[1]
    flat = [piece for group in pieces for piece in group]
    whole = pl.BlockSpec(memory_space=pltpu.VMEM)
    out = pl.pallas_call(
        functools.partial(project_kernel, groups, parts),
        in_specs=[pl.BlockSpec(memory_space=pltpu.SMEM)] + [whole] * (5 + len(flat)),
        out_specs=[whole] * (2 + experts),
        out_shape=[
            jax.ShapeDtypeStruct((tokens, width), jnp.float32),
            jax.ShapeDtypeStruct((tokens, experts), jnp.float32),
        ]
        + [jax.ShapeDtypeStruct((capacity, width), jnp.bfloat16)] * experts,
        cost_estimate=pl.CostEstimate(
            flops=2 * tokens * width * (width + experts * capacity),
            bytes_accessed=2 * width * (width + 4 * tokens + experts * capacity),
            transcendentals=0,
        ),
        compiler_params=pltpu.CompilerParams(vmem_limit_bytes=VMEM_BYTES),
        name="project",
    )(info, states, w_out, gain, w_router, slots, *flat)
    return out[0], out[1], list(out[2:])


def expert_kernel(shards, has_sum, pieces, rows_ref, *refs):
    if has_sum:
        sum_ref, refs = refs[0], refs[1:]
    halves, refs = refs[: 2 * shards], refs[2 * shards :]
    outs, (w_s, sems) = refs[:-2], refs[-2:]
    step = pl.program_id(0)
    half = halves[0].shape[1]

    def fetch(s, k):
        return pltpu.make_async_copy(
            halves[2 * s + k], w_s.at[s, :, pl.ds(k * half, half), :], sems.at[s, k]
        )

    @pl.when(step == 0)
    def _():
        for s in range(shards):
            for k in range(2):
                fetch(s, k).start()

    rows = rows_ref[...]
    total = sum_ref[...] if has_sum else None
    for s in range(shards):

        @pl.when(step == 0)
        def _():
            for k in range(2):
                fetch(s, k).wait()

        gate = dot_nt(rows, w_s[s, 0])
        up = dot_nt(rows, w_s[s, 1])
        hidden = (jax.nn.gelu(gate, approximate=True) * up).astype(jnp.bfloat16)
        term = dot(hidden, w_s[s, 2])
        total = term if total is None else total + term
    if not pieces:
        outs[0][...] = total
    else:
        capacity = outs[0].shape[0]
        at_once = rows.shape[0] // capacity
        value = total.astype(jnp.bfloat16)
        for i in range(len(outs)):

            @pl.when(step == i // at_once)
            def _():
                start = i % at_once * capacity
                outs[i][...] = value[start : start + capacity]


def expert(rows, total, halves, pieces):
    count, width = rows.shape
    shards = len(halves) // 2
    half = halves[0].shape[1]
    capacity = count // pieces if pieces else 16
    at_once = max(
        n for n in range(1, count + 1)
        if count % n == 0 and n <= 256 and n % 16 == 0 and n % capacity == 0
    )
    block = pl.BlockSpec((at_once, width), lambda i: (i, 0))
    has_sum = total is not None
    if pieces:
        out_specs = [pl.BlockSpec((capacity, width), lambda i: (0, 0))] * pieces
        out_shape = [jax.ShapeDtypeStruct((capacity, width), jnp.bfloat16)] * pieces
    else:
        out_specs, out_shape = [block], [jax.ShapeDtypeStruct((count, width), jnp.float32)]
    out = pl.pallas_call(
        functools.partial(expert_kernel, shards, has_sum, pieces),
        grid=(count // at_once,),
        in_specs=[block] + [block] * has_sum + [ANY] * len(halves),
        out_specs=out_specs,
        out_shape=out_shape,
        input_output_aliases={1: 0} if has_sum and not pieces else {},
        scratch_shapes=[
            pltpu.VMEM((shards, 3, 2 * half, width), jnp.bfloat16),
            pltpu.SemaphoreType.DMA((shards, 2)),
        ],
        cost_estimate=pl.CostEstimate(
            flops=2 * 6 * count * width * half * shards,
            bytes_accessed=shards * 12 * half * width + count * width * 8,
            transcendentals=count * 2 * half * shards,
        ),
        compiler_params=pltpu.CompilerParams(vmem_limit_bytes=VMEM_BYTES),
        name="experts",
    )(rows, *([total] if has_sum else []), *halves)
    return list(out)


def combine_kernel(residual, scores, routes, slots, *refs):
    returned, out = refs[:-1], refs[-1]
    tokens, experts = scores.shape
    capacity = returned[0].shape[0]
    mixed = None
    for k in range(TOP):
        gate = jnp.sum(
            jnp.where(iota((tokens, experts), 1) == routes[:, k : k + 1], scores[...], 0.0),
            axis=-1,
            keepdims=True,
        )
        picked = None
        for e in range(len(returned)):
            column = iota((tokens, capacity), 1) + e * capacity
            chosen = (column == slots[:, k : k + 1]).astype(jnp.bfloat16)
            term = dot(chosen, returned[e][...])
            picked = term if picked is None else picked + term
        term = picked * gate
        mixed = term if mixed is None else mixed + term
    out[...] = (residual[...] + mixed).astype(jnp.bfloat16)


def combine(residual, scores, routes, slots, returned):
    tokens, width = residual.shape
    whole = pl.BlockSpec(memory_space=pltpu.VMEM)
    return pl.pallas_call(
        combine_kernel,
        in_specs=[whole] * (4 + len(returned)),
        out_specs=whole,
        out_shape=jax.ShapeDtypeStruct((tokens, width), jnp.bfloat16),
        cost_estimate=pl.CostEstimate(
            flops=2 * TOP * tokens * width * len(returned) * returned[0].shape[0],
            bytes_accessed=width * (tokens * 6 + 2 * len(returned) * returned[0].shape[0]),
            transcendentals=0,
        ),
        compiler_params=pltpu.CompilerParams(vmem_limit_bytes=VMEM_BYTES),
        name="combine",
    )(residual, scores, routes, slots, *returned)


def body(
    states,
    gain_attn,
    w_qkv,
    w_out,
    cache_prev,
    cached_blocks,
    gain_moe,
    w_router,
    routes,
    w_gate_up,
    w_down,
):
    toks, blks = lax.axis_size("tok"), lax.axis_size("blk")
    tok, blk = lax.axis_index("tok"), lax.axis_index("blk")
    tok_low, blk_low = tok % 2, blk % 2
    requests, per, width = states.shape
    tokens = requests * per
    local = width // toks
    experts = w_router.shape[1]
    capacity = tokens * TOP * 5 // (4 * experts)
    info = jnp.concatenate([tok[None].astype(jnp.int32), cached_blocks])
    flat_states = states.reshape(tokens, width)

    def over_tok(value, d):
        return lax.ppermute(value, "tok", [(i, i ^ d) for i in range(toks)])

    def other_core(value):
        return lax.ppermute(value, "blk", [(i, i ^ 1) for i in range(blks)])

    gathered = [flat_states] + [None] * (toks - 1)
    for d in range(2, toks, 2):
        gathered[d] = over_tok(flat_states, d)
    gathered[1] = over_tok(flat_states, 1)
    for d in range(2, toks, 2):
        gathered[d + 1] = over_tok(gathered[d], 1)

    def heads_of(r, d):
        return lax.dynamic_slice_in_dim(cache_prev[r : r + 1], (tok ^ d) * local, local, axis=3)

    cached = []
    for r in range(requests):
        moved = [heads_of(r, d) for d in range(toks)]
        if r >= 1:
            moved = list(after(tuple(moved), gathered[-1], *(c[-1] for c in cached[: r - 1])))
        cached.append([moved[0]] + [over_tok(moved[d], d) for d in range(1, toks)])

    gate_up = w_gate_up[0].transpose(0, 2, 1)
    stacked = jnp.concatenate([gate_up, w_down], axis=0)
    half = stacked.shape[1] // 2
    stacked = stacked.reshape(3, 2, half, width)
    kept = lax.dynamic_index_in_dim(stacked, blk_low, axis=1, keepdims=False)
    given = lax.dynamic_index_in_dim(stacked, 1 - blk_low, axis=1, keepdims=False)
    taken = other_core(given)
    stays = tok_low == blk_low
    mine = jnp.where(stays, kept, taken)
    leaving = jnp.where(stays, taken, kept)

    w_local = lax.dynamic_slice_in_dim(
        w_qkv.reshape(width, 3, toks, local), tok, 1, axis=2
    ).reshape(width, 3 * local)
    fresh = []
    for piece in gathered:
        normed = normalize(piece.astype(jnp.float32), gain_attn).astype(jnp.bfloat16)
        fresh.append(dot(normed, w_local).astype(jnp.bfloat16).reshape(requests, per, 3 * local))

    route_flat = routes.reshape(tokens, TOP)
    assigned = route_flat.reshape(-1) ^ blk
    one_hot = (assigned[:, None] == jnp.arange(experts)[None, :]).astype(jnp.int32)
    ranks = jnp.sum(one_hot * (jnp.cumsum(one_hot, axis=0) - 1), axis=1)
    slots = (assigned * capacity + ranks).reshape(tokens, TOP)

    back, decode_cache = [], None
    for r in range(requests):
        attended, decode_cache = attend(info, fresh, cached[r], r, decode_cache, requests)
        back.append([attended[0]] + [over_tok(attended[d], d) for d in range(1, toks)])

    mine, leaving = after((mine, leaving), cached[max(0, requests - 2)][-1])
    shards = [mine, over_tok(leaving, 1)]
    for d in range(2, toks, 2):
        shards.append(over_tok(mine, d))
    for d in range(2, toks, 2):
        shards.append(over_tok(shards[1], d))
    swapped = [other_core(shard) for shard in shards]

    residual, scores, outgoing = project(
        info, flat_states, w_out, gain_moe.reshape(1, width), w_router, slots.T, back, capacity
    )

    def pairs(e):
        found = []
        for t in range(toks):
            for b in range(blks):
                to = b ^ e
                target = (t // 2 * 2 + to % 2) * blks + to // 2 * 2 + t % 2
                found.append((t * blks + b, target))
        return found

    incoming = [
        lax.ppermute(outgoing[e], ("tok", "blk"), pairs(e)) for e in range(experts)
    ]
    rows = jnp.concatenate(incoming, axis=0)
    total = None
    lasts = len(shards) - (toks // 2 - 1)
    stages = [[0], list(range(1, lasts)), list(range(lasts, len(shards)))]
    for i, stage in enumerate(stages):
        halves = [value for s in stage for value in (shards[s], swapped[s])]
        out = expert(rows, total, halves, experts if i == len(stages) - 1 else 0)
        total = out[0]
    returned = [
        lax.ppermute(out[e], ("tok", "blk"), [(j, i) for i, j in pairs(e)])
        for e in range(experts)
    ]
    out_hidden = combine(residual, scores, route_flat, slots, returned)
    return (out_hidden.reshape(requests, per, width), decode_cache)


def solution(mesh):
    return jax.shard_map(
        body,
        mesh=mesh,
        in_specs=(
            P("blk", "tok", None),
            P(),
            P(),
            P(),
            P("blk", "tok", None, None),
            P("blk"),
            P(),
            P(),
            P("tok", "blk", None, None),
            P("blk", None, None, "tok"),
            P("blk", "tok", None),
        ),
        out_specs=(P("blk", "tok", None), P("blk", None, None, "tok")),
        check_vma=False,
    )
```

```python
import functools
import math

import jax
import jax.numpy as jnp
from jax import lax
from jax.experimental import pallas as pl
from jax.experimental.pallas import tpu as pltpu
from jax.sharding import PartitionSpec as P

HEAD_DIM = 64
TOP = 2
BLOCK = 128
CHUNK = 512
LANES = 128
HIDDEN_SCORE = -1e30
EPS = 1e-06
VMEM_BYTES = 56 * 1024 * 1024
ANY = pl.BlockSpec(memory_space=pl.ANY)


def normalize(values, gain):
    return (
        values
        * lax.rsqrt(jnp.mean(values * values, -1, keepdims=True) + EPS)
        * gain.astype(jnp.float32)
    )


def after(value, *others):
    return lax.optimization_barrier((value, others))[0]


def dot(left, right):
    return jnp.dot(left, right, preferred_element_type=jnp.float32)


def dot_nt(left, right):
    return lax.dot_general(left, right, (((1,), (1,)), ((), ())), preferred_element_type=jnp.float32)


def iota(shape, dim):
    return lax.broadcasted_iota(jnp.int32, shape, dim)


def attention_kernel(parts, first, chained, info, *refs):
    fresh_in, cached_in, refs = refs[:parts], refs[parts : 2 * parts], refs[2 * parts :]
    if chained:
        refs = refs[parts + 1 :]
    outs, cache_out, refs = refs[:parts], refs[parts], refs[parts + 1 :]
    q_s, k_s, v_s, s_s, m_s, l_s, acc_s, o_s, fresh_s, zero_s, fresh_sem, old_sem = refs
    per, width = outs[0].shape
    group = per * parts
    held = cached_in[0].shape[1]
    unit = zero_s.shape[0]
    heads = width // HEAD_DIM
    me = info[0]
    req = first + pl.program_id(0)
    length = info[1 + req] * BLOCK
    zero_s[...] = jnp.zeros_like(zero_s)
    pick_row = iota((unit, 2 * unit), 0) * 2
    pick_col = iota((unit, 2 * unit), 1)
    pick_k = (pick_col == pick_row).astype(jnp.bfloat16)
    pick_v = (pick_col == pick_row + 1).astype(jnp.bfloat16)

    for d in range(parts):
        row = pl.multiple_of((me ^ d) * per, per)
        key, value = fresh_in[d][:, width : 2 * width], fresh_in[d][:, 2 * width :]
        q_s[heads, pl.ds(row, per), :] = fresh_in[d][:, :width]
        k_s[pl.ds(row, per), :] = key
        v_s[pl.ds(row, per), :] = value
        fresh_s[d] = jnp.stack([key, value], axis=1)
        pltpu.make_async_copy(
            fresh_s.at[d], cache_out.at[req, pl.ds(length + row, per)], fresh_sem.at[d]
        ).start()
        for i in range(held // unit):
            at = pl.multiple_of((me ^ d) * held + i * unit, unit)
            block = cached_in[d].at[0, pl.ds(i * unit, unit)]
            sem = old_sem.at[d * (held // unit) + i]

            @pl.when(at < length)
            def _():
                pltpu.make_async_copy(block, cache_out.at[req, pl.ds(at, unit)], sem).start()
                pairs = block[...].reshape(2 * unit, width)
                k_s[pl.ds(group + at, unit), :] = dot(pick_k, pairs).astype(jnp.bfloat16)
                v_s[pl.ds(group + at, unit), :] = dot(pick_v, pairs).astype(jnp.bfloat16)

            @pl.when(at >= length)
            def _():
                pltpu.make_async_copy(
                    zero_s, cache_out.at[req, pl.ds(at + group, unit)], sem
                ).start()

    tail = pl.ds(pl.multiple_of(group + length, BLOCK), CHUNK)
    k_s[tail, :] = jnp.zeros((CHUNK, width), jnp.bfloat16)
    v_s[tail, :] = jnp.zeros((CHUNK, width), jnp.bfloat16)
    chunks = (length + CHUNK - 1) // CHUNK
    own = group // CHUNK
    scale = HEAD_DIM ** (-0.5) * math.log2(math.e)

    def fold(values):
        folded = values[:, :LANES]
        for at in range(LANES, CHUNK, LANES):
            folded = jnp.maximum(folded, values[:, at : at + LANES])
        return folded

    lane_head = iota((group, width), 1) // HEAD_DIM
    for h in range(heads):
        q_s[h] = jnp.where(lane_head == h, q_s[heads], jnp.zeros((), jnp.bfloat16))
    for h in range(heads):
        for c in range(own):
            top = c * CHUNK
            scores = dot_nt(q_s[h, top:, :], k_s[top : top + CHUNK, :])
            rows = group - top
            visible = iota((rows, CHUNK), 1) <= iota((rows, CHUNK), 0)
            scores = jnp.where(visible, scores, HIDDEN_SCORE)
            s_s[c, h, top:, :] = scores
            if c == 0:
                m_s[h] = fold(scores)
            else:
                m_s[h, top:, :] = jnp.maximum(m_s[h, top:, :], fold(scores))

    def score_chunk(c, carry):
        start = pl.multiple_of(c * CHUNK, CHUNK)
        keys = k_s[pl.ds(group + start, CHUNK), :]
        seen = iota((1, CHUNK), 1) + start < length
        for h in range(heads):
            scores = jnp.where(seen, dot_nt(q_s[h], keys), HIDDEN_SCORE)
            s_s[own + c, h] = scores
            m_s[h] = jnp.maximum(m_s[h], fold(scores))
        return carry

    lax.fori_loop(0, chunks, score_chunk, 0)
    for h in range(heads):
        highest = jnp.max(m_s[h], axis=-1, keepdims=True) * scale
        m_s[h] = jnp.broadcast_to(highest, (group, LANES))

    def weigh(c, h, rows):
        pieces = [
            jnp.exp2(s_s[c, h, rows:, at : at + LANES] * scale - m_s[h, rows:, :])
            for at in range(0, CHUNK, LANES)
        ]
        total = pieces[0]
        for piece in pieces[1:]:
            total = total + piece
        return jnp.concatenate([p.astype(jnp.bfloat16) for p in pieces], axis=1), total

    for h in range(heads):
        for c in range(own):
            top = c * CHUNK
            weights, total = weigh(c, h, top)
            product = dot(weights, v_s[top : top + CHUNK, :])
            if c == 0:
                l_s[h] = total
                acc_s[h] = product
            else:
                l_s[h, top:, :] += total
                acc_s[h, top:, :] += product

    def value_chunk(c, carry):
        start = pl.multiple_of(c * CHUNK, CHUNK)
        values = v_s[pl.ds(group + start, CHUNK), :]
        for h in range(heads):
            weights, total = weigh(own + c, h, 0)
            l_s[h] += total
            acc_s[h] += dot(weights, values)
        return carry

    lax.fori_loop(0, chunks, value_chunk, 0)
    result = None
    for h in range(heads):
        value = acc_s[h] / jnp.sum(l_s[h], axis=-1, keepdims=True)
        result = value if h == 0 else jnp.where(lane_head == h, value, result)
    o_s[...] = result
    for d in range(parts):
        row = pl.multiple_of((me ^ d) * per, per)
        outs[d][...] = o_s[pl.ds(row, per), :].astype(jnp.bfloat16)
    for d in range(parts):
        pltpu.make_async_copy(
            fresh_s.at[d], cache_out.at[req, pl.ds(length, per)], fresh_sem.at[d]
        ).wait()
        for i in range(held // unit):
            pltpu.make_async_copy(
                zero_s, cache_out.at[req, pl.ds(0, unit)], old_sem.at[d * (held // unit) + i]
            ).wait()


def attend(info, fresh, cached, first, so_far, requests):
    parts = len(fresh)
    count, held, _, width = cached[0].shape
    per = fresh[0].shape[1]
    group, cache_full = per * parts, held * parts
    unit = math.gcd(held, BLOCK)
    heads = width // HEAD_DIM
    chained = so_far is not None
    slots = (group + cache_full) // CHUNK
    rows = group + cache_full + CHUNK
    in_specs = [pl.BlockSpec((None, per, 3 * width), lambda r, _: (first + r, 0, 0))] * parts
    in_specs += [pl.BlockSpec((1, held, 2, width), lambda r, _: (r, 0, 0, 0))] * parts
    operands = [info, *fresh, *cached]
    aliases = {}
    if chained:
        in_specs += [ANY] * len(so_far)
        aliases = {len(operands) + i: i for i in range(len(so_far))}
        operands += so_far
    out = pl.pallas_call(
        functools.partial(attention_kernel, parts, first, chained),
        grid_spec=pltpu.PrefetchScalarGridSpec(
            num_scalar_prefetch=1,
            grid=(count,),
            in_specs=in_specs,
            out_specs=[pl.BlockSpec((None, per, width), lambda r, _: (first + r, 0, 0))] * parts + [ANY],
            scratch_shapes=[
                pltpu.VMEM((heads + 1, group, width), jnp.bfloat16),
                pltpu.VMEM((rows, width), jnp.bfloat16),
                pltpu.VMEM((rows, width), jnp.bfloat16),
                pltpu.VMEM((slots, heads, group, CHUNK), jnp.float32),
                pltpu.VMEM((heads, group, LANES), jnp.float32),
                pltpu.VMEM((heads, group, LANES), jnp.float32),
                pltpu.VMEM((heads, group, width), jnp.float32),
                pltpu.VMEM((group, width), jnp.float32),
                pltpu.VMEM((parts, per, 2, width), jnp.bfloat16),
                pltpu.VMEM((unit, 2, width), jnp.bfloat16),
                pltpu.SemaphoreType.DMA((parts,)),
                pltpu.SemaphoreType.DMA((cache_full // unit,)),
            ],
        ),
        out_shape=[jax.ShapeDtypeStruct((requests, per, width), jnp.bfloat16)] * parts
        + [jax.ShapeDtypeStruct((requests, cache_full + group, 2, width), jnp.bfloat16)],
        input_output_aliases=aliases,
        compiler_params=pltpu.CompilerParams(vmem_limit_bytes=VMEM_BYTES),
        name="attention",
    )(*operands)
    return list(out)


def inward_kernel(count, info, gain, *refs):
    weights, pieces, outs = refs[:3], refs[3 : 3 + count], refs[3 + count :]
    width = weights[0].shape[1]
    for piece, out in zip(pieces, outs):
        normed = normalize(piece[...].astype(jnp.float32), gain[...]).astype(jnp.bfloat16)
        for i in range(3):
            out[:, i * width : (i + 1) * width] = dot(normed, weights[i][...]).astype(jnp.bfloat16)


def inward(info, gain, w_qkv, pieces, toks):
    count = len(pieces)
    tokens, width = pieces[0].shape
    local = width // toks

    def columns(i):
        return pl.BlockSpec((width, local), lambda _, info: (0, i * toks + info[0]))

    whole = pl.BlockSpec(memory_space=pltpu.VMEM)
    return pl.pallas_call(
        functools.partial(inward_kernel, count),
        grid_spec=pltpu.PrefetchScalarGridSpec(
            num_scalar_prefetch=1,
            grid=(1,),
            in_specs=[whole] + [columns(i) for i in range(3)] + [whole] * count,
            out_specs=[whole] * count,
        ),
        out_shape=[jax.ShapeDtypeStruct((tokens, 3 * local), jnp.bfloat16)] * count,
        compiler_params=pltpu.CompilerParams(vmem_limit_bytes=VMEM_BYTES),
        name="inward",
    )(info, gain.reshape(1, width), w_qkv, w_qkv, w_qkv, *pieces)


def project_kernel(groups, parts, info, states, w_out, gain, w_router, slots, *refs):
    pieces, refs = refs[: groups * parts], refs[groups * parts :]
    residual_ref, scores_ref, outgoing = refs[0], refs[1], refs[2:]
    me = info[0]
    width = pieces[0].shape[-1]
    per = pieces[0].shape[-2]
    tokens = states.shape[0]
    capacity = outgoing[0].shape[0]
    total = []
    for g in range(groups):
        rows = pieces[g * parts].shape[0] * per
        value = None
        for d in range(parts):
            piece = pieces[g * parts + d][...].reshape(rows, width)
            term = dot(piece, w_out[pl.ds(pl.multiple_of((me ^ d) * width, width), width), :])
            value = term if value is None else value + term
        total.append(value)
    residual = states[...].astype(jnp.float32) + jnp.concatenate(total, axis=0)
    residual_ref[...] = residual
    normed = normalize(residual, gain[...]).astype(jnp.bfloat16)
    scores_ref[...] = jax.nn.sigmoid(dot(normed, w_router[...]))
    for e in range(len(outgoing)):
        row = iota((capacity, tokens), 0) + e * capacity
        chosen = (row == slots[0:1, :]) | (row == slots[1:2, :])
        outgoing[e][...] = dot(chosen.astype(jnp.bfloat16), normed).astype(jnp.bfloat16)


def project(info, states, w_out, gain, w_router, slots, pieces, capacity):
    groups, parts = len(pieces), len(pieces[0])
    tokens, width = states.shape
    experts = w_router.shape[1]
    flat = [piece for group in pieces for piece in group]
    whole = pl.BlockSpec(memory_space=pltpu.VMEM)
    out = pl.pallas_call(
        functools.partial(project_kernel, groups, parts),
        in_specs=[pl.BlockSpec(memory_space=pltpu.SMEM)] + [whole] * (5 + len(flat)),
        out_specs=[whole] * (2 + experts // 2),
        out_shape=[
            jax.ShapeDtypeStruct((tokens, width), jnp.float32),
            jax.ShapeDtypeStruct((tokens, experts), jnp.float32),
        ]
        + [jax.ShapeDtypeStruct((2 * capacity, width), jnp.bfloat16)] * (experts // 2),
        compiler_params=pltpu.CompilerParams(vmem_limit_bytes=VMEM_BYTES),
        name="project",
    )(info, states, w_out, gain, w_router, slots, *flat)
    return out[0], out[1], list(out[2:])


def expert_kernel(shards, has_sum, pieces, rows_ref, *refs):
    if has_sum:
        sum_ref, refs = refs[0], refs[1:]
    halves, refs = refs[: 2 * shards], refs[2 * shards :]
    outs, (w_s, sems) = refs[:-2], refs[-2:]
    step = pl.program_id(0)
    half = halves[0].shape[1]

    def fetch(s, k):
        return pltpu.make_async_copy(
            halves[2 * s + k], w_s.at[s, :, pl.ds(k * half, half), :], sems.at[s, k]
        )

    @pl.when(step == 0)
    def _():
        for s in range(shards):
            for k in range(2):
                fetch(s, k).start()

    rows = rows_ref[...]
    total = sum_ref[...] if has_sum else None
    for s in range(shards):

        @pl.when(step == 0)
        def _():
            for k in range(2):
                fetch(s, k).wait()

        gate = dot_nt(rows, w_s[s, 0])
        up = dot_nt(rows, w_s[s, 1])
        hidden = (jax.nn.gelu(gate, approximate=True) * up).astype(jnp.bfloat16)
        term = dot(hidden, w_s[s, 2])
        total = term if total is None else total + term
    if not pieces:
        outs[0][...] = total
    else:
        capacity = outs[0].shape[0]
        at_once = rows.shape[0] // capacity
        value = total.astype(jnp.bfloat16)
        for i in range(len(outs)):

            @pl.when(step == i // at_once)
            def _():
                start = i % at_once * capacity
                outs[i][...] = value[start : start + capacity]


def expert(rows, total, halves, pieces):
    count, width = rows.shape
    shards = len(halves) // 2
    half = halves[0].shape[1]
    capacity = count // pieces if pieces else 16
    at_once = max(
        n for n in range(1, count + 1)
        if count % n == 0 and n <= 256 and n % 16 == 0 and n % capacity == 0
    )
    block = pl.BlockSpec((at_once, width), lambda i: (i, 0))
    has_sum = total is not None
    if pieces:
        out_specs = [pl.BlockSpec((capacity, width), lambda i: (0, 0))] * pieces
        out_shape = [jax.ShapeDtypeStruct((capacity, width), jnp.bfloat16)] * pieces
    else:
        out_specs, out_shape = [block], [jax.ShapeDtypeStruct((count, width), jnp.float32)]
    out = pl.pallas_call(
        functools.partial(expert_kernel, shards, has_sum, pieces),
        grid=(count // at_once,),
        in_specs=[block] + [block] * has_sum + [ANY] * len(halves),
        out_specs=out_specs,
        out_shape=out_shape,
        input_output_aliases={1: 0} if has_sum and not pieces else {},
        scratch_shapes=[
            pltpu.VMEM((shards, 3, 2 * half, width), jnp.bfloat16),
            pltpu.SemaphoreType.DMA((shards, 2)),
        ],
        compiler_params=pltpu.CompilerParams(vmem_limit_bytes=VMEM_BYTES),
        name="experts",
    )(rows, *([total] if has_sum else []), *halves)
    return list(out)


def combine_kernel(residual, scores, routes, slots, *refs):
    returned, out = refs[:-1], refs[-1]
    tokens, experts = scores.shape
    capacity = returned[0].shape[0]
    mixed = None
    for k in range(TOP):
        gate = jnp.sum(
            jnp.where(iota((tokens, experts), 1) == routes[:, k : k + 1], scores[...], 0.0),
            axis=-1,
            keepdims=True,
        )
        picked = None
        for e in range(len(returned)):
            column = iota((tokens, capacity), 1) + e * capacity
            chosen = (column == slots[:, k : k + 1]).astype(jnp.bfloat16)
            term = dot(chosen, returned[e][...])
            picked = term if picked is None else picked + term
        term = picked * gate
        mixed = term if mixed is None else mixed + term
    out[...] = (residual[...] + mixed).astype(jnp.bfloat16)


def combine(residual, scores, routes, slots, returned):
    tokens, width = residual.shape
    whole = pl.BlockSpec(memory_space=pltpu.VMEM)
    return pl.pallas_call(
        combine_kernel,
        in_specs=[whole] * (4 + len(returned)),
        out_specs=whole,
        out_shape=jax.ShapeDtypeStruct((tokens, width), jnp.bfloat16),
        compiler_params=pltpu.CompilerParams(vmem_limit_bytes=VMEM_BYTES),
        name="combine",
    )(residual, scores, routes, slots, *returned)


def body(
    states,
    gain_attn,
    w_qkv,
    w_out,
    cache_prev,
    cached_blocks,
    gain_moe,
    w_router,
    routes,
    w_gate_up,
    w_down,
):
    toks, blks = lax.axis_size("tok"), lax.axis_size("blk")
    tok, blk = lax.axis_index("tok"), lax.axis_index("blk")
    tok_low, blk_low = tok % 2, blk % 2
    requests, per, width = states.shape
    tokens = requests * per
    local = width // toks
    experts = w_router.shape[1]
    capacity = tokens * TOP * 5 // (4 * experts)
    info = jnp.concatenate([tok[None].astype(jnp.int32), cached_blocks])
    flat_states = states.reshape(tokens, width)

    def over_tok(value, d):
        return lax.ppermute(value, "tok", [(i, i ^ d) for i in range(toks)])

    def other_core(value):
        return lax.ppermute(value, "blk", [(i, i ^ 1) for i in range(blks)])

    def heads_of(r, d):
        return lax.dynamic_slice_in_dim(cache_prev[r : r + 1], (tok ^ d) * local, local, axis=3)

    def spread(values):
        return [values[0]] + [over_tok(values[d], d) for d in range(1, toks)]

    moved = [[heads_of(r, d) for d in range(toks)] for r in range(requests)]
    gathered = [flat_states] + [None] * (toks - 1)
    for d in range(2, toks, 2):
        gathered[d] = over_tok(flat_states, d)
    gathered[1] = over_tok(flat_states, 1)
    cached = [spread(moved[0])]

    gate_up = w_gate_up[0].transpose(0, 2, 1)
    stacked = jnp.concatenate([gate_up, w_down], axis=0)
    half = stacked.shape[1] // 2
    stacked = stacked.reshape(3, 2, half, width)
    kept = lax.dynamic_index_in_dim(stacked, blk_low, axis=1, keepdims=False)
    given = lax.dynamic_index_in_dim(stacked, 1 - blk_low, axis=1, keepdims=False)
    (gathered[::2], gathered[1], cached[0], moved[1:], kept, given) = lax.optimization_barrier(
        (gathered[::2], gathered[1], cached[0], moved[1:], kept, given)
    )

    for d in range(2, toks, 2):
        gathered[d + 1] = over_tok(gathered[d], 1)
    taken = other_core(given)
    cached.append(spread(moved[1]))
    fresh = list(inward(info, gain_attn, w_qkv, gathered[:-1], toks))
    gathered[-1], taken, fresh, cached[1], moved[2:] = lax.optimization_barrier(
        (gathered[-1], taken, fresh, cached[1], moved[2:])
    )
    for r in range(2, requests):
        cached.append(spread(moved[r]))
        if r + 1 < requests:
            cached[r], moved[r + 1 :] = lax.optimization_barrier((cached[r], moved[r + 1 :]))
    stays = tok_low == blk_low
    mine = jnp.where(stays, kept, taken)
    leaving = jnp.where(stays, taken, kept)

    own_swapped = other_core(mine)

    fresh += list(inward(info, gain_attn, w_qkv, gathered[-1:], toks))
    fresh = [piece.reshape(requests, per, 3 * local) for piece in fresh]
    so_far = attend(info, fresh, cached[0], 0, None, requests)
    (own_swapped, mine, leaving, so_far, cached[1:]) = lax.optimization_barrier(
        (own_swapped, mine, leaving, so_far, cached[1:])
    )

    route_flat = routes.reshape(tokens, TOP)
    assigned = route_flat.reshape(-1) ^ (blk - blk_low + tok_low)
    one_hot = (assigned[:, None] == jnp.arange(experts)[None, :]).astype(jnp.int32)
    ranks = jnp.sum(one_hot * (jnp.cumsum(one_hot, axis=0) - 1), axis=1)
    slots = (assigned * capacity + ranks).reshape(tokens, TOP)

    shards = [mine, over_tok(leaving, 1)]
    for d in range(2, toks, 2):
        shards.append(over_tok(mine, d))
    for r in range(1, requests):
        so_far = attend(info, fresh, cached[r], r, so_far, requests)
    decode_cache = so_far[-1]
    back = [spread(so_far[:-1])]
    residual, scores, outgoing = project(
        info, flat_states, w_out, gain_moe.reshape(1, width), w_router, slots.T, back, capacity
    )
    shards[1:] = after(shards[1:], outgoing)
    swapped = [own_swapped] + [other_core(shard) for shard in shards[1:]]
    early = len(shards)
    for d in range(2, toks, 2):
        shards.append(over_tok(shards[1], d))

    planes = blks // 2

    def over_planes(value, d):
        return lax.ppermute(value, "blk", [(i, i ^ (2 * d)) for i in range(blks)])

    arrived = [outgoing[0]] + [over_planes(outgoing[d], d) for d in range(1, planes)]
    crossing = jnp.concatenate([value[capacity:] for value in arrived], axis=0)
    rows = jnp.concatenate([value[:capacity] for value in arrived] + [over_tok(crossing, 1)], axis=0)
    halves = [value for s in range(early) for value in (shards[s], swapped[s])]
    total = expert(rows, None, halves, 0)[0]
    total, shards[early:] = lax.optimization_barrier((total, shards[early:]))
    halves = [value for shard in shards[early:] for value in (shard, other_core(shard))]
    out = expert(rows, total, halves, experts)

    def home(value, plane, column):
        return lax.ppermute(
            value,
            ("tok", "blk"),
            [
                (t * blks + b, (t ^ column) * blks + (b ^ (2 * plane)))
                for t in range(toks)
                for b in range(blks)
            ],
        )

    returned = [None] * experts
    for column in (1, 0):
        for plane in range(planes):
            value = out[column * planes + plane]
            if plane or column:
                value = home(value, plane, column)
            returned[2 * plane + column] = value
    out_hidden = combine(residual, scores, route_flat, slots, returned)
    return (out_hidden.reshape(requests, per, width), decode_cache)


def solution(mesh):
    return jax.shard_map(
        body,
        mesh=mesh,
        in_specs=(
            P("blk", "tok", None),
            P(),
            P(),
            P(),
            P("blk", "tok", None, None),
            P("blk"),
            P(),
            P(),
            P("tok", "blk", None, None),
            P("blk", None, None, "tok"),
            P("blk", "tok", None),
        ),
        out_specs=(P("blk", "tok", None), P("blk", None, None, "tok")),
        check_vma=False,
    )
```

```python
import functools
import math

import jax
import jax.numpy as jnp
from jax import lax
from jax.experimental import pallas as pl
from jax.experimental.pallas import tpu as pltpu
from jax.sharding import PartitionSpec as P

HEAD_DIM = 64
TOP = 2
BLOCK = 128
CHUNK = 512
LANES = 128
HIDDEN_SCORE = -1e30
EPS = 1e-06
VMEM_BYTES = 56 * 1024 * 1024
ANY = pl.BlockSpec(memory_space=pl.ANY)


def normalize(values, gain):
    return (
        values
        * lax.rsqrt(jnp.mean(values * values, -1, keepdims=True) + EPS)
        * gain.astype(jnp.float32)
    )


def after(value, *others):
    return lax.optimization_barrier((value, others))[0]


def dot(left, right):
    return jnp.dot(left, right, preferred_element_type=jnp.float32)


def dot_nt(left, right):
    return lax.dot_general(left, right, (((1,), (1,)), ((), ())), preferred_element_type=jnp.float32)


def iota(shape, dim):
    return lax.broadcasted_iota(jnp.int32, shape, dim)


def attention_kernel(parts, first, chained, info, *refs):
    fresh_in, cached_in, refs = refs[:parts], refs[parts : 2 * parts], refs[2 * parts :]
    if chained:
        refs = refs[parts + 1 :]
    outs, cache_out, refs = refs[:parts], refs[parts], refs[parts + 1 :]
    q_s, k_s, v_s, s_s, m_s, l_s, acc_s, o_s, fresh_s, zero_s, fresh_sem, old_sem = refs
    per, width = outs[0].shape
    group = per * parts
    held = cached_in[0].shape[1]
    unit = zero_s.shape[0]
    heads = width // HEAD_DIM
    me = info[0]
    req = first + pl.program_id(0)
    length = info[1 + req] * BLOCK
    zero_s[...] = jnp.zeros_like(zero_s)
    pick_row = iota((unit, 2 * unit), 0) * 2
    pick_col = iota((unit, 2 * unit), 1)
    pick_k = (pick_col == pick_row).astype(jnp.bfloat16)
    pick_v = (pick_col == pick_row + 1).astype(jnp.bfloat16)

    for d in range(parts):
        row = pl.multiple_of((me ^ d) * per, per)
        key, value = fresh_in[d][:, width : 2 * width], fresh_in[d][:, 2 * width :]
        q_s[heads, pl.ds(row, per), :] = fresh_in[d][:, :width]
        k_s[pl.ds(row, per), :] = key
        v_s[pl.ds(row, per), :] = value
        fresh_s[d] = jnp.stack([key, value], axis=1)
        pltpu.make_async_copy(
            fresh_s.at[d], cache_out.at[req, pl.ds(length + row, per)], fresh_sem.at[d]
        ).start()
        for i in range(held // unit):
            at = pl.multiple_of((me ^ d) * held + i * unit, unit)
            block = cached_in[d].at[0, pl.ds(i * unit, unit)]
            sem = old_sem.at[d * (held // unit) + i]

            @pl.when(at < length)
            def _():
                pltpu.make_async_copy(block, cache_out.at[req, pl.ds(at, unit)], sem).start()
                pairs = block[...].reshape(2 * unit, width)
                k_s[pl.ds(group + at, unit), :] = dot(pick_k, pairs).astype(jnp.bfloat16)
                v_s[pl.ds(group + at, unit), :] = dot(pick_v, pairs).astype(jnp.bfloat16)

            @pl.when(at >= length)
            def _():
                pltpu.make_async_copy(
                    zero_s, cache_out.at[req, pl.ds(at + group, unit)], sem
                ).start()

    tail = pl.ds(pl.multiple_of(group + length, BLOCK), CHUNK)
    k_s[tail, :] = jnp.zeros((CHUNK, width), jnp.bfloat16)
    v_s[tail, :] = jnp.zeros((CHUNK, width), jnp.bfloat16)
    chunks = (length + CHUNK - 1) // CHUNK
    own = group // CHUNK
    scale = HEAD_DIM ** (-0.5) * math.log2(math.e)

    def fold(values):
        folded = values[:, :LANES]
        for at in range(LANES, CHUNK, LANES):
            folded = jnp.maximum(folded, values[:, at : at + LANES])
        return folded

    lane_head = iota((group, width), 1) // HEAD_DIM
    for h in range(heads):
        q_s[h] = jnp.where(lane_head == h, q_s[heads], jnp.zeros((), jnp.bfloat16))
    for h in range(heads):
        for c in range(own):
            top = c * CHUNK
            scores = dot_nt(q_s[h, top:, :], k_s[top : top + CHUNK, :])
            rows = group - top
            visible = iota((rows, CHUNK), 1) <= iota((rows, CHUNK), 0)
            scores = jnp.where(visible, scores, HIDDEN_SCORE)
            s_s[c, h, top:, :] = scores
            if c == 0:
                m_s[h] = fold(scores)
            else:
                m_s[h, top:, :] = jnp.maximum(m_s[h, top:, :], fold(scores))

    def score_chunk(c, carry):
        start = pl.multiple_of(c * CHUNK, CHUNK)
        keys = k_s[pl.ds(group + start, CHUNK), :]
        seen = iota((1, CHUNK), 1) + start < length
        for h in range(heads):
            scores = jnp.where(seen, dot_nt(q_s[h], keys), HIDDEN_SCORE)
            s_s[own + c, h] = scores
            m_s[h] = jnp.maximum(m_s[h], fold(scores))
        return carry

    lax.fori_loop(0, chunks, score_chunk, 0)
    for h in range(heads):
        highest = jnp.max(m_s[h], axis=-1, keepdims=True) * scale
        m_s[h] = jnp.broadcast_to(highest, (group, LANES))

    def weigh(c, h, rows):
        pieces = [
            jnp.exp2(s_s[c, h, rows:, at : at + LANES] * scale - m_s[h, rows:, :])
            for at in range(0, CHUNK, LANES)
        ]
        total = pieces[0]
        for piece in pieces[1:]:
            total = total + piece
        return jnp.concatenate([p.astype(jnp.bfloat16) for p in pieces], axis=1), total

    for h in range(heads):
        for c in range(own):
            top = c * CHUNK
            weights, total = weigh(c, h, top)
            product = dot(weights, v_s[top : top + CHUNK, :])
            if c == 0:
                l_s[h] = total
                acc_s[h] = product
            else:
                l_s[h, top:, :] += total
                acc_s[h, top:, :] += product

    def value_chunk(c, carry):
        start = pl.multiple_of(c * CHUNK, CHUNK)
        values = v_s[pl.ds(group + start, CHUNK), :]
        for h in range(heads):
            weights, total = weigh(own + c, h, 0)
            l_s[h] += total
            acc_s[h] += dot(weights, values)
        return carry

    lax.fori_loop(0, chunks, value_chunk, 0)
    result = None
    for h in range(heads):
        value = acc_s[h] / jnp.sum(l_s[h], axis=-1, keepdims=True)
        result = value if h == 0 else jnp.where(lane_head == h, value, result)
    o_s[...] = result
    for d in range(parts):
        row = pl.multiple_of((me ^ d) * per, per)
        outs[d][...] = o_s[pl.ds(row, per), :].astype(jnp.bfloat16)
    for d in range(parts):
        pltpu.make_async_copy(
            fresh_s.at[d], cache_out.at[req, pl.ds(length, per)], fresh_sem.at[d]
        ).wait()
        for i in range(held // unit):
            pltpu.make_async_copy(
                zero_s, cache_out.at[req, pl.ds(0, unit)], old_sem.at[d * (held // unit) + i]
            ).wait()


def attend(info, fresh, cached, first, so_far, requests):
    parts = len(fresh)
    count, held, _, width = cached[0].shape
    per = fresh[0].shape[1]
    group, cache_full = per * parts, held * parts
    unit = math.gcd(held, BLOCK)
    heads = width // HEAD_DIM
    chained = so_far is not None
    slots = (group + cache_full) // CHUNK
    rows = group + cache_full + CHUNK
    in_specs = [pl.BlockSpec((None, per, 3 * width), lambda r, _: (first + r, 0, 0))] * parts
    in_specs += [pl.BlockSpec((1, held, 2, width), lambda r, _: (r, 0, 0, 0))] * parts
    operands = [info, *fresh, *cached]
    aliases = {}
    if chained:
        in_specs += [ANY] * len(so_far)
        aliases = {len(operands) + i: i for i in range(len(so_far))}
        operands += so_far
    out = pl.pallas_call(
        functools.partial(attention_kernel, parts, first, chained),
        grid_spec=pltpu.PrefetchScalarGridSpec(
            num_scalar_prefetch=1,
            grid=(count,),
            in_specs=in_specs,
            out_specs=[pl.BlockSpec((None, per, width), lambda r, _: (first + r, 0, 0))] * parts + [ANY],
            scratch_shapes=[
                pltpu.VMEM((heads + 1, group, width), jnp.bfloat16),
                pltpu.VMEM((rows, width), jnp.bfloat16),
                pltpu.VMEM((rows, width), jnp.bfloat16),
                pltpu.VMEM((slots, heads, group, CHUNK), jnp.float32),
                pltpu.VMEM((heads, group, LANES), jnp.float32),
                pltpu.VMEM((heads, group, LANES), jnp.float32),
                pltpu.VMEM((heads, group, width), jnp.float32),
                pltpu.VMEM((group, width), jnp.float32),
                pltpu.VMEM((parts, per, 2, width), jnp.bfloat16),
                pltpu.VMEM((unit, 2, width), jnp.bfloat16),
                pltpu.SemaphoreType.DMA((parts,)),
                pltpu.SemaphoreType.DMA((cache_full // unit,)),
            ],
        ),
        out_shape=[jax.ShapeDtypeStruct((requests, per, width), jnp.bfloat16)] * parts
        + [jax.ShapeDtypeStruct((requests, cache_full + group, 2, width), jnp.bfloat16)],
        input_output_aliases=aliases,
        compiler_params=pltpu.CompilerParams(vmem_limit_bytes=VMEM_BYTES),
        name="attention",
    )(*operands)
    return list(out)


def inward_kernel(count, info, gain, *refs):
    weights, pieces, outs = refs[:3], refs[3 : 3 + count], refs[3 + count :]
    width = weights[0].shape[1]
    for piece, out in zip(pieces, outs):
        normed = normalize(piece[...].astype(jnp.float32), gain[...]).astype(jnp.bfloat16)
        for i in range(3):
            out[:, i * width : (i + 1) * width] = dot(normed, weights[i][...]).astype(jnp.bfloat16)


def inward(info, gain, w_qkv, pieces, toks):
    count = len(pieces)
    tokens, width = pieces[0].shape
    local = width // toks

    def columns(i):
        return pl.BlockSpec((width, local), lambda _, info: (0, i * toks + info[0]))

    whole = pl.BlockSpec(memory_space=pltpu.VMEM)
    return pl.pallas_call(
        functools.partial(inward_kernel, count),
        grid_spec=pltpu.PrefetchScalarGridSpec(
            num_scalar_prefetch=1,
            grid=(1,),
            in_specs=[whole] + [columns(i) for i in range(3)] + [whole] * count,
            out_specs=[whole] * count,
        ),
        out_shape=[jax.ShapeDtypeStruct((tokens, 3 * local), jnp.bfloat16)] * count,
        compiler_params=pltpu.CompilerParams(vmem_limit_bytes=VMEM_BYTES),
        name="inward",
    )(info, gain.reshape(1, width), w_qkv, w_qkv, w_qkv, *pieces)


def project_kernel(groups, parts, capacity, messages, info, states, w_out, gain, w_router, slots, *refs):
    pieces, refs = refs[: groups * parts], refs[groups * parts :]
    residual_ref, scores_ref, outgoing = refs[0], refs[1], refs[2:]
    me = info[0]
    width = pieces[0].shape[-1]
    per = pieces[0].shape[-2]
    tokens = states.shape[0]
    total = []
    for g in range(groups):
        rows = pieces[g * parts].shape[0] * per
        value = None
        for d in range(parts):
            piece = pieces[g * parts + d][...].reshape(rows, width)
            term = dot(piece, w_out[pl.ds(pl.multiple_of((me ^ d) * width, width), width), :])
            value = term if value is None else value + term
        total.append(value)
    residual = states[...].astype(jnp.float32) + jnp.concatenate(total, axis=0)
    residual_ref[...] = residual
    normed = normalize(residual, gain[...]).astype(jnp.bfloat16)
    scores_ref[...] = jax.nn.sigmoid(dot_nt(normed, w_router[...]))
    for blocks, ref in zip(messages, outgoing):
        row = iota((len(blocks) * capacity, tokens), 0)
        slot = row + blocks[0] * capacity
        for i in range(1, len(blocks)):
            slot = jnp.where(row >= i * capacity, row + (blocks[i] - i) * capacity, slot)
        chosen = (slot == slots[0:1, :]) | (slot == slots[1:2, :])
        ref[...] = dot(chosen.astype(jnp.bfloat16), normed).astype(jnp.bfloat16)


def project(info, states, w_out, gain, w_router, slots, pieces, capacity, messages):
    groups, parts = len(pieces), len(pieces[0])
    tokens, width = states.shape
    experts = w_router.shape[0]
    flat = [piece for group in pieces for piece in group]
    whole = pl.BlockSpec(memory_space=pltpu.VMEM)
    out = pl.pallas_call(
        functools.partial(project_kernel, groups, parts, capacity, messages),
        in_specs=[pl.BlockSpec(memory_space=pltpu.SMEM)] + [whole] * (5 + len(flat)),
        out_specs=[whole] * (2 + len(messages)),
        out_shape=[
            jax.ShapeDtypeStruct((tokens, width), jnp.float32),
            jax.ShapeDtypeStruct((tokens, experts), jnp.float32),
        ]
        + [jax.ShapeDtypeStruct((len(m) * capacity, width), jnp.bfloat16) for m in messages],
        compiler_params=pltpu.CompilerParams(vmem_limit_bytes=VMEM_BYTES),
        name="project",
    )(info, states, w_out, gain, w_router, slots, *flat)
    return out[0], out[1], list(out[2:])


def expert_kernel(loads, shards, has_sum, capacity, messages, rows_ref, *refs):
    if has_sum:
        sum_ref, refs = refs[0], refs[1:]
    held, refs = refs[: len(loads)], refs[len(loads) :]
    outs, (w_s, sems) = refs[:-2], refs[-2:]
    step = pl.program_id(0)
    half = held[0].shape[1]

    def fetch(i):
        start, count, shard, part, k = loads[i]
        return pltpu.make_async_copy(
            held[i].at[pl.ds(start, count)],
            w_s.at[shard, pl.ds(part, count), pl.ds(k * half, half), :],
            sems.at[i],
        )

    @pl.when(step == 0)
    def _():
        for i in range(len(loads)):
            fetch(i).start()

    rows = rows_ref[...]
    total = sum_ref[...] if has_sum else None
    for s in range(shards):

        @pl.when(step == 0)
        def _():
            for i in range(len(loads)):
                if loads[i][2] == s:
                    fetch(i).wait()

        gate = dot_nt(rows, w_s[s, 0])
        up = dot_nt(rows, w_s[s, 1])
        hidden = (jax.nn.gelu(gate, approximate=True) * up).astype(jnp.bfloat16)
        term = dot(hidden, w_s[s, 2])
        total = term if total is None else total + term
    if not messages:
        outs[0][...] = total
    else:
        value = total.astype(jnp.bfloat16)
        at = 0
        for out in outs:
            start = at % rows.shape[0]

            @pl.when(step == at // rows.shape[0])
            def _():
                out[...] = value[start : start + out.shape[0]]

            at += out.shape[0]


def expert(rows, total, weights, capacity, messages):
    count, width = rows.shape
    held, loads = [piece[0] for piece in weights], [piece[1:] for piece in weights]
    shards = 1 + max(load[2] for load in loads)
    half = held[0].shape[1]
    at_once = max(
        n for n in range(1, count + 1)
        if count % n == 0 and n <= 256 and n % 16 == 0 and n % (2 * capacity) == 0
    )
    block = pl.BlockSpec((at_once, width), lambda i: (i, 0))
    has_sum = total is not None
    if messages:
        sizes = [len(m) * capacity for m in messages]
        out_specs = [pl.BlockSpec((n, width), lambda i: (0, 0)) for n in sizes]
        out_shape = [jax.ShapeDtypeStruct((n, width), jnp.bfloat16) for n in sizes]
    else:
        out_specs, out_shape = [block], [jax.ShapeDtypeStruct((count, width), jnp.float32)]
    out = pl.pallas_call(
        functools.partial(expert_kernel, loads, shards, has_sum, capacity, messages),
        grid=(count // at_once,),
        in_specs=[block] + [block] * has_sum + [ANY] * len(held),
        out_specs=out_specs,
        out_shape=out_shape,
        input_output_aliases={1: 0} if has_sum and not messages else {},
        scratch_shapes=[
            pltpu.VMEM((shards, 3, 2 * half, width), jnp.bfloat16),
            pltpu.SemaphoreType.DMA((len(held),)),
        ],
        compiler_params=pltpu.CompilerParams(vmem_limit_bytes=VMEM_BYTES),
        name="experts",
    )(rows, *([total] if has_sum else []), *held)
    return list(out)


def combine_kernel(capacity, blocks, residual, scores, routes, slots, *refs):
    returned, out = refs[:-1], refs[-1]
    tokens, experts = scores.shape
    mixed = None
    for k in range(TOP):
        gate = jnp.sum(
            jnp.where(iota((tokens, experts), 1) == routes[:, k : k + 1], scores[...], 0.0),
            axis=-1,
            keepdims=True,
        )
        picked = None
        for block, ref in zip(blocks, returned):
            column = iota((tokens, capacity), 1) + block * capacity
            chosen = (column == slots[:, k : k + 1]).astype(jnp.bfloat16)
            term = dot(chosen, ref[:capacity, :])
            picked = term if picked is None else picked + term
        term = picked * gate
        mixed = term if mixed is None else mixed + term
    out[...] = (residual[...] + mixed).astype(jnp.bfloat16)


def combine(residual, scores, routes, slots, capacity, blocks, returned):
    tokens, width = residual.shape
    whole = pl.BlockSpec(memory_space=pltpu.VMEM)
    return pl.pallas_call(
        functools.partial(combine_kernel, capacity, blocks),
        in_specs=[whole] * (4 + len(returned)),
        out_specs=whole,
        out_shape=jax.ShapeDtypeStruct((tokens, width), jnp.bfloat16),
        compiler_params=pltpu.CompilerParams(vmem_limit_bytes=VMEM_BYTES),
        name="combine",
    )(residual, scores, routes, slots, *returned)


def body(
    states,
    gain_attn,
    w_qkv,
    w_out,
    cache_prev,
    cached_blocks,
    gain_moe,
    w_router,
    routes,
    w_gate_up,
    w_down,
):
    toks, blks = lax.axis_size("tok"), lax.axis_size("blk")
    tok, blk = lax.axis_index("tok"), lax.axis_index("blk")
    tok_low, blk_low = tok % 2, blk % 2
    requests, per, width = states.shape
    tokens = requests * per
    local = width // toks
    experts = w_router.shape[1]
    capacity = tokens * TOP * 5 // (4 * experts)
    info = jnp.concatenate([tok[None].astype(jnp.int32), cached_blocks])
    flat_states = states.reshape(tokens, width)

    def over_tok(value, d):
        return lax.ppermute(value, "tok", [(i, i ^ d) for i in range(toks)])

    def other_core(value):
        return lax.ppermute(value, "blk", [(i, i ^ 1) for i in range(blks)])

    def heads_of(r, d):
        return lax.dynamic_slice(
            cache_prev, (r, 0, 0, (tok ^ d) * local), (1, *cache_prev.shape[1:3], local)
        )

    def spread(values):
        return [values[0]] + [over_tok(values[d], d) for d in range(1, toks)]

    join = lax.optimization_barrier
    far = list(range(2, toks, 2))

    gathered = [flat_states] + [None] * (toks - 1)
    for d in far:
        gathered[d] = over_tok(flat_states, d)
    gathered[1] = over_tok(flat_states, 1)
    gate_up = w_gate_up[0].transpose(0, 2, 1)
    stacked = jnp.concatenate([gate_up, w_down], axis=0)
    half = stacked.shape[1] // 2
    stacked = stacked.reshape(3, 2, half, width)
    kept = lax.dynamic_index_in_dim(stacked, blk_low, axis=1, keepdims=False)
    given = lax.dynamic_index_in_dim(stacked, 1 - blk_low, axis=1, keepdims=False)
    moved = [[heads_of(r, d) for d in range(toks)] for r in range(requests)]
    gathered[::2], gathered[1], given, kept, moved = join(
        (gathered[::2], gathered[1], given, kept, moved)
    )
    taken = other_core(given)
    stays = tok_low == blk_low
    mine = jnp.where(stays, kept, taken)
    mine_parts = [jnp.where(stays, kept[p : p + 1], taken[p : p + 1]) for p in range(3)]
    leaving_gate = jnp.where(stays, taken[:1], kept[:1])
    leaving_rest = jnp.where(stays, taken[1:], kept[1:])

    route_flat = routes.reshape(tokens, TOP)
    assigned = route_flat.reshape(-1) ^ (blk - blk_low + tok_low)
    one_hot = (assigned[:, None] == jnp.arange(experts)[None, :]).astype(jnp.int32)
    ranks = jnp.sum(one_hot * (jnp.cumsum(one_hot, axis=0) - 1), axis=1)
    slots = (assigned * capacity + ranks).reshape(tokens, TOP)
    tables = (route_flat, slots, slots.T, w_router.T)

    for d in far:
        gathered[d + 1] = over_tok(gathered[d], 1)
    cached = [spread(moved[0])]
    far_gate = [over_tok(mine_parts[0], d) for d in far]
    fresh = list(inward(info, gain_attn, w_qkv, gathered[:-1], toks))
    weights_held = (mine, mine_parts, leaving_gate, leaving_rest)
    gathered[-1], fresh, cached[0], far_gate, moved[1:], weights_held, tables = join(
        (gathered[-1], fresh, cached[0], far_gate, moved[1:], weights_held, tables)
    )
    route_flat, slots, slots_across, router_across = tables
    mine, mine_parts, leaving_gate, leaving_rest = weights_held

    cached.append(spread(moved[1]))
    own_swapped = other_core(mine)
    fresh += list(inward(info, gain_attn, w_qkv, gathered[-1:], toks))
    fresh = [piece.reshape(requests, per, 3 * local) for piece in fresh]
    so_far = attend(info, fresh, cached[0], 0, None, requests)
    cached[1], own_swapped, so_far, far_gate, moved[2:] = join(
        (cached[1], own_swapped, so_far, far_gate, moved[2:])
    )
    for r in range(2, requests):
        cached.append(spread(moved[r]))
        so_far = attend(info, fresh, cached[r - 1], r - 1, so_far, requests)
        if r + 1 < requests:
            cached[r], moved[r + 1 :], so_far = join((cached[r], moved[r + 1 :], so_far))
    far_gate_swapped = [other_core(piece) for piece in far_gate]
    leaving_gate, mine_parts, cached[-1], so_far, far_gate_swapped = join(
        (leaving_gate, mine_parts, cached[-1], so_far, far_gate_swapped)
    )

    near_gate = over_tok(leaving_gate, 1)
    far_up = [over_tok(mine_parts[1], d) for d in far]
    so_far = attend(info, fresh, cached[-1], requests - 1, so_far, requests)
    decode_cache = so_far[-1]
    back = spread(so_far[:-1])
    back, near_gate, far_up, leaving_rest, mine_parts = join(
        (back, near_gate, far_up, leaving_rest, mine_parts)
    )

    near_rest = over_tok(leaving_rest, 1)
    both = jnp.concatenate([mine_parts[2], near_gate], axis=0)
    far_both = [over_tok(both, d) for d in far]
    planes = blks // 2
    opposite = planes // 2
    leaving_by = [[(d, 0), (d, 1)] for d in range(planes) if d != opposite]
    leaving_by += [[(opposite, 1)], [(opposite, 0)]]
    messages = [[2 * d + c for d, c in blocks] for blocks in leaving_by]
    residual, scores, outgoing = project(
        info, flat_states, w_out, gain_moe.reshape(1, width), router_across, slots_across, [back],
        capacity, messages,
    )

    def home(value, plane, column):
        return lax.ppermute(
            value,
            ("tok", "blk"),
            [
                (t * blks + b, (t ^ column) * blks + (b ^ (2 * plane)))
                for t in range(toks)
                for b in range(blks)
            ],
        )

    place = {}
    for blocks, value in zip(leaving_by, outgoing):
        plane = blocks[0][0]
        if plane:
            value = home(value, plane, 0)
        for i, at in enumerate(blocks):
            place[at] = value[i * capacity : (i + 1) * capacity] if len(blocks) > 1 else value
        if blocks == [(opposite, 1)]:
            near_rest, far_both, place = join((near_rest, far_both, place))
    last_rest = [over_tok(near_rest, d) for d in far]
    first = [near_gate, near_rest, *far_up, *far_both]
    first_swapped = other_core(jnp.concatenate(first, axis=0))
    crossed = over_tok(jnp.concatenate([place[(d, 1)] for d in range(planes)], axis=0), 1)
    homeward = [[(opposite, c)] for c in (0, 1)]
    homeward += [[(d, c)] for c in (1, 0) for d in range(planes) if d != opposite]
    for d in range(planes):
        place[(d, 1)] = crossed[d * capacity : (d + 1) * capacity]
    rows = jnp.concatenate([place[at] for blocks in homeward for at in blocks], axis=0)
    count = len(far)
    weights = [(mine, 0, 3, 0, 0, 0), (own_swapped, 0, 3, 0, 0, 1)]
    weights += [(near_gate, 0, 1, 1, 0, 0), (near_rest, 0, 2, 1, 1, 0), (first_swapped, 0, 3, 1, 0, 1)]
    for i in range(count):
        weights += [(far_gate[i], 0, 1, 2 + i, 0, 0), (far_gate_swapped[i], 0, 1, 2 + i, 0, 1)]
        weights += [(far_up[i], 0, 1, 2 + i, 1, 0), (first_swapped, 3 + i, 1, 2 + i, 1, 1)]
        weights += [(far_both[i], 0, 1, 2 + i, 2, 0)]
        weights += [(first_swapped, 3 + count + 2 * i, 1, 2 + i, 2, 1)]
    total = expert(rows, None, weights, capacity, [])[0]
    total, last_rest = join((total, last_rest))
    last_swapped = other_core(jnp.concatenate(last_rest, axis=0))
    weights = []
    for i in range(count):
        weights += [(far_both[i], 1, 1, i, 0, 0)]
        weights += [(first_swapped, 3 + count + 2 * i + 1, 1, i, 0, 1)]
        weights += [(last_rest[i], 0, 2, i, 1, 0), (last_swapped, 2 * i, 2, i, 1, 1)]
    out = expert(rows, total, weights, capacity, homeward)
    returned, blocks = [], []
    for message, value in zip(homeward, out):
        plane, column = message[0]
        if plane or column:
            value = home(value, plane, column)
        returned.append(value)
        blocks.append(2 * plane + column)
    out_hidden = combine(residual, scores, route_flat, slots, capacity, blocks, returned)
    return (out_hidden.reshape(requests, per, width), decode_cache)


def solution(mesh):
    return jax.shard_map(
        body,
        mesh=mesh,
        in_specs=(
            P("blk", "tok", None),
            P(),
            P(),
            P(),
            P("blk", "tok", None, None),
            P("blk"),
            P(),
            P(),
            P("tok", "blk", None, None),
            P("blk", None, None, "tok"),
            P("blk", "tok", None),
        ),
        out_specs=(P("blk", "tok", None), P("blk", None, None, "tok")),
        check_vma=False,
    )
```

```python
import functools
import math

import jax
import jax.numpy as jnp
from jax import lax
from jax.experimental import pallas as pl
from jax.experimental.pallas import tpu as pltpu
from jax.sharding import PartitionSpec as P

HEAD_DIM = 64
TOP = 2
BLOCK = 128
CHUNK = 512
LANES = 128
HIDDEN_SCORE = -1e30
EPS = 1e-06
VMEM_BYTES = 56 * 1024 * 1024
ANY = pl.BlockSpec(memory_space=pl.ANY)


def normalize(values, gain):
    return (
        values
        * lax.rsqrt(jnp.mean(values * values, -1, keepdims=True) + EPS)
        * gain.astype(jnp.float32)
    )


def after(value, *others):
    return lax.optimization_barrier((value, others))[0]


def dot(left, right):
    return jnp.dot(left, right, preferred_element_type=jnp.float32)


def dot_nt(left, right):
    return lax.dot_general(left, right, (((1,), (1,)), ((), ())), preferred_element_type=jnp.float32)


def iota(shape, dim):
    return lax.broadcasted_iota(jnp.int32, shape, dim)


def attention_kernel(parts, first, chained, info, *refs):
    fresh_in, cached_in, refs = refs[:parts], refs[parts : 2 * parts], refs[2 * parts :]
    if chained:
        refs = refs[parts + 1 :]
    outs, cache_out, refs = refs[:parts], refs[parts], refs[parts + 1 :]
    q_s, k_s, v_s, s_s, m_s, l_s, acc_s, o_s, fresh_s, zero_s, fresh_sem, old_sem = refs
    per, width = outs[0].shape
    group = per * parts
    held = cached_in[0].shape[1]
    unit = zero_s.shape[0]
    heads = width // HEAD_DIM
    me = info[0]
    req = info[1 + cache_out.shape[0] + first + pl.program_id(0)]
    length = info[1 + req] * BLOCK
    zero_s[...] = jnp.zeros_like(zero_s)
    pick_row = iota((unit, 2 * unit), 0) * 2
    pick_col = iota((unit, 2 * unit), 1)
    pick_k = (pick_col == pick_row).astype(jnp.bfloat16)
    pick_v = (pick_col == pick_row + 1).astype(jnp.bfloat16)

    for d in range(parts):
        row = pl.multiple_of((me ^ d) * per, per)
        key, value = fresh_in[d][:, width : 2 * width], fresh_in[d][:, 2 * width :]
        q_s[heads, pl.ds(row, per), :] = fresh_in[d][:, :width]
        k_s[pl.ds(row, per), :] = key
        v_s[pl.ds(row, per), :] = value
        fresh_s[d] = jnp.stack([key, value], axis=1)
        pltpu.make_async_copy(
            fresh_s.at[d], cache_out.at[req, pl.ds(length + row, per)], fresh_sem.at[d]
        ).start()
        for i in range(held // unit):
            at = pl.multiple_of((me ^ d) * held + i * unit, unit)
            block = cached_in[d].at[0, pl.ds(i * unit, unit)]
            sem = old_sem.at[d * (held // unit) + i]

            @pl.when(at < length)
            def _():
                pltpu.make_async_copy(block, cache_out.at[req, pl.ds(at, unit)], sem).start()
                pairs = block[...].reshape(2 * unit, width)
                k_s[pl.ds(group + at, unit), :] = dot(pick_k, pairs).astype(jnp.bfloat16)
                v_s[pl.ds(group + at, unit), :] = dot(pick_v, pairs).astype(jnp.bfloat16)

            @pl.when(at >= length)
            def _():
                pltpu.make_async_copy(
                    zero_s, cache_out.at[req, pl.ds(at + group, unit)], sem
                ).start()

    tail = pl.ds(pl.multiple_of(group + length, BLOCK), CHUNK)
    k_s[tail, :] = jnp.zeros((CHUNK, width), jnp.bfloat16)
    v_s[tail, :] = jnp.zeros((CHUNK, width), jnp.bfloat16)
    chunks = (length + CHUNK - 1) // CHUNK
    own = group // CHUNK
    scale = HEAD_DIM ** (-0.5) * math.log2(math.e)

    def fold(values):
        folded = values[:, :LANES]
        for at in range(LANES, CHUNK, LANES):
            folded = jnp.maximum(folded, values[:, at : at + LANES])
        return folded

    lane_head = iota((group, width), 1) // HEAD_DIM
    for h in range(heads):
        q_s[h] = jnp.where(lane_head == h, q_s[heads], jnp.zeros((), jnp.bfloat16))
    for h in range(heads):
        for c in range(own):
            top = c * CHUNK
            scores = dot_nt(q_s[h, top:, :], k_s[top : top + CHUNK, :])
            rows = group - top
            visible = iota((rows, CHUNK), 1) <= iota((rows, CHUNK), 0)
            scores = jnp.where(visible, scores, HIDDEN_SCORE)
            s_s[c, h, top:, :] = scores
            if c == 0:
                m_s[h] = fold(scores)
            else:
                m_s[h, top:, :] = jnp.maximum(m_s[h, top:, :], fold(scores))

    def score_chunk(c, carry):
        start = pl.multiple_of(c * CHUNK, CHUNK)
        keys = k_s[pl.ds(group + start, CHUNK), :]
        seen = iota((1, CHUNK), 1) + start < length
        for h in range(heads):
            scores = jnp.where(seen, dot_nt(q_s[h], keys), HIDDEN_SCORE)
            s_s[own + c, h] = scores
            m_s[h] = jnp.maximum(m_s[h], fold(scores))
        return carry

    lax.fori_loop(0, chunks, score_chunk, 0)
    for h in range(heads):
        highest = jnp.max(m_s[h], axis=-1, keepdims=True) * scale
        m_s[h] = jnp.broadcast_to(highest, (group, LANES))

    def weigh(c, h, rows):
        pieces = [
            jnp.exp2(s_s[c, h, rows:, at : at + LANES] * scale - m_s[h, rows:, :])
            for at in range(0, CHUNK, LANES)
        ]
        total = pieces[0]
        for piece in pieces[1:]:
            total = total + piece
        return jnp.concatenate([p.astype(jnp.bfloat16) for p in pieces], axis=1), total

    for h in range(heads):
        for c in range(own):
            top = c * CHUNK
            weights, total = weigh(c, h, top)
            product = dot(weights, v_s[top : top + CHUNK, :])
            if c == 0:
                l_s[h] = total
                acc_s[h] = product
            else:
                l_s[h, top:, :] += total
                acc_s[h, top:, :] += product

    def value_chunk(c, carry):
        start = pl.multiple_of(c * CHUNK, CHUNK)
        values = v_s[pl.ds(group + start, CHUNK), :]
        for h in range(heads):
            weights, total = weigh(own + c, h, 0)
            l_s[h] += total
            acc_s[h] += dot(weights, values)
        return carry

    lax.fori_loop(0, chunks, value_chunk, 0)
    result = None
    for h in range(heads):
        value = acc_s[h] / jnp.sum(l_s[h], axis=-1, keepdims=True)
        result = value if h == 0 else jnp.where(lane_head == h, value, result)
    o_s[...] = result
    for d in range(parts):
        row = pl.multiple_of((me ^ d) * per, per)
        outs[d][...] = o_s[pl.ds(row, per), :].astype(jnp.bfloat16)
    for d in range(parts):
        pltpu.make_async_copy(
            fresh_s.at[d], cache_out.at[req, pl.ds(length, per)], fresh_sem.at[d]
        ).wait()
        for i in range(held // unit):
            pltpu.make_async_copy(
                zero_s, cache_out.at[req, pl.ds(0, unit)], old_sem.at[d * (held // unit) + i]
            ).wait()


def attend(info, fresh, cached, first, so_far, requests):
    parts = len(fresh)
    count, held, _, width = cached[0].shape
    per = fresh[0].shape[1]
    group, cache_full = per * parts, held * parts
    unit = math.gcd(held, BLOCK)
    heads = width // HEAD_DIM
    chained = so_far is not None
    slots = (group + cache_full) // CHUNK
    rows = group + cache_full + CHUNK
    def request(r, info):
        return (info[1 + requests + first + r], 0, 0)

    in_specs = [pl.BlockSpec((None, per, 3 * width), request)] * parts
    in_specs += [pl.BlockSpec((1, held, 2, width), lambda r, _: (r, 0, 0, 0))] * parts
    operands = [info, *fresh, *cached]
    aliases = {}
    if chained:
        in_specs += [ANY] * len(so_far)
        aliases = {len(operands) + i: i for i in range(len(so_far))}
        operands += so_far
    out = pl.pallas_call(
        functools.partial(attention_kernel, parts, first, chained),
        grid_spec=pltpu.PrefetchScalarGridSpec(
            num_scalar_prefetch=1,
            grid=(count,),
            in_specs=in_specs,
            out_specs=[pl.BlockSpec((None, per, width), request)] * parts + [ANY],
            scratch_shapes=[
                pltpu.VMEM((heads + 1, group, width), jnp.bfloat16),
                pltpu.VMEM((rows, width), jnp.bfloat16),
                pltpu.VMEM((rows, width), jnp.bfloat16),
                pltpu.VMEM((slots, heads, group, CHUNK), jnp.float32),
                pltpu.VMEM((heads, group, LANES), jnp.float32),
                pltpu.VMEM((heads, group, LANES), jnp.float32),
                pltpu.VMEM((heads, group, width), jnp.float32),
                pltpu.VMEM((group, width), jnp.float32),
                pltpu.VMEM((parts, per, 2, width), jnp.bfloat16),
                pltpu.VMEM((unit, 2, width), jnp.bfloat16),
                pltpu.SemaphoreType.DMA((parts,)),
                pltpu.SemaphoreType.DMA((cache_full // unit,)),
            ],
        ),
        out_shape=[jax.ShapeDtypeStruct((requests, per, width), jnp.bfloat16)] * parts
        + [jax.ShapeDtypeStruct((requests, cache_full + group, 2, width), jnp.bfloat16)],
        input_output_aliases=aliases,
        compiler_params=pltpu.CompilerParams(vmem_limit_bytes=VMEM_BYTES),
        name="attention",
    )(*operands)
    return list(out)


def inward_kernel(count, info, gain, *refs):
    weights, pieces, outs = refs[:3], refs[3 : 3 + count], refs[3 + count :]
    width = weights[0].shape[1]
    for piece, out in zip(pieces, outs):
        normed = normalize(piece[...].astype(jnp.float32), gain[...]).astype(jnp.bfloat16)
        for i in range(3):
            out[:, i * width : (i + 1) * width] = dot(normed, weights[i][...]).astype(jnp.bfloat16)


def inward(info, gain, w_qkv, pieces, toks):
    count = len(pieces)
    tokens, width = pieces[0].shape
    local = width // toks

    def columns(i):
        return pl.BlockSpec((width, local), lambda _, info: (0, i * toks + info[0]))

    whole = pl.BlockSpec(memory_space=pltpu.VMEM)
    return pl.pallas_call(
        functools.partial(inward_kernel, count),
        grid_spec=pltpu.PrefetchScalarGridSpec(
            num_scalar_prefetch=1,
            grid=(1,),
            in_specs=[whole] + [columns(i) for i in range(3)] + [whole] * count,
            out_specs=[whole] * count,
        ),
        out_shape=[jax.ShapeDtypeStruct((tokens, 3 * local), jnp.bfloat16)] * count,
        compiler_params=pltpu.CompilerParams(vmem_limit_bytes=VMEM_BYTES),
        name="inward",
    )(info, gain.reshape(1, width), w_qkv, w_qkv, w_qkv, *pieces)


def project_kernel(groups, parts, capacity, messages, info, states, w_out, gain, w_router, slots, *refs):
    pieces, refs = refs[: groups * parts], refs[groups * parts :]
    residual_ref, scores_ref, outgoing = refs[0], refs[1], refs[2:]
    me = info[0]
    width = pieces[0].shape[-1]
    per = pieces[0].shape[-2]
    tokens = states.shape[0]
    total = []
    for g in range(groups):
        rows = pieces[g * parts].shape[0] * per
        value = None
        for d in range(parts):
            piece = pieces[g * parts + d][...].reshape(rows, width)
            term = dot(piece, w_out[pl.ds(pl.multiple_of((me ^ d) * width, width), width), :])
            value = term if value is None else value + term
        total.append(value)
    residual = states[...].astype(jnp.float32) + jnp.concatenate(total, axis=0)
    residual_ref[...] = residual
    normed = normalize(residual, gain[...]).astype(jnp.bfloat16)
    scores_ref[...] = jax.nn.sigmoid(dot_nt(normed, w_router[...]))
    for blocks, ref in zip(messages, outgoing):
        row = iota((len(blocks) * capacity, tokens), 0)
        slot = row + blocks[0] * capacity
        for i in range(1, len(blocks)):
            slot = jnp.where(row >= i * capacity, row + (blocks[i] - i) * capacity, slot)
        chosen = (slot == slots[0:1, :]) | (slot == slots[1:2, :])
        ref[...] = dot(chosen.astype(jnp.bfloat16), normed).astype(jnp.bfloat16)


def project(info, states, w_out, gain, w_router, slots, pieces, capacity, messages):
    groups, parts = len(pieces), len(pieces[0])
    tokens, width = states.shape
    experts = w_router.shape[0]
    flat = [piece for group in pieces for piece in group]
    whole = pl.BlockSpec(memory_space=pltpu.VMEM)
    out = pl.pallas_call(
        functools.partial(project_kernel, groups, parts, capacity, messages),
        in_specs=[pl.BlockSpec(memory_space=pltpu.SMEM)] + [whole] * (5 + len(flat)),
        out_specs=[whole] * (2 + len(messages)),
        out_shape=[
            jax.ShapeDtypeStruct((tokens, width), jnp.float32),
            jax.ShapeDtypeStruct((tokens, experts), jnp.float32),
        ]
        + [jax.ShapeDtypeStruct((len(m) * capacity, width), jnp.bfloat16) for m in messages],
        compiler_params=pltpu.CompilerParams(vmem_limit_bytes=VMEM_BYTES),
        name="project",
    )(info, states, w_out, gain, w_router, slots, *flat)
    return out[0], out[1], list(out[2:])


def expert_kernel(arrays, loads, has_sum, messages, rows_ref, *refs):
    if has_sum:
        sum_ref, refs = refs[0], refs[1:]
    held, refs = refs[:arrays], refs[arrays:]
    outs, (w_s, sems) = refs[:-2], refs[-2:]
    step = pl.program_id(0)
    shards, _, units, _ = w_s.shape
    half = units // 2

    def fetch(i):
        which, start, count, shard, part, at = loads[i]
        return pltpu.make_async_copy(
            held[which].at[pl.ds(start, count)],
            w_s.at[shard, part, pl.ds(at, count)],
            sems.at[i],
        )

    @pl.when(step == 0)
    def _():
        for i in range(len(loads)):
            fetch(i).start()

    rows = rows_ref[...]
    total = sum_ref[...] if has_sum else None
    for s in range(shards):

        @pl.when(step == 0)
        def _():
            for i in range(len(loads)):
                if loads[i][3] == s:
                    fetch(i).wait()

        gate = dot_nt(rows, w_s[s, 0])
        up = dot_nt(rows, w_s[s, 1])
        hidden = (jax.nn.gelu(gate, approximate=True) * up).astype(jnp.bfloat16)
        term = dot(hidden, w_s[s, 2])
        total = term if total is None else total + term
    if not messages:
        outs[0][...] = total
    else:
        value = total.astype(jnp.bfloat16)
        at = 0
        for out in outs:
            start = at % rows.shape[0]

            @pl.when(step == at // rows.shape[0])
            def _():
                out[...] = value[start : start + out.shape[0]]

            at += out.shape[0]


def expert(rows, total, weights, half, capacity, messages, span, largest):
    width = rows.shape[1]
    first, count = span
    held, loads = [], []
    for value, start, row, many, shard, k in weights:
        which = next((i for i, other in enumerate(held) if other is value), len(held))
        if which == len(held):
            held.append(value)
        for part in range(3):
            low, high = max(row, part * half), min(row + many, (part + 1) * half)
            if low < high:
                at = k * half + low - part * half
                loads.append((which, start + low - row, high - low, shard, part, at))
    shards = 1 + max(load[3] for load in loads)
    at_once = max(
        n for n in range(1, count + 1)
        if count % n == 0 and first % n == 0 and n <= largest
        and n % 16 == 0 and n % (2 * capacity) == 0
    )
    block = pl.BlockSpec((at_once, width), lambda i: (first // at_once + i, 0))
    has_sum = total is not None
    if messages:
        sizes = [len(m) * capacity for m in messages]
        out_specs = [pl.BlockSpec((n, width), lambda i: (0, 0)) for n in sizes]
        out_shape = [jax.ShapeDtypeStruct((n, width), jnp.bfloat16) for n in sizes]
    else:
        out_specs, out_shape = [block], [jax.ShapeDtypeStruct(rows.shape, jnp.float32)]
    out = pl.pallas_call(
        functools.partial(expert_kernel, len(held), loads, has_sum, messages),
        grid=(count // at_once,),
        in_specs=[block] + [block] * has_sum + [ANY] * len(held),
        out_specs=out_specs,
        out_shape=out_shape,
        input_output_aliases={1: 0} if has_sum and not messages else {},
        scratch_shapes=[
            pltpu.VMEM((shards, 3, 2 * half, width), jnp.bfloat16),
            pltpu.SemaphoreType.DMA((len(loads),)),
        ],
        compiler_params=pltpu.CompilerParams(vmem_limit_bytes=VMEM_BYTES),
        name="experts",
    )(rows, *([total] if has_sum else []), *held)
    return list(out)


def combine_kernel(capacity, blocks, residual, scores, routes, slots, *refs):
    returned, out = refs[:-1], refs[-1]
    tokens, experts = scores.shape
    values = jnp.concatenate([ref[...] for ref in returned], axis=0)
    column = iota((1, len(blocks) * capacity), 1)
    slot = column + blocks[0] * capacity
    for i in range(1, len(blocks)):
        slot = jnp.where(column >= i * capacity, column + (blocks[i] - i) * capacity, slot)
    mixed = None
    for k in range(TOP):
        gate = jnp.sum(
            jnp.where(iota((tokens, experts), 1) == routes[:, k : k + 1], scores[...], 0.0),
            axis=-1,
            keepdims=True,
        )
        chosen = (slot == slots[:, k : k + 1]).astype(jnp.bfloat16)
        term = dot(chosen, values) * gate
        mixed = term if mixed is None else mixed + term
    out[...] = (residual[...] + mixed).astype(jnp.bfloat16)


def combine(residual, scores, routes, slots, capacity, blocks, returned):
    tokens, width = residual.shape
    whole = pl.BlockSpec(memory_space=pltpu.VMEM)
    return pl.pallas_call(
        functools.partial(combine_kernel, capacity, blocks),
        in_specs=[whole] * (4 + len(returned)),
        out_specs=whole,
        out_shape=jax.ShapeDtypeStruct((tokens, width), jnp.bfloat16),
        compiler_params=pltpu.CompilerParams(vmem_limit_bytes=VMEM_BYTES),
        name="combine",
    )(residual, scores, routes, slots, *returned)


def body(
    states,
    gain_attn,
    w_qkv,
    w_out,
    cache_prev,
    cached_blocks,
    gain_moe,
    w_router,
    routes,
    w_gate_up,
    w_down,
):
    toks, blks = lax.axis_size("tok"), lax.axis_size("blk")
    tok, blk = lax.axis_index("tok"), lax.axis_index("blk")
    tok_low, blk_low = tok % 2, blk % 2
    requests, per, width = states.shape
    tokens = requests * per
    local = width // toks
    experts = w_router.shape[1]
    capacity = tokens * TOP * 5 // (4 * experts)
    number = jnp.arange(requests)
    ahead = (cached_blocks[None, :] > cached_blocks[:, None]) | (
        (cached_blocks[None, :] == cached_blocks[:, None]) & (number[None, :] < number[:, None])
    )
    place = jnp.where(number < 2, 1 - number, number)
    rank = jnp.sum(ahead.astype(jnp.int32), axis=1)
    order = jnp.sum(
        jnp.where(rank[None, :] == place[:, None], number[None, :], 0), axis=1
    ).astype(jnp.int32)
    info = jnp.concatenate([tok[None].astype(jnp.int32), cached_blocks, order])
    flat_states = states.reshape(tokens, width)

    def over_tok(value, d):
        return lax.ppermute(value, "tok", [(i, i ^ d) for i in range(toks)])

    def other_core(value):
        return lax.ppermute(value, "blk", [(i, i ^ 1) for i in range(blks)])

    def heads_of(r, d):
        return lax.dynamic_slice(
            cache_prev, (order[r], 0, 0, (tok ^ d) * local), (1, *cache_prev.shape[1:3], local)
        )

    def spread(values):
        return [values[0]] + [over_tok(values[d], d) for d in range(1, toks)]

    join = lax.optimization_barrier
    far = list(range(2, toks, 2))

    gathered = [flat_states] + [None] * (toks - 1)
    for d in far:
        gathered[d] = over_tok(flat_states, d)
    gathered[1] = over_tok(flat_states, 1)
    gate_up = w_gate_up[0].transpose(0, 2, 1)
    stacked = jnp.concatenate([gate_up, w_down], axis=0)
    half = stacked.shape[1] // 2
    stacked = stacked.reshape(3, 2, half, width)

    def half_of(k):
        return lax.dynamic_index_in_dim(stacked, k, axis=1, keepdims=False).reshape(-1, width)

    kept, given = half_of(blk_low), half_of(1 - blk_low)
    whole, little = 3 * half, half // 32 * 16
    moved = [[heads_of(r, d) for d in range(toks)] for r in range(requests)]
    gathered[::2], gathered[1], given, kept, moved = join(
        (gathered[::2], gathered[1], given, kept, moved)
    )
    taken = other_core(given)
    stays = tok_low == blk_low
    mine = jnp.where(stays, kept, taken)

    def pick(ours, low, high):
        return jnp.where(stays if ours else ~stays, kept[low:high], taken[low:high])

    mine_cut = [pick(True, 0, half), pick(True, half, half + little)]
    mine_cut.append(
        jnp.concatenate([pick(True, half + little, whole), pick(False, whole - half, whole)], axis=0)
    )
    leaving_cut = [pick(False, 0, little), pick(False, little, whole)]

    route_flat = routes.reshape(tokens, TOP)
    assigned = route_flat.reshape(-1) ^ (blk - blk_low + tok_low)
    one_hot = (assigned[:, None] == jnp.arange(experts)[None, :]).astype(jnp.int32)
    ranks = jnp.sum(one_hot * (jnp.cumsum(one_hot, axis=0) - 1), axis=1)
    slots = (assigned * capacity + ranks).reshape(tokens, TOP)
    tables = (route_flat, slots, slots.T, w_router.T)

    for d in far:
        gathered[d + 1] = over_tok(gathered[d], 1)
    cached = [spread(moved[0])]
    far_1 = [over_tok(mine_cut[0], d) for d in far]
    fresh = list(inward(info, gain_attn, w_qkv, gathered[:-1], toks))
    weights_held = (mine, mine_cut[1:], leaving_cut)
    gathered[-1], fresh, cached[0], far_1, moved[1:], weights_held = join(
        (gathered[-1], fresh, cached[0], far_1, moved[1:], weights_held)
    )
    mine, (mine_2, mine_3), leaving_cut = weights_held

    cached.append(spread(moved[1]))
    own_swapped = other_core(mine)
    fresh += list(inward(info, gain_attn, w_qkv, gathered[-1:], toks))
    fresh = [piece.reshape(requests, per, 3 * local) for piece in fresh]
    so_far = attend(info, fresh, cached[0], 0, None, requests)
    cached[1], own_swapped, so_far, far_1, moved[2:], tables = join(
        (cached[1], own_swapped, so_far, far_1, moved[2:], tables)
    )
    route_flat, slots, slots_across, router_across = tables
    for r in range(2, requests):
        cached.append(spread(moved[r]))
        so_far = attend(info, fresh, cached[r - 1], r - 1, so_far, requests)
        if r + 1 < requests:
            cached[r], moved[r + 1 :], so_far = join((cached[r], moved[r + 1 :], so_far))
    far_1_swapped = [other_core(piece) for piece in far_1]
    leaving_cut, mine_2, mine_3, cached[-1], so_far, far_1_swapped = join(
        (leaving_cut, mine_2, mine_3, cached[-1], so_far, far_1_swapped)
    )

    near_1 = over_tok(leaving_cut[0], 1)
    far_2 = [over_tok(mine_2, d) for d in far]
    so_far = attend(info, fresh, cached[-1], requests - 1, so_far, requests)
    decode_cache = so_far[-1]
    back = spread(so_far[:-1])
    back, near_1, far_2, leaving_cut, mine_3 = join((back, near_1, far_2, leaving_cut, mine_3))

    near_2 = over_tok(leaving_cut[1], 1)
    far_3 = [over_tok(mine_3, d) for d in far]

    planes = blks // 2
    opposite = planes // 2
    leaving_by = [[(d, 0), (d, 1)] for d in range(planes) if d != opposite]
    leaving_by += [[(opposite, 1)], [(opposite, 0)]]
    messages = [[2 * d + c for d, c in blocks] for blocks in leaving_by]
    residual, scores, outgoing = project(
        info, flat_states, w_out, gain_moe.reshape(1, width), router_across, slots_across, [back],
        capacity, messages,
    )

    def home(value, plane, column):
        return lax.ppermute(
            value,
            ("tok", "blk"),
            [
                (t * blks + b, (t ^ column) * blks + (b ^ (2 * plane)))
                for t in range(toks)
                for b in range(blks)
            ],
        )

    place = {}
    for blocks, value in zip(leaving_by, outgoing):
        plane = blocks[0][0]
        if plane:
            value = home(value, plane, 0)
        for i, at in enumerate(blocks):
            place[at] = value[i * capacity : (i + 1) * capacity] if len(blocks) > 1 else value
        if blocks == [(opposite, 1)]:
            ahead = [(d, 1) for d in range(opposite)]
            crossed = over_tok(jnp.concatenate([place[at] for at in ahead], axis=0), 1)
            near_2, far_3, place, crossed = join((near_2, far_3, place, crossed))
    inner = whole - half - little
    onward = jnp.concatenate([near_1, near_2[:inner]], axis=0)
    last = [over_tok(onward, d) for d in far]
    first_swapped = other_core(
        jnp.concatenate([near_1, near_2, *far_2, *(value[:inner] for value in far_3)], axis=0)
    )
    behind = [(d, 1) for d in range(opposite, planes)]
    crossed = [crossed, over_tok(jnp.concatenate([place[at] for at in behind], axis=0), 1)]
    far_4 = after([value[inner:] for value in far_3], crossed[1])
    last_4 = [over_tok(value, 1) for value in far_4]
    homeward = [[(d, c)] for c in (1, 0) for d in range(planes) if d != opposite]
    homeward += [[(opposite, c)] for c in (0, 1)]
    for value, blocks in zip(crossed, (ahead, behind)):
        for i, at in enumerate(blocks):
            place[at] = value[i * capacity : (i + 1) * capacity]
    rows = jnp.concatenate([place[at] for blocks in homeward for at in blocks], axis=0)
    weights = [(mine, 0, 0, whole, 0, 0), (own_swapped, 0, 0, whole, 0, 1)]
    weights += [(near_1, 0, 0, little, 1, 0), (near_2, 0, little, whole - little, 1, 0)]
    weights += [(first_swapped, 0, 0, whole, 1, 1)]
    for i in range(len(far)):
        shard, at = 2 + i, whole + i * little
        weights += [(far_1[i], 0, 0, half, shard, 0), (far_1_swapped[i], 0, 0, half, shard, 1)]
        weights += [(far_2[i], 0, half, little, shard, 0)]
        weights += [(first_swapped, at, half, little, shard, 1)]
        at = whole + len(far) * little + i * inner
        weights += [(far_3[i], 0, half + little, inner, shard, 0)]
        weights += [(first_swapped, at, half + little, inner, shard, 1)]
    everything = (0, rows.shape[0])
    total = expert(rows, None, weights, half, capacity, [], everything, 480)[0]
    total, last, last_4 = join((total, last, last_4))
    late = []
    for i in range(len(far)):
        late += [(last[i], 0, 0, whole - half, i, 0), (other_core(last[i]), 0, 0, whole - half, i, 1)]
        late += [(last_4[i], 0, whole - half, half, i, 0)]
        late += [(other_core(last_4[i]), 0, whole - half, half, i, 1)]
    cut = 2 * capacity
    while cut % 16 or rows.shape[0] % cut:
        cut += 2 * capacity
    rest = rows.shape[0] - cut
    parts = rest // capacity
    out = expert(rows, total, late, half, capacity, homeward[:parts], (0, rest), cut)
    total = after(total, *out)
    out += expert(rows, total, late, half, capacity, homeward[parts:], (rest, cut), cut)
    returned, blocks = [], []
    for message, value in zip(homeward, out):
        plane, column = message[0]
        if plane or column:
            value = home(value, plane, column)
        returned.append(value)
        blocks.append(2 * plane + column)
    out_hidden = combine(residual, scores, route_flat, slots, capacity, blocks, returned)
    return (out_hidden.reshape(requests, per, width), decode_cache)


def solution(mesh):
    return jax.shard_map(
        body,
        mesh=mesh,
        in_specs=(
            P("blk", "tok", None),
            P(),
            P(),
            P(),
            P("blk", "tok", None, None),
            P("blk"),
            P(),
            P(),
            P("tok", "blk", None, None),
            P("blk", None, None, "tok"),
            P("blk", "tok", None),
        ),
        out_specs=(P("blk", "tok", None), P("blk", None, None, "tok")),
        check_vma=False,
    )
```

```python
import functools
import math

import jax
import jax.numpy as jnp
from jax import lax
from jax.experimental import pallas as pl
from jax.experimental.pallas import tpu as pltpu
from jax.sharding import PartitionSpec as P

HEAD_DIM = 64
TOP = 2
BLOCK = 128
CHUNK = 512
LANES = 128
HIDDEN_SCORE = -1e30
EPS = 1e-06
VMEM_BYTES = 56 * 1024 * 1024
ANY = pl.BlockSpec(memory_space=pl.ANY)


def normalize(values, gain):
    return (
        values
        * lax.rsqrt(jnp.mean(values * values, -1, keepdims=True) + EPS)
        * gain.astype(jnp.float32)
    )


def after(value, *others):
    return lax.optimization_barrier((value, others))[0]


def dot(left, right):
    return jnp.dot(left, right, preferred_element_type=jnp.float32)


def dot_nt(left, right):
    return lax.dot_general(left, right, (((1,), (1,)), ((), ())), preferred_element_type=jnp.float32)


def iota(shape, dim):
    return lax.broadcasted_iota(jnp.int32, shape, dim)


def attention_kernel(parts, first, chained, info, *refs):
    fresh_in, cached_in, refs = refs[:parts], refs[parts : 2 * parts], refs[2 * parts :]
    if chained:
        refs = refs[parts + 1 :]
    outs, cache_out, refs = refs[:parts], refs[parts], refs[parts + 1 :]
    q_s, k_s, v_s, s_s, m_s, l_s, acc_s, o_s, fresh_s, zero_s, fresh_sem, old_sem = refs
    per, width = outs[0].shape
    group = per * parts
    held = cached_in[0].shape[1]
    unit = zero_s.shape[0]
    heads = width // HEAD_DIM
    me = info[0]
    req = info[1 + cache_out.shape[0] + first + pl.program_id(0)]
    length = info[1 + req] * BLOCK
    zero_s[...] = jnp.zeros_like(zero_s)
    pick_row = iota((unit, 2 * unit), 0) * 2
    pick_col = iota((unit, 2 * unit), 1)
    pick_k = (pick_col == pick_row).astype(jnp.bfloat16)
    pick_v = (pick_col == pick_row + 1).astype(jnp.bfloat16)

    for d in range(parts):
        row = pl.multiple_of((me ^ d) * per, per)
        key, value = fresh_in[d][:, width : 2 * width], fresh_in[d][:, 2 * width :]
        q_s[heads, pl.ds(row, per), :] = fresh_in[d][:, :width]
        k_s[pl.ds(row, per), :] = key
        v_s[pl.ds(row, per), :] = value
        fresh_s[d] = jnp.stack([key, value], axis=1)
        pltpu.make_async_copy(
            fresh_s.at[d], cache_out.at[req, pl.ds(length + row, per)], fresh_sem.at[d]
        ).start()
        for i in range(held // unit):
            at = pl.multiple_of((me ^ d) * held + i * unit, unit)
            block = cached_in[d].at[0, pl.ds(i * unit, unit)]
            sem = old_sem.at[d * (held // unit) + i]

            @pl.when(at < length)
            def _():
                pltpu.make_async_copy(block, cache_out.at[req, pl.ds(at, unit)], sem).start()
                pairs = block[...].reshape(2 * unit, width)
                k_s[pl.ds(group + at, unit), :] = dot(pick_k, pairs).astype(jnp.bfloat16)
                v_s[pl.ds(group + at, unit), :] = dot(pick_v, pairs).astype(jnp.bfloat16)

            @pl.when(at >= length)
            def _():
                pltpu.make_async_copy(
                    zero_s, cache_out.at[req, pl.ds(at + group, unit)], sem
                ).start()

    tail = pl.ds(pl.multiple_of(group + length, BLOCK), CHUNK)
    k_s[tail, :] = jnp.zeros((CHUNK, width), jnp.bfloat16)
    v_s[tail, :] = jnp.zeros((CHUNK, width), jnp.bfloat16)
    chunks = (length + CHUNK - 1) // CHUNK
    own = group // CHUNK
    scale = HEAD_DIM ** (-0.5) * math.log2(math.e)

    def fold(values):
        folded = values[:, :LANES]
        for at in range(LANES, CHUNK, LANES):
            folded = jnp.maximum(folded, values[:, at : at + LANES])
        return folded

    lane_head = iota((group, width), 1) // HEAD_DIM
    for h in range(heads):
        q_s[h] = jnp.where(lane_head == h, q_s[heads], jnp.zeros((), jnp.bfloat16))
    for h in range(heads):
        for c in range(own):
            top = c * CHUNK
            scores = dot_nt(q_s[h, top:, :], k_s[top : top + CHUNK, :])
            rows = group - top
            visible = iota((rows, CHUNK), 1) <= iota((rows, CHUNK), 0)
            scores = jnp.where(visible, scores, HIDDEN_SCORE)
            s_s[c, h, top:, :] = scores
            if c == 0:
                m_s[h] = fold(scores)
            else:
                m_s[h, top:, :] = jnp.maximum(m_s[h, top:, :], fold(scores))

    def score_chunk(c, carry):
        start = pl.multiple_of(c * CHUNK, CHUNK)
        keys = k_s[pl.ds(group + start, CHUNK), :]
        seen = iota((1, CHUNK), 1) + start < length
        for h in range(heads):
            scores = jnp.where(seen, dot_nt(q_s[h], keys), HIDDEN_SCORE)
            s_s[own + c, h] = scores
            m_s[h] = jnp.maximum(m_s[h], fold(scores))
        return carry

    lax.fori_loop(0, chunks, score_chunk, 0)
    for h in range(heads):
        highest = jnp.max(m_s[h], axis=-1, keepdims=True) * scale
        m_s[h] = jnp.broadcast_to(highest, (group, LANES))

    def weigh(c, h, rows):
        pieces = [
            jnp.exp2(s_s[c, h, rows:, at : at + LANES] * scale - m_s[h, rows:, :])
            for at in range(0, CHUNK, LANES)
        ]
        total = pieces[0]
        for piece in pieces[1:]:
            total = total + piece
        return jnp.concatenate([p.astype(jnp.bfloat16) for p in pieces], axis=1), total

    for h in range(heads):
        for c in range(own):
            top = c * CHUNK
            weights, total = weigh(c, h, top)
            product = dot(weights, v_s[top : top + CHUNK, :])
            if c == 0:
                l_s[h] = total
                acc_s[h] = product
            else:
                l_s[h, top:, :] += total
                acc_s[h, top:, :] += product

    def value_chunk(c, carry):
        start = pl.multiple_of(c * CHUNK, CHUNK)
        values = v_s[pl.ds(group + start, CHUNK), :]
        for h in range(heads):
            weights, total = weigh(own + c, h, 0)
            l_s[h] += total
            acc_s[h] += dot(weights, values)
        return carry

    lax.fori_loop(0, chunks, value_chunk, 0)
    result = None
    for h in range(heads):
        value = acc_s[h] / jnp.sum(l_s[h], axis=-1, keepdims=True)
        result = value if h == 0 else jnp.where(lane_head == h, value, result)
    o_s[...] = result
    for d in range(parts):
        row = pl.multiple_of((me ^ d) * per, per)
        outs[d][...] = o_s[pl.ds(row, per), :].astype(jnp.bfloat16)
    for d in range(parts):
        pltpu.make_async_copy(
            fresh_s.at[d], cache_out.at[req, pl.ds(length, per)], fresh_sem.at[d]
        ).wait()
        for i in range(held // unit):
            pltpu.make_async_copy(
                zero_s, cache_out.at[req, pl.ds(0, unit)], old_sem.at[d * (held // unit) + i]
            ).wait()


def attend(info, fresh, cached, first, so_far, requests):
    parts = len(fresh)
    count, held, _, width = cached[0].shape
    per = fresh[0].shape[1]
    group, cache_full = per * parts, held * parts
    unit = math.gcd(held, BLOCK)
    heads = width // HEAD_DIM
    chained = so_far is not None
    slots = (group + cache_full) // CHUNK
    rows = group + cache_full + CHUNK
    def request(r, info):
        return (info[1 + requests + first + r], 0, 0)

    in_specs = [pl.BlockSpec((None, per, 3 * width), request)] * parts
    in_specs += [pl.BlockSpec((1, held, 2, width), lambda r, _: (r, 0, 0, 0))] * parts
    operands = [info, *fresh, *cached]
    aliases = {}
    if chained:
        in_specs += [ANY] * len(so_far)
        aliases = {len(operands) + i: i for i in range(len(so_far))}
        operands += so_far
    out = pl.pallas_call(
        functools.partial(attention_kernel, parts, first, chained),
        grid_spec=pltpu.PrefetchScalarGridSpec(
            num_scalar_prefetch=1,
            grid=(count,),
            in_specs=in_specs,
            out_specs=[pl.BlockSpec((None, per, width), request)] * parts + [ANY],
            scratch_shapes=[
                pltpu.VMEM((heads + 1, group, width), jnp.bfloat16),
                pltpu.VMEM((rows, width), jnp.bfloat16),
                pltpu.VMEM((rows, width), jnp.bfloat16),
                pltpu.VMEM((slots, heads, group, CHUNK), jnp.float32),
                pltpu.VMEM((heads, group, LANES), jnp.float32),
                pltpu.VMEM((heads, group, LANES), jnp.float32),
                pltpu.VMEM((heads, group, width), jnp.float32),
                pltpu.VMEM((group, width), jnp.float32),
                pltpu.VMEM((parts, per, 2, width), jnp.bfloat16),
                pltpu.VMEM((unit, 2, width), jnp.bfloat16),
                pltpu.SemaphoreType.DMA((parts,)),
                pltpu.SemaphoreType.DMA((cache_full // unit,)),
            ],
        ),
        out_shape=[jax.ShapeDtypeStruct((requests, per, width), jnp.bfloat16)] * parts
        + [jax.ShapeDtypeStruct((requests, cache_full + group, 2, width), jnp.bfloat16)],
        input_output_aliases=aliases,
        compiler_params=pltpu.CompilerParams(vmem_limit_bytes=VMEM_BYTES),
        name="attention",
    )(*operands)
    return list(out)


def inward_kernel(cuts, info, gain, *refs):
    weights, refs = refs[:3], refs[3:]
    pieces, outs = refs[: sum(cuts)], refs[sum(cuts) :]
    width = weights[0].shape[1]
    at = 0
    for cut, out in zip(cuts, outs):
        row = 0
        for piece in pieces[at : at + cut]:
            normed = normalize(piece[...].astype(jnp.float32), gain[...]).astype(jnp.bfloat16)
            rows = pl.ds(row, piece.shape[0])
            for i in range(3):
                value = dot(normed, weights[i][...]).astype(jnp.bfloat16)
                out[rows, i * width : (i + 1) * width] = value
            row += piece.shape[0]
        at += cut


def inward(info, gain, w_qkv, pieces, toks):
    flat = [part for piece in pieces for part in piece]
    width = flat[0].shape[1]
    tokens = sum(part.shape[0] for part in pieces[0])
    local = width // toks

    def columns(i):
        return pl.BlockSpec((width, local), lambda _, info: (0, i * toks + info[0]))

    whole = pl.BlockSpec(memory_space=pltpu.VMEM)
    return pl.pallas_call(
        functools.partial(inward_kernel, [len(piece) for piece in pieces]),
        grid_spec=pltpu.PrefetchScalarGridSpec(
            num_scalar_prefetch=1,
            grid=(1,),
            in_specs=[whole] + [columns(i) for i in range(3)] + [whole] * len(flat),
            out_specs=[whole] * len(pieces),
        ),
        out_shape=[jax.ShapeDtypeStruct((tokens, 3 * local), jnp.bfloat16)] * len(pieces),
        compiler_params=pltpu.CompilerParams(vmem_limit_bytes=VMEM_BYTES),
        name="inward",
    )(info, gain.reshape(1, width), w_qkv, w_qkv, w_qkv, *flat)


def project_kernel(groups, parts, capacity, messages, info, states, w_out, gain, w_router, slots, *refs):
    pieces, refs = refs[: groups * parts], refs[groups * parts :]
    residual_ref, scores_ref, outgoing = refs[0], refs[1], refs[2:]
    me = info[0]
    width = pieces[0].shape[-1]
    per = pieces[0].shape[-2]
    tokens = states.shape[0]
    total = []
    for g in range(groups):
        rows = pieces[g * parts].shape[0] * per
        value = None
        for d in range(parts):
            piece = pieces[g * parts + d][...].reshape(rows, width)
            term = dot(piece, w_out[pl.ds(pl.multiple_of((me ^ d) * width, width), width), :])
            value = term if value is None else value + term
        total.append(value)
    residual = states[...].astype(jnp.float32) + jnp.concatenate(total, axis=0)
    residual_ref[...] = residual
    normed = normalize(residual, gain[...]).astype(jnp.bfloat16)
    scores_ref[...] = jax.nn.sigmoid(dot_nt(normed, w_router[...]))
    for blocks, ref in zip(messages, outgoing):
        row = iota((len(blocks) * capacity, tokens), 0)
        slot = row + blocks[0] * capacity
        for i in range(1, len(blocks)):
            slot = jnp.where(row >= i * capacity, row + (blocks[i] - i) * capacity, slot)
        chosen = (slot == slots[0:1, :]) | (slot == slots[1:2, :])
        ref[...] = dot(chosen.astype(jnp.bfloat16), normed).astype(jnp.bfloat16)


def project(info, states, w_out, gain, w_router, slots, pieces, capacity, messages):
    groups, parts = len(pieces), len(pieces[0])
    tokens, width = states.shape
    experts = w_router.shape[0]
    flat = [piece for group in pieces for piece in group]
    whole = pl.BlockSpec(memory_space=pltpu.VMEM)
    out = pl.pallas_call(
        functools.partial(project_kernel, groups, parts, capacity, messages),
        in_specs=[pl.BlockSpec(memory_space=pltpu.SMEM)] + [whole] * (5 + len(flat)),
        out_specs=[whole] * (2 + len(messages)),
        out_shape=[
            jax.ShapeDtypeStruct((tokens, width), jnp.float32),
            jax.ShapeDtypeStruct((tokens, experts), jnp.float32),
        ]
        + [jax.ShapeDtypeStruct((len(m) * capacity, width), jnp.bfloat16) for m in messages],
        compiler_params=pltpu.CompilerParams(vmem_limit_bytes=VMEM_BYTES),
        name="project",
    )(info, states, w_out, gain, w_router, slots, *flat)
    return out[0], out[1], list(out[2:])


def expert_kernel(arrays, loads, has_sum, messages, rows_ref, *refs):
    if has_sum:
        sum_ref, refs = refs[0], refs[1:]
    held, refs = refs[:arrays], refs[arrays:]
    outs, (w_s, sems) = refs[:-2], refs[-2:]
    step = pl.program_id(0)
    shards, _, units, _ = w_s.shape
    half = units // 2

    def fetch(i):
        which, start, count, shard, part, at = loads[i]
        return pltpu.make_async_copy(
            held[which].at[pl.ds(start, count)],
            w_s.at[shard, part, pl.ds(at, count)],
            sems.at[i],
        )

    @pl.when(step == 0)
    def _():
        for i in range(len(loads)):
            fetch(i).start()

    rows = rows_ref[...]
    total = sum_ref[...] if has_sum else None
    for s in range(shards):

        @pl.when(step == 0)
        def _():
            for i in range(len(loads)):
                if loads[i][3] == s:
                    fetch(i).wait()

        gate = dot_nt(rows, w_s[s, 0])
        up = dot_nt(rows, w_s[s, 1])
        hidden = (jax.nn.gelu(gate, approximate=True) * up).astype(jnp.bfloat16)
        term = dot(hidden, w_s[s, 2])
        total = term if total is None else total + term
    if not messages:
        outs[0][...] = total
    else:
        value = total.astype(jnp.bfloat16)
        at = 0
        for out in outs:
            start = at % rows.shape[0]

            @pl.when(step == at // rows.shape[0])
            def _():
                out[...] = value[start : start + out.shape[0]]

            at += out.shape[0]


def expert(rows, total, weights, half, capacity, messages, span, largest):
    width = rows.shape[1]
    first, count = span
    held, loads = [], []
    for value, start, row, many, shard, k in weights:
        which = next((i for i, other in enumerate(held) if other is value), len(held))
        if which == len(held):
            held.append(value)
        for part in range(3):
            low, high = max(row, part * half), min(row + many, (part + 1) * half)
            if low < high:
                at = k * half + low - part * half
                loads.append((which, start + low - row, high - low, shard, part, at))
    shards = 1 + max(load[3] for load in loads)
    at_once = max(
        n for n in range(1, count + 1)
        if count % n == 0 and first % n == 0 and n <= largest
        and n % 16 == 0 and n % (2 * capacity) == 0
    )
    block = pl.BlockSpec((at_once, width), lambda i: (first // at_once + i, 0))
    has_sum = total is not None
    if messages:
        sizes = [len(m) * capacity for m in messages]
        out_specs = [pl.BlockSpec((n, width), lambda i: (0, 0)) for n in sizes]
        out_shape = [jax.ShapeDtypeStruct((n, width), jnp.bfloat16) for n in sizes]
    else:
        out_specs, out_shape = [block], [jax.ShapeDtypeStruct(rows.shape, jnp.float32)]
    out = pl.pallas_call(
        functools.partial(expert_kernel, len(held), loads, has_sum, messages),
        grid=(count // at_once,),
        in_specs=[block] + [block] * has_sum + [ANY] * len(held),
        out_specs=out_specs,
        out_shape=out_shape,
        input_output_aliases={1: 0} if has_sum and not messages else {},
        scratch_shapes=[
            pltpu.VMEM((shards, 3, 2 * half, width), jnp.bfloat16),
            pltpu.SemaphoreType.DMA((len(loads),)),
        ],
        compiler_params=pltpu.CompilerParams(vmem_limit_bytes=VMEM_BYTES),
        name="experts",
    )(rows, *([total] if has_sum else []), *held)
    return list(out)


def combine_kernel(capacity, blocks, residual, scores, routes, slots, *refs):
    returned, out = refs[:-1], refs[-1]
    tokens, experts = scores.shape
    values = jnp.concatenate([ref[...] for ref in returned], axis=0)
    column = iota((1, len(blocks) * capacity), 1)
    slot = column + blocks[0] * capacity
    for i in range(1, len(blocks)):
        slot = jnp.where(column >= i * capacity, column + (blocks[i] - i) * capacity, slot)
    mixed = None
    for k in range(TOP):
        gate = jnp.sum(
            jnp.where(iota((tokens, experts), 1) == routes[:, k : k + 1], scores[...], 0.0),
            axis=-1,
            keepdims=True,
        )
        chosen = (slot == slots[:, k : k + 1]).astype(jnp.bfloat16)
        term = dot(chosen, values) * gate
        mixed = term if mixed is None else mixed + term
    out[...] = (residual[...] + mixed).astype(jnp.bfloat16)


def combine(residual, scores, routes, slots, capacity, blocks, returned):
    tokens, width = residual.shape
    whole = pl.BlockSpec(memory_space=pltpu.VMEM)
    return pl.pallas_call(
        functools.partial(combine_kernel, capacity, blocks),
        in_specs=[whole] * (4 + len(returned)),
        out_specs=whole,
        out_shape=jax.ShapeDtypeStruct((tokens, width), jnp.bfloat16),
        compiler_params=pltpu.CompilerParams(vmem_limit_bytes=VMEM_BYTES),
        name="combine",
    )(residual, scores, routes, slots, *returned)


def body(
    states,
    gain_attn,
    w_qkv,
    w_out,
    cache_prev,
    cached_blocks,
    gain_moe,
    w_router,
    routes,
    w_gate_up,
    w_down,
):
    toks, blks = lax.axis_size("tok"), lax.axis_size("blk")
    tok, blk = lax.axis_index("tok"), lax.axis_index("blk")
    tok_low, blk_low = tok % 2, blk % 2
    requests, per, width = states.shape
    tokens = requests * per
    local = width // toks
    experts = w_router.shape[1]
    capacity = tokens * TOP * 5 // (4 * experts)
    number = jnp.arange(requests)
    ahead = (cached_blocks[None, :] > cached_blocks[:, None]) | (
        (cached_blocks[None, :] == cached_blocks[:, None]) & (number[None, :] < number[:, None])
    )
    place = jnp.where(number < 2, 1 - number, number)
    rank = jnp.sum(ahead.astype(jnp.int32), axis=1)
    order = jnp.sum(
        jnp.where(rank[None, :] == place[:, None], number[None, :], 0), axis=1
    ).astype(jnp.int32)
    info = jnp.concatenate([tok[None].astype(jnp.int32), cached_blocks, order])
    flat_states = states.reshape(tokens, width)

    def over_tok(value, d):
        return lax.ppermute(value, "tok", [(i, i ^ d) for i in range(toks)])

    def other_core(value):
        return lax.ppermute(value, "blk", [(i, i ^ 1) for i in range(blks)])

    def heads_of(r, d):
        return lax.dynamic_slice(
            cache_prev, (order[r], 0, 0, (tok ^ d) * local), (1, *cache_prev.shape[1:3], local)
        )

    def spread(values):
        return [values[0]] + [over_tok(values[d], d) for d in range(1, toks)]

    join = lax.optimization_barrier
    far = list(range(2, toks, 2))

    gathered = [flat_states] + [None] * (toks - 1)
    for d in far:
        gathered[d] = over_tok(flat_states, d)
    gathered[1] = over_tok(flat_states, 1)
    gate_up = w_gate_up[0].transpose(0, 2, 1)
    stacked = jnp.concatenate([gate_up, w_down], axis=0)
    half = stacked.shape[1] // 2
    stacked = stacked.reshape(3, 2, half, width)

    def half_of(k):
        return lax.dynamic_index_in_dim(stacked, k, axis=1, keepdims=False).reshape(-1, width)

    kept, given = half_of(blk_low), half_of(1 - blk_low)
    whole, little = 3 * half, half // 32 * 16
    moved = [[heads_of(r, d) for d in range(toks)] for r in range(requests)]
    gathered[::2], gathered[1], given, kept, moved = join(
        (gathered[::2], gathered[1], given, kept, moved)
    )
    top = tokens // 2
    direct = gathered[:2] + [gathered[d] for d in far]
    across = [(over_tok(gathered[d][:top], 1), over_tok(gathered[1][top:], d)) for d in far]
    cached = [spread(moved[0])]
    fresh = list(inward(info, gain_attn, w_qkv, [[piece] for piece in direct], toks))
    taken = other_core(given)
    stays = tok_low == blk_low
    mine = jnp.where(stays, kept, taken)

    def pick(ours, low, high):
        return jnp.where(stays if ours else ~stays, kept[low:high], taken[low:high])

    inner = whole - little
    mine_cut = [pick(True, 0, little)]
    mine_cut.append(
        jnp.concatenate([pick(True, little, whole), pick(False, whole - half, whole)], axis=0)
    )
    leaving_cut = [pick(False, 0, little), pick(False, little, whole)]
    across, fresh, cached[0], moved[1:], mine, mine_cut, leaving_cut = join(
        (across, fresh, cached[0], moved[1:], mine, mine_cut, leaving_cut)
    )

    cached.append(spread(moved[1]))
    fresh_across = list(inward(info, gain_attn, w_qkv, across, toks))
    ordered = fresh[:2]
    for i in range(len(far)):
        ordered += [fresh[2 + i], fresh_across[i]]
    ordered = [ordered[0], ordered[1]] + ordered[2:]
    fresh = [piece.reshape(requests, per, 3 * local) for piece in ordered]
    so_far = attend(info, fresh, cached[0], 0, None, requests)
    begun = so_far[0]
    cached[1], so_far, moved[2:] = join((cached[1], so_far, moved[2:]))
    for r in range(2, requests):
        cached.append(spread(moved[r]))
        so_far = attend(info, fresh, cached[r - 1], r - 1, so_far, requests)
        if r + 1 < requests:
            cached[r], moved[r + 1 :], so_far = join((cached[r], moved[r + 1 :], so_far))
    own_swapped = other_core(mine)
    route_flat = after(routes, begun).reshape(tokens, TOP)
    assigned = route_flat.reshape(-1) ^ (blk - blk_low + tok_low)
    one_hot = (assigned[:, None] == jnp.arange(experts)[None, :]).astype(jnp.int32)
    ranks = jnp.sum(one_hot * (jnp.cumsum(one_hot, axis=0) - 1), axis=1)
    slots = (assigned * capacity + ranks).reshape(tokens, TOP)
    slots_across = jnp.concatenate([slots[:, k] for k in range(TOP)]).reshape(TOP, tokens)
    router_across = after(w_router, begun).T
    tables = (route_flat, slots, slots_across, router_across)
    leaving_cut, mine_cut, cached[-1], so_far, own_swapped, tables = join(
        (leaving_cut, mine_cut, cached[-1], so_far, own_swapped, tables)
    )
    route_flat, slots, slots_across, router_across = tables

    near_1 = over_tok(leaving_cut[0], 1)
    far_1 = [over_tok(mine_cut[0], d) for d in far]
    so_far = attend(info, fresh, cached[-1], requests - 1, so_far, requests)
    decode_cache = so_far[-1]
    back = spread(so_far[:-1])
    back, near_1, far_1, leaving_cut, mine_cut = join((back, near_1, far_1, leaving_cut, mine_cut))

    near_2 = over_tok(leaving_cut[1], 1)
    far_2 = [over_tok(mine_cut[1], d) for d in far]

    planes = blks // 2
    opposite = planes // 2
    leaving_by = [[(d, 0), (d, 1)] for d in range(planes) if d != opposite]
    leaving_by += [[(opposite, 1)], [(opposite, 0)]]
    messages = [[2 * d + c for d, c in blocks] for blocks in leaving_by]
    residual, scores, outgoing = project(
        info, flat_states, w_out, gain_moe.reshape(1, width), router_across, slots_across, [back],
        capacity, messages,
    )

    def home(value, plane, column):
        return lax.ppermute(
            value,
            ("tok", "blk"),
            [
                (t * blks + b, (t ^ column) * blks + (b ^ (2 * plane)))
                for t in range(toks)
                for b in range(blks)
            ],
        )

    place = {}
    for blocks, value in zip(leaving_by, outgoing):
        plane = blocks[0][0]
        if plane:
            value = home(value, plane, 0)
        for i, at in enumerate(blocks):
            place[at] = value[i * capacity : (i + 1) * capacity] if len(blocks) > 1 else value
    ahead = [(d, 1) for d in range(opposite)]
    crossed = over_tok(jnp.concatenate([place[at] for at in ahead], axis=0), 1)
    near_2, place, crossed = join((near_2, place, crossed))
    onward = jnp.concatenate([near_1, near_2[: inner - half]], axis=0)
    last = [over_tok(onward, d) for d in far]
    first_swapped = other_core(
        jnp.concatenate([near_1, near_2, *far_1, *(value[:inner] for value in far_2)], axis=0)
    )
    behind = [(d, 1) for d in range(opposite, planes)]
    crossed = [crossed, over_tok(jnp.concatenate([place[at] for at in behind], axis=0), 1)]
    onward = after([value[inner:] for value in far_2], crossed[1])
    last_2 = [over_tok(value, 1) for value in onward]
    homeward = [[(d, c)] for c in (1, 0) for d in range(1, planes) if d != opposite]
    homeward += [[(opposite, c)] for c in (0, 1)] + [[(0, 1)], [(0, 0)]]
    for value, blocks in zip(crossed, (ahead, behind)):
        for i, at in enumerate(blocks):
            place[at] = value[i * capacity : (i + 1) * capacity]
    rows = jnp.concatenate([place[at] for blocks in homeward for at in blocks], axis=0)
    weights = [(mine, 0, 0, whole, 0, 0), (own_swapped, 0, 0, whole, 0, 1)]
    weights += [(near_1, 0, 0, little, 1, 0), (near_2, 0, little, whole - little, 1, 0)]
    weights += [(first_swapped, 0, 0, whole, 1, 1)]
    for i in range(len(far)):
        shard, at = 2 + i, whole + i * little
        weights += [(far_1[i], 0, 0, little, shard, 0), (first_swapped, at, 0, little, shard, 1)]
        at = whole + len(far) * little + i * inner
        weights += [(far_2[i], 0, little, inner, shard, 0)]
        weights += [(first_swapped, at, little, inner, shard, 1)]
    everything = (0, rows.shape[0])
    total = expert(rows, None, weights, half, capacity, [], everything, 480)[0]
    total, last, last_2 = join((total, last, last_2))
    late = []
    for i in range(len(far)):
        late += [(last[i], 0, 0, whole - half, i, 0), (other_core(last[i]), 0, 0, whole - half, i, 1)]
        late += [(last_2[i], 0, whole - half, half, i, 0)]
        late += [(other_core(last_2[i]), 0, whole - half, half, i, 1)]
    unit = 2 * capacity
    while unit % 16 or rows.shape[0] % unit:
        unit += 2 * capacity
    rest = rows.shape[0] // unit // 2 * unit
    cut = rows.shape[0] - rest
    parts = rest // capacity
    out = expert(rows, total, late, half, capacity, homeward[:parts], (0, rest), unit)
    total = after(total, *out)
    out += expert(rows, total, late, half, capacity, homeward[parts:], (rest, cut), unit)
    returned, blocks = [], []
    for message, value in zip(homeward, out):
        plane, column = message[0]
        if plane or column:
            value = home(value, plane, column)
        returned.append(value)
        blocks.append(2 * plane + column)
    out_hidden = combine(residual, scores, route_flat, slots, capacity, blocks, returned)
    return (out_hidden.reshape(requests, per, width), decode_cache)


def solution(mesh):
    return jax.shard_map(
        body,
        mesh=mesh,
        in_specs=(
            P("blk", "tok", None),
            P(),
            P(),
            P(),
            P("blk", "tok", None, None),
            P("blk"),
            P(),
            P(),
            P("tok", "blk", None, None),
            P("blk", None, None, "tok"),
            P("blk", "tok", None),
        ),
        out_specs=(P("blk", "tok", None), P("blk", None, None, "tok")),
        check_vma=False,
    )
```

```python
import functools
import math

import jax
import jax.numpy as jnp
from jax import lax
from jax.experimental import pallas as pl
from jax.experimental.pallas import tpu as pltpu
from jax.sharding import PartitionSpec as P

HEAD_DIM = 64
TOP = 2
BLOCK = 128
CHUNK = 512
LANES = 128
HIDDEN_SCORE = -1e30
EPS = 1e-06
VMEM_BYTES = 56 * 1024 * 1024
ANY = pl.BlockSpec(memory_space=pl.ANY)


def normalize(values, gain):
    return (
        values
        * lax.rsqrt(jnp.mean(values * values, -1, keepdims=True) + EPS)
        * gain.astype(jnp.float32)
    )


def after(value, *others):
    return lax.optimization_barrier((value, others))[0]


def dot(left, right):
    return jnp.dot(left, right, preferred_element_type=jnp.float32)


def dot_nt(left, right):
    return lax.dot_general(left, right, (((1,), (1,)), ((), ())), preferred_element_type=jnp.float32)


def iota(shape, dim):
    return lax.broadcasted_iota(jnp.int32, shape, dim)


def attention_kernel(parts, first, chained, info, *refs):
    fresh_in, cached_in, refs = refs[:parts], refs[parts : 2 * parts], refs[2 * parts :]
    if chained:
        refs = refs[parts + 1 :]
    outs, cache_out, refs = refs[:parts], refs[parts], refs[parts + 1 :]
    q_s, k_s, v_s, s_s, m_s, l_s, acc_s, o_s, fresh_s, zero_s, fresh_sem, old_sem = refs
    per, width = outs[0].shape
    group = per * parts
    held = cached_in[0].shape[1]
    unit = zero_s.shape[0]
    heads = width // HEAD_DIM
    me = info[0]
    req = info[1 + cache_out.shape[0] + first + pl.program_id(0)]
    length = info[1 + req] * BLOCK
    zero_s[...] = jnp.zeros_like(zero_s)
    pick_row = iota((unit, 2 * unit), 0) * 2
    pick_col = iota((unit, 2 * unit), 1)
    pick_k = (pick_col == pick_row).astype(jnp.bfloat16)
    pick_v = (pick_col == pick_row + 1).astype(jnp.bfloat16)

    for d in range(parts):
        row = pl.multiple_of((me ^ d) * per, per)
        key, value = fresh_in[d][:, width : 2 * width], fresh_in[d][:, 2 * width :]
        q_s[heads, pl.ds(row, per), :] = fresh_in[d][:, :width]
        k_s[pl.ds(row, per), :] = key
        v_s[pl.ds(row, per), :] = value
        fresh_s[d] = jnp.stack([key, value], axis=1)
        pltpu.make_async_copy(
            fresh_s.at[d], cache_out.at[req, pl.ds(length + row, per)], fresh_sem.at[d]
        ).start()
        for i in range(held // unit):
            at = pl.multiple_of((me ^ d) * held + i * unit, unit)
            block = cached_in[d].at[0, pl.ds(i * unit, unit)]
            sem = old_sem.at[d * (held // unit) + i]

            @pl.when(at < length)
            def _():
                pltpu.make_async_copy(block, cache_out.at[req, pl.ds(at, unit)], sem).start()
                pairs = block[...].reshape(2 * unit, width)
                k_s[pl.ds(group + at, unit), :] = dot(pick_k, pairs).astype(jnp.bfloat16)
                v_s[pl.ds(group + at, unit), :] = dot(pick_v, pairs).astype(jnp.bfloat16)

            @pl.when(at >= length)
            def _():
                pltpu.make_async_copy(
                    zero_s, cache_out.at[req, pl.ds(at + group, unit)], sem
                ).start()

    tail = pl.ds(pl.multiple_of(group + length, BLOCK), CHUNK)
    k_s[tail, :] = jnp.zeros((CHUNK, width), jnp.bfloat16)
    v_s[tail, :] = jnp.zeros((CHUNK, width), jnp.bfloat16)
    chunks = (length + CHUNK - 1) // CHUNK
    own = group // CHUNK
    scale = HEAD_DIM ** (-0.5) * math.log2(math.e)

    def fold(values):
        folded = values[:, :LANES]
        for at in range(LANES, CHUNK, LANES):
            folded = jnp.maximum(folded, values[:, at : at + LANES])
        return folded

    lane_head = iota((group, width), 1) // HEAD_DIM
    for h in range(heads):
        q_s[h] = jnp.where(lane_head == h, q_s[heads], jnp.zeros((), jnp.bfloat16))
    for h in range(heads):
        for c in range(own):
            top = c * CHUNK
            scores = dot_nt(q_s[h, top:, :], k_s[top : top + CHUNK, :])
            rows = group - top
            visible = iota((rows, CHUNK), 1) <= iota((rows, CHUNK), 0)
            scores = jnp.where(visible, scores, HIDDEN_SCORE)
            s_s[c, h, top:, :] = scores
            if c == 0:
                m_s[h] = fold(scores)
            else:
                m_s[h, top:, :] = jnp.maximum(m_s[h, top:, :], fold(scores))

    def score_chunk(c, carry):
        start = pl.multiple_of(c * CHUNK, CHUNK)
        keys = k_s[pl.ds(group + start, CHUNK), :]
        seen = iota((1, CHUNK), 1) + start < length
        for h in range(heads):
            scores = jnp.where(seen, dot_nt(q_s[h], keys), HIDDEN_SCORE)
            s_s[own + c, h] = scores
            m_s[h] = jnp.maximum(m_s[h], fold(scores))
        return carry

    lax.fori_loop(0, chunks, score_chunk, 0)
    for h in range(heads):
        highest = jnp.max(m_s[h], axis=-1, keepdims=True) * scale
        m_s[h] = jnp.broadcast_to(highest, (group, LANES))

    def weigh(c, h, rows):
        pieces = [
            jnp.exp2(s_s[c, h, rows:, at : at + LANES] * scale - m_s[h, rows:, :])
            for at in range(0, CHUNK, LANES)
        ]
        total = pieces[0]
        for piece in pieces[1:]:
            total = total + piece
        return jnp.concatenate([p.astype(jnp.bfloat16) for p in pieces], axis=1), total

    for h in range(heads):
        for c in range(own):
            top = c * CHUNK
            weights, total = weigh(c, h, top)
            product = dot(weights, v_s[top : top + CHUNK, :])
            if c == 0:
                l_s[h] = total
                acc_s[h] = product
            else:
                l_s[h, top:, :] += total
                acc_s[h, top:, :] += product

    def value_chunk(c, carry):
        start = pl.multiple_of(c * CHUNK, CHUNK)
        values = v_s[pl.ds(group + start, CHUNK), :]
        for h in range(heads):
            weights, total = weigh(own + c, h, 0)
            l_s[h] += total
            acc_s[h] += dot(weights, values)
        return carry

    lax.fori_loop(0, chunks, value_chunk, 0)
    result = None
    for h in range(heads):
        value = acc_s[h] / jnp.sum(l_s[h], axis=-1, keepdims=True)
        result = value if h == 0 else jnp.where(lane_head == h, value, result)
    o_s[...] = result
    for d in range(parts):
        row = pl.multiple_of((me ^ d) * per, per)
        outs[d][...] = o_s[pl.ds(row, per), :].astype(jnp.bfloat16)
    for d in range(parts):
        pltpu.make_async_copy(
            fresh_s.at[d], cache_out.at[req, pl.ds(length, per)], fresh_sem.at[d]
        ).wait()
        for i in range(held // unit):
            pltpu.make_async_copy(
                zero_s, cache_out.at[req, pl.ds(0, unit)], old_sem.at[d * (held // unit) + i]
            ).wait()


def attend(info, fresh, cached, first, so_far, requests):
    parts = len(fresh)
    count, held, _, width = cached[0].shape
    per = fresh[0].shape[1]
    group, cache_full = per * parts, held * parts
    unit = math.gcd(held, BLOCK)
    heads = width // HEAD_DIM
    chained = so_far is not None
    slots = (group + cache_full) // CHUNK
    rows = group + cache_full + CHUNK
    def request(r, info):
        return (info[1 + requests + first + r], 0, 0)

    in_specs = [pl.BlockSpec((None, per, 3 * width), request)] * parts
    in_specs += [pl.BlockSpec((1, held, 2, width), lambda r, _: (r, 0, 0, 0))] * parts
    operands = [info, *fresh, *cached]
    aliases = {}
    if chained:
        in_specs += [ANY] * len(so_far)
        aliases = {len(operands) + i: i for i in range(len(so_far))}
        operands += so_far
    out = pl.pallas_call(
        functools.partial(attention_kernel, parts, first, chained),
        grid_spec=pltpu.PrefetchScalarGridSpec(
            num_scalar_prefetch=1,
            grid=(count,),
            in_specs=in_specs,
            out_specs=[pl.BlockSpec((None, per, width), request)] * parts + [ANY],
            scratch_shapes=[
                pltpu.VMEM((heads + 1, group, width), jnp.bfloat16),
                pltpu.VMEM((rows, width), jnp.bfloat16),
                pltpu.VMEM((rows, width), jnp.bfloat16),
                pltpu.VMEM((slots, heads, group, CHUNK), jnp.float32),
                pltpu.VMEM((heads, group, LANES), jnp.float32),
                pltpu.VMEM((heads, group, LANES), jnp.float32),
                pltpu.VMEM((heads, group, width), jnp.float32),
                pltpu.VMEM((group, width), jnp.float32),
                pltpu.VMEM((parts, per, 2, width), jnp.bfloat16),
                pltpu.VMEM((unit, 2, width), jnp.bfloat16),
                pltpu.SemaphoreType.DMA((parts,)),
                pltpu.SemaphoreType.DMA((cache_full // unit,)),
            ],
        ),
        out_shape=[jax.ShapeDtypeStruct((requests, per, width), jnp.bfloat16)] * parts
        + [jax.ShapeDtypeStruct((requests, cache_full + group, 2, width), jnp.bfloat16)],
        input_output_aliases=aliases,
        compiler_params=pltpu.CompilerParams(vmem_limit_bytes=VMEM_BYTES),
        name="attention",
    )(*operands)
    return list(out)


def inward_kernel(cuts, info, gain, *refs):
    weights, refs = refs[:3], refs[3:]
    pieces, outs = refs[: sum(cuts)], refs[sum(cuts) :]
    width = weights[0].shape[1]
    at = 0
    for cut, out in zip(cuts, outs):
        row = 0
        for piece in pieces[at : at + cut]:
            normed = normalize(piece[...].astype(jnp.float32), gain[...]).astype(jnp.bfloat16)
            rows = pl.ds(row, piece.shape[0])
            for i in range(3):
                value = dot(normed, weights[i][...]).astype(jnp.bfloat16)
                out[rows, i * width : (i + 1) * width] = value
            row += piece.shape[0]
        at += cut


def inward(info, gain, w_qkv, pieces, toks):
    flat = [part for piece in pieces for part in piece]
    width = flat[0].shape[1]
    tokens = sum(part.shape[0] for part in pieces[0])
    local = width // toks

    def columns(i):
        return pl.BlockSpec((width, local), lambda _, info: (0, i * toks + info[0]))

    whole = pl.BlockSpec(memory_space=pltpu.VMEM)
    return pl.pallas_call(
        functools.partial(inward_kernel, [len(piece) for piece in pieces]),
        grid_spec=pltpu.PrefetchScalarGridSpec(
            num_scalar_prefetch=1,
            grid=(1,),
            in_specs=[whole] + [columns(i) for i in range(3)] + [whole] * len(flat),
            out_specs=[whole] * len(pieces),
        ),
        out_shape=[jax.ShapeDtypeStruct((tokens, 3 * local), jnp.bfloat16)] * len(pieces),
        compiler_params=pltpu.CompilerParams(vmem_limit_bytes=VMEM_BYTES),
        name="inward",
    )(info, gain.reshape(1, width), w_qkv, w_qkv, w_qkv, *flat)


def project_kernel(groups, parts, capacity, messages, info, states, w_out, gain, w_router, slots, *refs):
    pieces, refs = refs[: groups * parts], refs[groups * parts :]
    residual_ref, scores_ref, outgoing = refs[0], refs[1], refs[2:]
    me = info[0]
    width = pieces[0].shape[-1]
    per = pieces[0].shape[-2]
    tokens = states.shape[0]
    total = []
    for g in range(groups):
        rows = pieces[g * parts].shape[0] * per
        value = None
        for d in range(parts):
            piece = pieces[g * parts + d][...].reshape(rows, width)
            term = dot(piece, w_out[pl.ds(pl.multiple_of((me ^ d) * width, width), width), :])
            value = term if value is None else value + term
        total.append(value)
    residual = states[...].astype(jnp.float32) + jnp.concatenate(total, axis=0)
    residual_ref[...] = residual
    normed = normalize(residual, gain[...]).astype(jnp.bfloat16)
    scores_ref[...] = jax.nn.sigmoid(dot_nt(normed, w_router[...]))
    for blocks, ref in zip(messages, outgoing):
        row = iota((len(blocks) * capacity, tokens), 0)
        slot = row + blocks[0] * capacity
        for i in range(1, len(blocks)):
            slot = jnp.where(row >= i * capacity, row + (blocks[i] - i) * capacity, slot)
        chosen = (slot == slots[0:1, :]) | (slot == slots[1:2, :])
        ref[...] = dot(chosen.astype(jnp.bfloat16), normed).astype(jnp.bfloat16)


def project(info, states, w_out, gain, w_router, slots, pieces, capacity, messages):
    groups, parts = len(pieces), len(pieces[0])
    tokens, width = states.shape
    experts = w_router.shape[0]
    flat = [piece for group in pieces for piece in group]
    whole = pl.BlockSpec(memory_space=pltpu.VMEM)
    out = pl.pallas_call(
        functools.partial(project_kernel, groups, parts, capacity, messages),
        in_specs=[pl.BlockSpec(memory_space=pltpu.SMEM)] + [whole] * (5 + len(flat)),
        out_specs=[whole] * (2 + len(messages)),
        out_shape=[
            jax.ShapeDtypeStruct((tokens, width), jnp.float32),
            jax.ShapeDtypeStruct((tokens, experts), jnp.float32),
        ]
        + [jax.ShapeDtypeStruct((len(m) * capacity, width), jnp.bfloat16) for m in messages],
        compiler_params=pltpu.CompilerParams(vmem_limit_bytes=VMEM_BYTES),
        name="project",
    )(info, states, w_out, gain, w_router, slots, *flat)
    return out[0], out[1], list(out[2:])


def expert_kernel(arrays, loads, has_sum, messages, rows_ref, *refs):
    if has_sum:
        sum_ref, refs = refs[0], refs[1:]
    held, refs = refs[:arrays], refs[arrays:]
    outs, (w_s, sems) = refs[:-2], refs[-2:]
    step = pl.program_id(0)
    shards, _, units, _ = w_s.shape
    half = units // 2

    def fetch(i):
        which, start, count, shard, part, at = loads[i]
        return pltpu.make_async_copy(
            held[which].at[pl.ds(start, count)],
            w_s.at[shard, part, pl.ds(at, count)],
            sems.at[i],
        )

    @pl.when(step == 0)
    def _():
        for i in range(len(loads)):
            fetch(i).start()

    rows = rows_ref[...]
    total = sum_ref[...] if has_sum else None
    for s in range(shards):

        @pl.when(step == 0)
        def _():
            for i in range(len(loads)):
                if loads[i][3] == s:
                    fetch(i).wait()

        gate = dot_nt(rows, w_s[s, 0])
        up = dot_nt(rows, w_s[s, 1])
        hidden = (jax.nn.gelu(gate, approximate=True) * up).astype(jnp.bfloat16)
        term = dot(hidden, w_s[s, 2])
        total = term if total is None else total + term
    if not messages:
        outs[0][...] = total
    else:
        value = total.astype(jnp.bfloat16)
        at = 0
        for out in outs:
            start = at % rows.shape[0]

            @pl.when(step == at // rows.shape[0])
            def _():
                out[...] = value[start : start + out.shape[0]]

            at += out.shape[0]


def expert(rows, total, weights, half, capacity, messages, span, largest):
    width = rows.shape[1]
    first, count = span
    held, loads = [], []
    for value, start, row, many, shard, k in weights:
        which = next((i for i, other in enumerate(held) if other is value), len(held))
        if which == len(held):
            held.append(value)
        for part in range(3):
            low, high = max(row, part * half), min(row + many, (part + 1) * half)
            if low < high:
                at = k * half + low - part * half
                loads.append((which, start + low - row, high - low, shard, part, at))
    shards = 1 + max(load[3] for load in loads)
    at_once = max(
        n for n in range(1, count + 1)
        if count % n == 0 and first % n == 0 and n <= largest
        and n % 16 == 0 and n % (2 * capacity) == 0
    )
    block = pl.BlockSpec((at_once, width), lambda i: (first // at_once + i, 0))
    has_sum = total is not None
    if messages:
        sizes = [len(m) * capacity for m in messages]
        out_specs = [pl.BlockSpec((n, width), lambda i: (0, 0)) for n in sizes]
        out_shape = [jax.ShapeDtypeStruct((n, width), jnp.bfloat16) for n in sizes]
    else:
        out_specs, out_shape = [block], [jax.ShapeDtypeStruct(rows.shape, jnp.float32)]
    out = pl.pallas_call(
        functools.partial(expert_kernel, len(held), loads, has_sum, messages),
        grid=(count // at_once,),
        in_specs=[block] + [block] * has_sum + [ANY] * len(held),
        out_specs=out_specs,
        out_shape=out_shape,
        input_output_aliases={1: 0} if has_sum and not messages else {},
        scratch_shapes=[
            pltpu.VMEM((shards, 3, 2 * half, width), jnp.bfloat16),
            pltpu.SemaphoreType.DMA((len(loads),)),
        ],
        compiler_params=pltpu.CompilerParams(vmem_limit_bytes=62 * 1024 * 1024),
        name="experts",
    )(rows, *([total] if has_sum else []), *held)
    return list(out)


def combine_kernel(capacity, blocks, residual, scores, routes, slots, *refs):
    returned, out = refs[:-1], refs[-1]
    tokens, experts = scores.shape
    values = jnp.concatenate([ref[...] for ref in returned], axis=0)
    column = iota((1, len(blocks) * capacity), 1)
    slot = column + blocks[0] * capacity
    for i in range(1, len(blocks)):
        slot = jnp.where(column >= i * capacity, column + (blocks[i] - i) * capacity, slot)
    mixed = None
    for k in range(TOP):
        gate = jnp.sum(
            jnp.where(iota((tokens, experts), 1) == routes[:, k : k + 1], scores[...], 0.0),
            axis=-1,
            keepdims=True,
        )
        chosen = (slot == slots[:, k : k + 1]).astype(jnp.bfloat16)
        term = dot(chosen, values) * gate
        mixed = term if mixed is None else mixed + term
    out[...] = (residual[...] + mixed).astype(jnp.bfloat16)


def combine(residual, scores, routes, slots, capacity, blocks, returned):
    tokens, width = residual.shape
    whole = pl.BlockSpec(memory_space=pltpu.VMEM)
    return pl.pallas_call(
        functools.partial(combine_kernel, capacity, blocks),
        in_specs=[whole] * (4 + len(returned)),
        out_specs=whole,
        out_shape=jax.ShapeDtypeStruct((tokens, width), jnp.bfloat16),
        compiler_params=pltpu.CompilerParams(vmem_limit_bytes=VMEM_BYTES),
        name="combine",
    )(residual, scores, routes, slots, *returned)


def body(
    states,
    gain_attn,
    w_qkv,
    w_out,
    cache_prev,
    cached_blocks,
    gain_moe,
    w_router,
    routes,
    w_gate_up,
    w_down,
):
    toks, blks = lax.axis_size("tok"), lax.axis_size("blk")
    tok, blk = lax.axis_index("tok"), lax.axis_index("blk")
    tok_low, blk_low = tok % 2, blk % 2
    requests, per, width = states.shape
    tokens = requests * per
    local = width // toks
    experts = w_router.shape[1]
    capacity = tokens * TOP * 5 // (4 * experts)
    number = jnp.arange(requests)
    ahead = (cached_blocks[None, :] > cached_blocks[:, None]) | (
        (cached_blocks[None, :] == cached_blocks[:, None]) & (number[None, :] < number[:, None])
    )
    place = jnp.where(number < 2, 1 - number, number)
    rank = jnp.sum(ahead.astype(jnp.int32), axis=1)
    order = jnp.sum(
        jnp.where(rank[None, :] == place[:, None], number[None, :], 0), axis=1
    ).astype(jnp.int32)
    info = jnp.concatenate([tok[None].astype(jnp.int32), cached_blocks, order])
    flat_states = states.reshape(tokens, width)

    def over_tok(value, d):
        return lax.ppermute(value, "tok", [(i, i ^ d) for i in range(toks)])

    def other_core(value):
        return lax.ppermute(value, "blk", [(i, i ^ 1) for i in range(blks)])

    def heads_of(r, d):
        return lax.dynamic_slice(
            cache_prev, (order[r], 0, 0, (tok ^ d) * local), (1, *cache_prev.shape[1:3], local)
        )

    def spread(values):
        return [values[0]] + [over_tok(values[d], d) for d in range(1, toks)]

    join = lax.optimization_barrier
    far = list(range(2, toks, 2))

    gathered = [flat_states] + [None] * (toks - 1)
    for d in far:
        gathered[d] = over_tok(flat_states, d)
    gathered[1] = over_tok(flat_states, 1)
    gate_up = w_gate_up[0].transpose(0, 2, 1)
    stacked = jnp.concatenate([gate_up, w_down], axis=0)
    half = stacked.shape[1] // 2
    stacked = stacked.reshape(3, 2, half, width)

    def half_of(k):
        return lax.dynamic_index_in_dim(stacked, k, axis=1, keepdims=False).reshape(-1, width)

    kept, given = half_of(blk_low), half_of(1 - blk_low)
    whole, little = 3 * half, half // 32 * 16
    moved = [[heads_of(r, d) for d in range(toks)] for r in range(requests)]
    gathered[::2], gathered[1], given, kept, moved = join(
        (gathered[::2], gathered[1], given, kept, moved)
    )
    top = tokens // 2
    direct = gathered[:2] + [gathered[d] for d in far]
    across = [(over_tok(gathered[d][:top], 1), over_tok(gathered[1][top:], d)) for d in far]
    cached = [spread(moved[0])]
    fresh = list(inward(info, gain_attn, w_qkv, [[piece] for piece in direct], toks))
    taken = other_core(given)
    stays = tok_low == blk_low
    mine = jnp.where(stays, kept, taken)

    def pick(ours, low, high):
        return jnp.where(stays if ours else ~stays, kept[low:high], taken[low:high])

    inner = whole - little
    mine_cut = [pick(True, 0, little)]
    mine_cut.append(
        jnp.concatenate([pick(True, little, whole), pick(False, whole - half, whole)], axis=0)
    )
    leaving_cut = [pick(False, 0, little), pick(False, little, whole)]
    across, fresh, cached[0], moved[1:], mine, mine_cut, leaving_cut = join(
        (across, fresh, cached[0], moved[1:], mine, mine_cut, leaving_cut)
    )

    cached.append(spread(moved[1]))
    fresh_across = list(inward(info, gain_attn, w_qkv, across, toks))
    ordered = fresh[:2]
    for i in range(len(far)):
        ordered += [fresh[2 + i], fresh_across[i]]
    ordered = [ordered[0], ordered[1]] + ordered[2:]
    fresh = [piece.reshape(requests, per, 3 * local) for piece in ordered]
    so_far = attend(info, fresh, cached[0], 0, None, requests)
    begun = so_far[0]
    cached[1], so_far, moved[2:] = join((cached[1], so_far, moved[2:]))
    for r in range(2, requests):
        cached.append(spread(moved[r]))
        so_far = attend(info, fresh, cached[r - 1], r - 1, so_far, requests)
        if r + 1 < requests:
            cached[r], moved[r + 1 :], so_far = join((cached[r], moved[r + 1 :], so_far))
    own_swapped = other_core(mine)
    route_flat = after(routes, begun).reshape(tokens, TOP)
    assigned = route_flat.reshape(-1) ^ (blk - blk_low + tok_low)
    one_hot = (assigned[:, None] == jnp.arange(experts)[None, :]).astype(jnp.int32)
    ranks = jnp.sum(one_hot * (jnp.cumsum(one_hot, axis=0) - 1), axis=1)
    slots = (assigned * capacity + ranks).reshape(tokens, TOP)
    slots_across = jnp.concatenate([slots[:, k] for k in range(TOP)]).reshape(TOP, tokens)
    router_across = after(w_router, begun).T
    tables = (route_flat, slots, slots_across, router_across)
    leaving_cut, mine_cut, cached[-1], so_far, own_swapped, tables = join(
        (leaving_cut, mine_cut, cached[-1], so_far, own_swapped, tables)
    )
    route_flat, slots, slots_across, router_across = tables

    near_1 = over_tok(leaving_cut[0], 1)
    far_1 = [over_tok(mine_cut[0], d) for d in far]
    so_far = attend(info, fresh, cached[-1], requests - 1, so_far, requests)
    decode_cache = so_far[-1]
    back = spread(so_far[:-1])
    back, near_1, far_1, leaving_cut, mine_cut = join((back, near_1, far_1, leaving_cut, mine_cut))

    near_2 = over_tok(leaving_cut[1], 1)
    far_2 = [over_tok(mine_cut[1], d) for d in far]

    planes = blks // 2
    opposite = planes // 2
    leaving_by = [[(d, 0), (d, 1)] for d in range(planes) if d != opposite]
    leaving_by += [[(opposite, 1)], [(opposite, 0)]]
    messages = [[2 * d + c for d, c in blocks] for blocks in leaving_by]
    residual, scores, outgoing = project(
        info, flat_states, w_out, gain_moe.reshape(1, width), router_across, slots_across, [back],
        capacity, messages,
    )

    def home(value, plane, column):
        return lax.ppermute(
            value,
            ("tok", "blk"),
            [
                (t * blks + b, (t ^ column) * blks + (b ^ (2 * plane)))
                for t in range(toks)
                for b in range(blks)
            ],
        )

    place = {}
    for blocks, value in zip(leaving_by, outgoing):
        plane = blocks[0][0]
        if plane:
            value = home(value, plane, 0)
        for i, at in enumerate(blocks):
            place[at] = value[i * capacity : (i + 1) * capacity] if len(blocks) > 1 else value
    ahead = [(d, 1) for d in range(opposite)]
    crossed = over_tok(jnp.concatenate([place[at] for at in ahead], axis=0), 1)
    near_2, place, crossed = join((near_2, place, crossed))
    onward = jnp.concatenate([near_1, near_2[: inner - half]], axis=0)
    last = [over_tok(onward, d) for d in far]
    first_swapped = other_core(
        jnp.concatenate([near_1, near_2, *far_1, *(value[:inner] for value in far_2)], axis=0)
    )
    behind = [(d, 1) for d in range(opposite, planes)]
    crossed = [crossed, over_tok(jnp.concatenate([place[at] for at in behind], axis=0), 1)]
    onward = after([value[inner:] for value in far_2], crossed[1])
    last_2 = [over_tok(value, 1) for value in onward]
    homeward = [[(d, c)] for c in (1, 0) for d in range(1, planes) if d != opposite]
    homeward += [[(opposite, c)] for c in (0, 1)] + [[(0, 1)], [(0, 0)]]
    for value, blocks in zip(crossed, (ahead, behind)):
        for i, at in enumerate(blocks):
            place[at] = value[i * capacity : (i + 1) * capacity]
    rows = jnp.concatenate([place[at] for blocks in homeward for at in blocks], axis=0)
    weights = [(mine, 0, 0, whole, 0, 0), (own_swapped, 0, 0, whole, 0, 1)]
    weights += [(near_1, 0, 0, little, 1, 0), (near_2, 0, little, whole - little, 1, 0)]
    weights += [(first_swapped, 0, 0, whole, 1, 1)]
    for i in range(len(far)):
        shard, at = 2 + i, whole + i * little
        weights += [(far_1[i], 0, 0, little, shard, 0), (first_swapped, at, 0, little, shard, 1)]
        at = whole + len(far) * little + i * inner
        weights += [(far_2[i], 0, little, inner, shard, 0)]
        weights += [(first_swapped, at, little, inner, shard, 1)]
    everything = (0, rows.shape[0])
    total = expert(rows, None, weights, half, capacity, [], everything, 480)[0]
    total, last, last_2 = join((total, last, last_2))
    late = []
    for i in range(len(far)):
        late += [(last[i], 0, 0, whole - half, i, 0), (other_core(last[i]), 0, 0, whole - half, i, 1)]
        late += [(last_2[i], 0, whole - half, half, i, 0)]
        late += [(other_core(last_2[i]), 0, whole - half, half, i, 1)]
    unit = 2 * capacity
    while unit % 16 or rows.shape[0] % unit:
        unit += 2 * capacity
    rest = unit
    cut = rows.shape[0] - rest
    parts = rest // capacity
    out = expert(rows, total, late, half, capacity, homeward[:parts], (0, rest), unit)
    total = after(total, *out)
    out += expert(rows, total, late, half, capacity, homeward[parts:], (rest, cut), unit)
    returned, blocks = [], []
    for message, value in zip(homeward, out):
        plane, column = message[0]
        if plane or column:
            value = home(value, plane, column)
        returned.append(value)
        blocks.append(2 * plane + column)
    out_hidden = combine(residual, scores, route_flat, slots, capacity, blocks, returned)
    return (out_hidden.reshape(requests, per, width), decode_cache)


def solution(mesh):
    return jax.shard_map(
        body,
        mesh=mesh,
        in_specs=(
            P("blk", "tok", None),
            P(),
            P(),
            P(),
            P("blk", "tok", None, None),
            P("blk"),
            P(),
            P(),
            P("tok", "blk", None, None),
            P("blk", None, None, "tok"),
            P("blk", "tok", None),
        ),
        out_specs=(P("blk", "tok", None), P("blk", None, None, "tok")),
        check_vma=False,
    )
```

```python
import functools
import math

import jax
import jax.numpy as jnp
from jax import lax
from jax.experimental import pallas as pl
from jax.experimental.pallas import tpu as pltpu
from jax.sharding import PartitionSpec as P

HEAD_DIM = 64
TOP = 2
BLOCK = 128
CHUNK = 512
LANES = 128
HIDDEN_SCORE = -1e30
EPS = 1e-06
VMEM_BYTES = 56 * 1024 * 1024
SMALL_VMEM_BYTES = 24 * 1024 * 1024
ANY = pl.BlockSpec(memory_space=pl.ANY)


def normalize(values, gain):
    return (
        values
        * lax.rsqrt(jnp.mean(values * values, -1, keepdims=True) + EPS)
        * gain.astype(jnp.float32)
    )


def after(value, *others):
    return lax.optimization_barrier((value, others))[0]


def dot(left, right):
    return jnp.dot(left, right, preferred_element_type=jnp.float32)


def dot_nt(left, right):
    return lax.dot_general(left, right, (((1,), (1,)), ((), ())), preferred_element_type=jnp.float32)


def iota(shape, dim):
    return lax.broadcasted_iota(jnp.int32, shape, dim)


def attention_kernel(parts, first, chained, info, *refs):
    fresh_in, cached_in, refs = refs[:parts], refs[parts : 2 * parts], refs[2 * parts :]
    if chained:
        refs = refs[parts + 1 :]
    outs, cache_out, refs = refs[:parts], refs[parts], refs[parts + 1 :]
    q_s, k_s, v_s, s_s, m_s, l_s, acc_s, o_s, fresh_s, zero_s, fresh_sem, old_sem = refs
    per, width = outs[0].shape
    group = per * parts
    held = cached_in[0].shape[1]
    unit = zero_s.shape[0]
    heads = width // HEAD_DIM
    me = info[0]
    req = info[1 + cache_out.shape[0] + first + pl.program_id(0)]
    length = info[1 + req] * BLOCK
    zero_s[...] = jnp.zeros_like(zero_s)
    pick_row = iota((unit, 2 * unit), 0) * 2
    pick_col = iota((unit, 2 * unit), 1)
    pick_k = (pick_col == pick_row).astype(jnp.bfloat16)
    pick_v = (pick_col == pick_row + 1).astype(jnp.bfloat16)

    for d in range(parts):
        row = pl.multiple_of((me ^ d) * per, per)
        key, value = fresh_in[d][:, width : 2 * width], fresh_in[d][:, 2 * width :]
        q_s[heads, pl.ds(row, per), :] = fresh_in[d][:, :width]
        k_s[pl.ds(row, per), :] = key
        v_s[pl.ds(row, per), :] = value
        fresh_s[d] = jnp.stack([key, value], axis=1)
        pltpu.make_async_copy(
            fresh_s.at[d], cache_out.at[req, pl.ds(length + row, per)], fresh_sem.at[d]
        ).start()
        for i in range(held // unit):
            at = pl.multiple_of((me ^ d) * held + i * unit, unit)
            block = cached_in[d].at[0, pl.ds(i * unit, unit)]
            sem = old_sem.at[d * (held // unit) + i]

            @pl.when(at < length)
            def _():
                pltpu.make_async_copy(block, cache_out.at[req, pl.ds(at, unit)], sem).start()
                pairs = block[...].reshape(2 * unit, width)
                k_s[pl.ds(group + at, unit), :] = dot(pick_k, pairs).astype(jnp.bfloat16)
                v_s[pl.ds(group + at, unit), :] = dot(pick_v, pairs).astype(jnp.bfloat16)

            @pl.when(at >= length)
            def _():
                pltpu.make_async_copy(
                    zero_s, cache_out.at[req, pl.ds(at + group, unit)], sem
                ).start()

    tail = pl.ds(pl.multiple_of(group + length, BLOCK), CHUNK)
    k_s[tail, :] = jnp.zeros((CHUNK, width), jnp.bfloat16)
    v_s[tail, :] = jnp.zeros((CHUNK, width), jnp.bfloat16)
    chunks = (length + CHUNK - 1) // CHUNK
    own = group // CHUNK
    scale = HEAD_DIM ** (-0.5) * math.log2(math.e)

    def fold(values):
        folded = values[:, :LANES]
        for at in range(LANES, CHUNK, LANES):
            folded = jnp.maximum(folded, values[:, at : at + LANES])
        return folded

    lane_head = iota((group, width), 1) // HEAD_DIM
    for h in range(heads):
        q_s[h] = jnp.where(lane_head == h, q_s[heads], jnp.zeros((), jnp.bfloat16))
    for h in range(heads):
        for c in range(own):
            top = c * CHUNK
            scores = dot_nt(q_s[h, top:, :], k_s[top : top + CHUNK, :])
            rows = group - top
            visible = iota((rows, CHUNK), 1) <= iota((rows, CHUNK), 0)
            scores = jnp.where(visible, scores, HIDDEN_SCORE)
            s_s[c, h, top:, :] = scores
            if c == 0:
                m_s[h] = fold(scores)
            else:
                m_s[h, top:, :] = jnp.maximum(m_s[h, top:, :], fold(scores))

    def score_chunk(c, carry):
        start = pl.multiple_of(c * CHUNK, CHUNK)
        keys = k_s[pl.ds(group + start, CHUNK), :]
        seen = iota((1, CHUNK), 1) + start < length
        for h in range(heads):
            scores = jnp.where(seen, dot_nt(q_s[h], keys), HIDDEN_SCORE)
            s_s[own + c, h] = scores
            m_s[h] = jnp.maximum(m_s[h], fold(scores))
        return carry

    lax.fori_loop(0, chunks, score_chunk, 0)
    for h in range(heads):
        highest = jnp.max(m_s[h], axis=-1, keepdims=True) * scale
        m_s[h] = jnp.broadcast_to(highest, (group, LANES))

    def weigh(c, h, rows):
        pieces = [
            jnp.exp2(s_s[c, h, rows:, at : at + LANES] * scale - m_s[h, rows:, :])
            for at in range(0, CHUNK, LANES)
        ]
        total = pieces[0]
        for piece in pieces[1:]:
            total = total + piece
        return jnp.concatenate([p.astype(jnp.bfloat16) for p in pieces], axis=1), total

    for h in range(heads):
        for c in range(own):
            top = c * CHUNK
            weights, total = weigh(c, h, top)
            product = dot(weights, v_s[top : top + CHUNK, :])
            if c == 0:
                l_s[h] = total
                acc_s[h] = product
            else:
                l_s[h, top:, :] += total
                acc_s[h, top:, :] += product

    def value_chunk(c, carry):
        start = pl.multiple_of(c * CHUNK, CHUNK)
        values = v_s[pl.ds(group + start, CHUNK), :]
        for h in range(heads):
            weights, total = weigh(own + c, h, 0)
            l_s[h] += total
            acc_s[h] += dot(weights, values)
        return carry

    lax.fori_loop(0, chunks, value_chunk, 0)
    result = None
    for h in range(heads):
        value = acc_s[h] / jnp.sum(l_s[h], axis=-1, keepdims=True)
        result = value if h == 0 else jnp.where(lane_head == h, value, result)
    o_s[...] = result
    for d in range(parts):
        row = pl.multiple_of((me ^ d) * per, per)
        outs[d][...] = o_s[pl.ds(row, per), :].astype(jnp.bfloat16)
    for d in range(parts):
        pltpu.make_async_copy(
            fresh_s.at[d], cache_out.at[req, pl.ds(length, per)], fresh_sem.at[d]
        ).wait()
        for i in range(held // unit):
            pltpu.make_async_copy(
                zero_s, cache_out.at[req, pl.ds(0, unit)], old_sem.at[d * (held // unit) + i]
            ).wait()


def attend(info, fresh, cached, first, so_far, requests):
    parts = len(fresh)
    count, held, _, width = cached[0].shape
    per = fresh[0].shape[1]
    group, cache_full = per * parts, held * parts
    unit = math.gcd(held, BLOCK)
    heads = width // HEAD_DIM
    chained = so_far is not None
    slots = (group + cache_full) // CHUNK
    rows = group + cache_full + CHUNK
    def request(r, info):
        return (info[1 + requests + first + r], 0, 0)

    in_specs = [pl.BlockSpec((None, per, 3 * width), request)] * parts
    in_specs += [pl.BlockSpec((1, held, 2, width), lambda r, _: (r, 0, 0, 0))] * parts
    operands = [info, *fresh, *cached]
    aliases = {}
    if chained:
        in_specs += [ANY] * len(so_far)
        aliases = {len(operands) + i: i for i in range(len(so_far))}
        operands += so_far
    out = pl.pallas_call(
        functools.partial(attention_kernel, parts, first, chained),
        grid_spec=pltpu.PrefetchScalarGridSpec(
            num_scalar_prefetch=1,
            grid=(count,),
            in_specs=in_specs,
            out_specs=[pl.BlockSpec((None, per, width), request)] * parts + [ANY],
            scratch_shapes=[
                pltpu.VMEM((heads + 1, group, width), jnp.bfloat16),
                pltpu.VMEM((rows, width), jnp.bfloat16),
                pltpu.VMEM((rows, width), jnp.bfloat16),
                pltpu.VMEM((slots, heads, group, CHUNK), jnp.float32),
                pltpu.VMEM((heads, group, LANES), jnp.float32),
                pltpu.VMEM((heads, group, LANES), jnp.float32),
                pltpu.VMEM((heads, group, width), jnp.float32),
                pltpu.VMEM((group, width), jnp.float32),
                pltpu.VMEM((parts, per, 2, width), jnp.bfloat16),
                pltpu.VMEM((unit, 2, width), jnp.bfloat16),
                pltpu.SemaphoreType.DMA((parts,)),
                pltpu.SemaphoreType.DMA((cache_full // unit,)),
            ],
        ),
        out_shape=[jax.ShapeDtypeStruct((requests, per, width), jnp.bfloat16)] * parts
        + [jax.ShapeDtypeStruct((requests, cache_full + group, 2, width), jnp.bfloat16)],
        input_output_aliases=aliases,
        compiler_params=pltpu.CompilerParams(vmem_limit_bytes=VMEM_BYTES),
        name="attention",
    )(*operands)
    return list(out)


def inward_kernel(cuts, info, gain, *refs):
    weights, refs = refs[:3], refs[3:]
    pieces, outs = refs[: sum(cuts)], refs[sum(cuts) :]
    width = weights[0].shape[1]
    at = 0
    for cut, out in zip(cuts, outs):
        row = 0
        for piece in pieces[at : at + cut]:
            normed = normalize(piece[...].astype(jnp.float32), gain[...]).astype(jnp.bfloat16)
            rows = pl.ds(row, piece.shape[0])
            for i in range(3):
                value = dot(normed, weights[i][...]).astype(jnp.bfloat16)
                out[rows, i * width : (i + 1) * width] = value
            row += piece.shape[0]
        at += cut


def inward(info, gain, w_qkv, pieces, toks):
    flat = [part for piece in pieces for part in piece]
    width = flat[0].shape[1]
    tokens = sum(part.shape[0] for part in pieces[0])
    local = width // toks

    def columns(i):
        return pl.BlockSpec((width, local), lambda _, info: (0, i * toks + info[0]))

    whole = pl.BlockSpec(memory_space=pltpu.VMEM)
    return pl.pallas_call(
        functools.partial(inward_kernel, [len(piece) for piece in pieces]),
        grid_spec=pltpu.PrefetchScalarGridSpec(
            num_scalar_prefetch=1,
            grid=(1,),
            in_specs=[whole] + [columns(i) for i in range(3)] + [whole] * len(flat),
            out_specs=[whole] * len(pieces),
        ),
        out_shape=[jax.ShapeDtypeStruct((tokens, 3 * local), jnp.bfloat16)] * len(pieces),
        compiler_params=pltpu.CompilerParams(vmem_limit_bytes=SMALL_VMEM_BYTES),
        name="inward",
    )(info, gain.reshape(1, width), w_qkv, w_qkv, w_qkv, *flat)


def project_kernel(groups, parts, capacity, messages, info, states, w_out, gain, w_router, slots, *refs):
    pieces, refs = refs[: groups * parts], refs[groups * parts :]
    residual_ref, scores_ref, outgoing = refs[0], refs[1], refs[2:]
    me = info[0]
    width = pieces[0].shape[-1]
    per = pieces[0].shape[-2]
    tokens = states.shape[0]
    total = []
    for g in range(groups):
        rows = pieces[g * parts].shape[0] * per
        value = None
        for d in range(parts):
            piece = pieces[g * parts + d][...].reshape(rows, width)
            term = dot(piece, w_out[pl.ds(pl.multiple_of((me ^ d) * width, width), width), :])
            value = term if value is None else value + term
        total.append(value)
    residual = states[...].astype(jnp.float32) + jnp.concatenate(total, axis=0)
    residual_ref[...] = residual
    normed = normalize(residual, gain[...]).astype(jnp.bfloat16)
    scores_ref[...] = jax.nn.sigmoid(dot_nt(normed, w_router[...]))
    for blocks, ref in zip(messages, outgoing):
        row = iota((len(blocks) * capacity, tokens), 0)
        slot = row + blocks[0] * capacity
        for i in range(1, len(blocks)):
            slot = jnp.where(row >= i * capacity, row + (blocks[i] - i) * capacity, slot)
        chosen = (slot == slots[0:1, :]) | (slot == slots[1:2, :])
        ref[...] = dot(chosen.astype(jnp.bfloat16), normed).astype(jnp.bfloat16)


def project(info, states, w_out, gain, w_router, slots, pieces, capacity, messages):
    groups, parts = len(pieces), len(pieces[0])
    tokens, width = states.shape
    experts = w_router.shape[0]
    flat = [piece for group in pieces for piece in group]
    whole = pl.BlockSpec(memory_space=pltpu.VMEM)
    out = pl.pallas_call(
        functools.partial(project_kernel, groups, parts, capacity, messages),
        in_specs=[pl.BlockSpec(memory_space=pltpu.SMEM)] + [whole] * (5 + len(flat)),
        out_specs=[whole] * (2 + len(messages)),
        out_shape=[
            jax.ShapeDtypeStruct((tokens, width), jnp.float32),
            jax.ShapeDtypeStruct((tokens, experts), jnp.float32),
        ]
        + [jax.ShapeDtypeStruct((len(m) * capacity, width), jnp.bfloat16) for m in messages],
        compiler_params=pltpu.CompilerParams(vmem_limit_bytes=SMALL_VMEM_BYTES),
        name="project",
    )(info, states, w_out, gain, w_router, slots, *flat)
    return out[0], out[1], list(out[2:])


def expert_kernel(arrays, loads, has_sum, messages, rows_ref, *refs):
    if has_sum:
        sum_ref, refs = refs[0], refs[1:]
    held, refs = refs[:arrays], refs[arrays:]
    outs, (w_s, sems) = refs[:-2], refs[-2:]
    step = pl.program_id(0)
    shards, _, units, _ = w_s.shape
    half = units // 2

    def fetch(i):
        which, start, count, shard, part, at = loads[i]
        return pltpu.make_async_copy(
            held[which].at[pl.ds(start, count)],
            w_s.at[shard, part, pl.ds(at, count)],
            sems.at[i],
        )

    @pl.when(step == 0)
    def _():
        for i in range(len(loads)):
            fetch(i).start()

    rows = rows_ref[...]
    total = sum_ref[...] if has_sum else None
    for s in range(shards):

        @pl.when(step == 0)
        def _():
            for i in range(len(loads)):
                if loads[i][3] == s:
                    fetch(i).wait()

        gate = dot_nt(rows, w_s[s, 0])
        up = dot_nt(rows, w_s[s, 1])
        hidden = (jax.nn.gelu(gate, approximate=True) * up).astype(jnp.bfloat16)
        term = dot(hidden, w_s[s, 2])
        total = term if total is None else total + term
    if not messages:
        outs[0][...] = total
    else:
        value = total.astype(jnp.bfloat16)
        at = 0
        for out in outs:
            start = at % rows.shape[0]

            @pl.when(step == at // rows.shape[0])
            def _():
                out[...] = value[start : start + out.shape[0]]

            at += out.shape[0]


def expert(rows, total, weights, half, capacity, messages, span, largest):
    width = rows.shape[1]
    first, count = span
    held, loads = [], []
    for value, start, row, many, shard, k in weights:
        which = next((i for i, other in enumerate(held) if other is value), len(held))
        if which == len(held):
            held.append(value)
        for part in range(3):
            low, high = max(row, part * half), min(row + many, (part + 1) * half)
            if low < high:
                at = k * half + low - part * half
                loads.append((which, start + low - row, high - low, shard, part, at))
    shards = 1 + max(load[3] for load in loads)
    at_once = max(
        n for n in range(1, count + 1)
        if count % n == 0 and first % n == 0 and n <= largest
        and n % 16 == 0 and n % (2 * capacity) == 0
    )
    block = pl.BlockSpec((at_once, width), lambda i: (first // at_once + i, 0))
    has_sum = total is not None
    if messages:
        sizes = [len(m) * capacity for m in messages]
        out_specs = [pl.BlockSpec((n, width), lambda i: (0, 0)) for n in sizes]
        out_shape = [jax.ShapeDtypeStruct((n, width), jnp.bfloat16) for n in sizes]
    else:
        out_specs, out_shape = [block], [jax.ShapeDtypeStruct(rows.shape, jnp.float32)]
    out = pl.pallas_call(
        functools.partial(expert_kernel, len(held), loads, has_sum, messages),
        grid=(count // at_once,),
        in_specs=[block] + [block] * has_sum + [ANY] * len(held),
        out_specs=out_specs,
        out_shape=out_shape,
        input_output_aliases={1: 0} if has_sum and not messages else {},
        scratch_shapes=[
            pltpu.VMEM((shards, 3, 2 * half, width), jnp.bfloat16),
            pltpu.SemaphoreType.DMA((len(loads),)),
        ],
        compiler_params=pltpu.CompilerParams(vmem_limit_bytes=62 * 1024 * 1024),
        name="experts",
    )(rows, *([total] if has_sum else []), *held)
    return list(out)


def combine_kernel(capacity, blocks, residual, scores, routes, slots, *refs):
    returned, out = refs[:-1], refs[-1]
    tokens, experts = scores.shape
    values = jnp.concatenate([ref[...] for ref in returned], axis=0)
    column = iota((1, len(blocks) * capacity), 1)
    slot = column + blocks[0] * capacity
    for i in range(1, len(blocks)):
        slot = jnp.where(column >= i * capacity, column + (blocks[i] - i) * capacity, slot)
    mixed = None
    for k in range(TOP):
        gate = jnp.sum(
            jnp.where(iota((tokens, experts), 1) == routes[:, k : k + 1], scores[...], 0.0),
            axis=-1,
            keepdims=True,
        )
        chosen = (slot == slots[:, k : k + 1]).astype(jnp.bfloat16)
        term = dot(chosen, values) * gate
        mixed = term if mixed is None else mixed + term
    out[...] = (residual[...] + mixed).astype(jnp.bfloat16)


def combine(residual, scores, routes, slots, capacity, blocks, returned):
    tokens, width = residual.shape
    whole = pl.BlockSpec(memory_space=pltpu.VMEM)
    return pl.pallas_call(
        functools.partial(combine_kernel, capacity, blocks),
        in_specs=[whole] * (4 + len(returned)),
        out_specs=whole,
        out_shape=jax.ShapeDtypeStruct((tokens, width), jnp.bfloat16),
        compiler_params=pltpu.CompilerParams(vmem_limit_bytes=SMALL_VMEM_BYTES),
        name="combine",
    )(residual, scores, routes, slots, *returned)


def body(
    states,
    gain_attn,
    w_qkv,
    w_out,
    cache_prev,
    cached_blocks,
    gain_moe,
    w_router,
    routes,
    w_gate_up,
    w_down,
):
    toks, blks = lax.axis_size("tok"), lax.axis_size("blk")
    tok, blk = lax.axis_index("tok"), lax.axis_index("blk")
    tok_low, blk_low = tok % 2, blk % 2
    requests, per, width = states.shape
    tokens = requests * per
    local = width // toks
    experts = w_router.shape[1]
    capacity = tokens * TOP * 5 // (4 * experts)
    number = jnp.arange(requests)
    ahead = (cached_blocks[None, :] > cached_blocks[:, None]) | (
        (cached_blocks[None, :] == cached_blocks[:, None]) & (number[None, :] < number[:, None])
    )
    place = jnp.where(number < 2, 1 - number, number)
    rank = jnp.sum(ahead.astype(jnp.int32), axis=1)
    order = jnp.sum(
        jnp.where(rank[None, :] == place[:, None], number[None, :], 0), axis=1
    ).astype(jnp.int32)
    info = jnp.concatenate([tok[None].astype(jnp.int32), cached_blocks, order])
    flat_states = states.reshape(tokens, width)

    def over_tok(value, d):
        return lax.ppermute(value, "tok", [(i, i ^ d) for i in range(toks)])

    def other_core(value):
        return lax.ppermute(value, "blk", [(i, i ^ 1) for i in range(blks)])

    def heads_of(r, d):
        return lax.dynamic_slice(
            cache_prev, (order[r], 0, 0, (tok ^ d) * local), (1, *cache_prev.shape[1:3], local)
        )

    def spread(values):
        return [values[0]] + [over_tok(values[d], d) for d in range(1, toks)]

    join = lax.optimization_barrier
    far = list(range(2, toks, 2))

    gathered = [flat_states] + [None] * (toks - 1)
    for d in far:
        gathered[d] = over_tok(flat_states, d)
    gathered[1] = over_tok(flat_states, 1)
    gate_up = w_gate_up[0].transpose(0, 2, 1)
    stacked = jnp.concatenate([gate_up, w_down], axis=0)
    half = stacked.shape[1] // 2
    stacked = stacked.reshape(3, 2, half, width)

    def half_of(k):
        return lax.dynamic_index_in_dim(stacked, k, axis=1, keepdims=False).reshape(-1, width)

    kept, given = half_of(blk_low), half_of(1 - blk_low)
    whole, little = 3 * half, half // 32 * 16
    moved = [[heads_of(r, d) for d in range(toks)] for r in range(requests)]
    gathered[::2], gathered[1], given, kept, moved = join(
        (gathered[::2], gathered[1], given, kept, moved)
    )
    top = tokens // 2
    direct = gathered[:2] + [gathered[d] for d in far]
    across = [(over_tok(gathered[d][:top], 1), over_tok(gathered[1][top:], d)) for d in far]
    cached = [spread(moved[0])]
    fresh = list(inward(info, gain_attn, w_qkv, [[piece] for piece in direct], toks))
    taken = other_core(given)
    stays = tok_low == blk_low
    mine = jnp.where(stays, kept, taken)

    def pick(ours, low, high):
        return jnp.where(stays if ours else ~stays, kept[low:high], taken[low:high])

    inner = whole - little
    mine_cut = [pick(True, 0, little)]
    mine_cut.append(
        jnp.concatenate([pick(True, little, whole), pick(False, whole - half, whole)], axis=0)
    )
    leaving_cut = [pick(False, 0, little), pick(False, little, whole)]
    across, fresh, cached[0], moved[1:], mine, mine_cut, leaving_cut = join(
        (across, fresh, cached[0], moved[1:], mine, mine_cut, leaving_cut)
    )

    cached.append(spread(moved[1]))
    fresh_across = list(inward(info, gain_attn, w_qkv, across, toks))
    ordered = fresh[:2]
    for i in range(len(far)):
        ordered += [fresh[2 + i], fresh_across[i]]
    ordered = [ordered[0], ordered[1]] + ordered[2:]
    fresh = [piece.reshape(requests, per, 3 * local) for piece in ordered]
    so_far = attend(info, fresh, cached[0], 0, None, requests)
    begun = so_far[0]
    cached[1], so_far, moved[2:] = join((cached[1], so_far, moved[2:]))
    for r in range(2, requests):
        cached.append(spread(moved[r]))
        so_far = attend(info, fresh, cached[r - 1], r - 1, so_far, requests)
        if r + 1 < requests:
            cached[r], moved[r + 1 :], so_far = join((cached[r], moved[r + 1 :], so_far))
    own_swapped = other_core(mine)
    route_flat = after(routes, begun).reshape(tokens, TOP)
    assigned = route_flat.reshape(-1) ^ (blk - blk_low + tok_low)
    one_hot = (assigned[:, None] == jnp.arange(experts)[None, :]).astype(jnp.int32)
    ranks = jnp.sum(one_hot * (jnp.cumsum(one_hot, axis=0) - 1), axis=1)
    slots = (assigned * capacity + ranks).reshape(tokens, TOP)
    slots_across = jnp.concatenate([slots[:, k] for k in range(TOP)]).reshape(TOP, tokens)
    router_across = after(w_router, begun).T
    tables = (route_flat, slots, slots_across, router_across)
    leaving_cut, mine_cut, cached[-1], so_far, own_swapped, tables = join(
        (leaving_cut, mine_cut, cached[-1], so_far, own_swapped, tables)
    )
    route_flat, slots, slots_across, router_across = tables

    near_1 = over_tok(leaving_cut[0], 1)
    far_1 = [over_tok(mine_cut[0], d) for d in far]
    so_far = attend(info, fresh, cached[-1], requests - 1, so_far, requests)
    decode_cache = so_far[-1]
    back = spread(so_far[:-1])
    back, near_1, far_1, leaving_cut, mine_cut = join((back, near_1, far_1, leaving_cut, mine_cut))

    near_2 = over_tok(leaving_cut[1], 1)
    far_2 = [over_tok(mine_cut[1], d) for d in far]

    planes = blks // 2
    opposite = planes // 2
    leaving_by = [[(d, 0), (d, 1)] for d in range(planes) if d != opposite]
    leaving_by += [[(opposite, 1)], [(opposite, 0)]]
    messages = [[2 * d + c for d, c in blocks] for blocks in leaving_by]
    residual, scores, outgoing = project(
        info, flat_states, w_out, gain_moe.reshape(1, width), router_across, slots_across, [back],
        capacity, messages,
    )

    def home(value, plane, column):
        return lax.ppermute(
            value,
            ("tok", "blk"),
            [
                (t * blks + b, (t ^ column) * blks + (b ^ (2 * plane)))
                for t in range(toks)
                for b in range(blks)
            ],
        )

    place = {}
    for blocks, value in zip(leaving_by, outgoing):
        plane = blocks[0][0]
        if plane:
            value = home(value, plane, 0)
        for i, at in enumerate(blocks):
            place[at] = value[i * capacity : (i + 1) * capacity] if len(blocks) > 1 else value
    ahead = [(d, 1) for d in range(opposite)]
    crossed = over_tok(jnp.concatenate([place[at] for at in ahead], axis=0), 1)
    near_2, place, crossed = join((near_2, place, crossed))
    onward = jnp.concatenate([near_1, near_2[: inner - half]], axis=0)
    last = [over_tok(onward, d) for d in far]
    first_swapped = other_core(
        jnp.concatenate([near_1, near_2, *far_1, *(value[:inner] for value in far_2)], axis=0)
    )
    behind = [(d, 1) for d in range(opposite, planes)]
    crossed = [crossed, over_tok(jnp.concatenate([place[at] for at in behind], axis=0), 1)]
    onward = after([value[inner:] for value in far_2], crossed[1])
    last_2 = [over_tok(value, 1) for value in onward]
    homeward = [[(d, c)] for c in (1, 0) for d in range(1, planes) if d != opposite]
    homeward += [[(opposite, c)] for c in (0, 1)] + [[(0, 1)], [(0, 0)]]
    for value, blocks in zip(crossed, (ahead, behind)):
        for i, at in enumerate(blocks):
            place[at] = value[i * capacity : (i + 1) * capacity]
    rows = jnp.concatenate([place[at] for blocks in homeward for at in blocks], axis=0)
    weights = [(mine, 0, 0, whole, 0, 0), (own_swapped, 0, 0, whole, 0, 1)]
    weights += [(near_1, 0, 0, little, 1, 0), (near_2, 0, little, whole - little, 1, 0)]
    weights += [(first_swapped, 0, 0, whole, 1, 1)]
    for i in range(len(far)):
        shard, at = 2 + i, whole + i * little
        weights += [(far_1[i], 0, 0, little, shard, 0), (first_swapped, at, 0, little, shard, 1)]
        at = whole + len(far) * little + i * inner
        weights += [(far_2[i], 0, little, inner, shard, 0)]
        weights += [(first_swapped, at, little, inner, shard, 1)]
    everything = (0, rows.shape[0])
    total = expert(rows, None, weights, half, capacity, [], everything, 480)[0]
    total, last, last_2 = join((total, last, last_2))
    late = []
    for i in range(len(far)):
        late += [(last[i], 0, 0, whole - half, i, 0), (other_core(last[i]), 0, 0, whole - half, i, 1)]
        late += [(last_2[i], 0, whole - half, half, i, 0)]
        late += [(other_core(last_2[i]), 0, whole - half, half, i, 1)]
    unit = 2 * capacity
    while unit % 16 or rows.shape[0] % unit:
        unit += 2 * capacity
    rest = unit
    cut = rows.shape[0] - rest
    parts = rest // capacity
    out = expert(rows, total, late, half, capacity, homeward[:parts], (0, rest), unit)
    total = after(total, *out)
    out += expert(rows, total, late, half, capacity, homeward[parts:], (rest, cut), unit)
    returned, blocks = [], []
    for message, value in zip(homeward, out):
        plane, column = message[0]
        if plane or column:
            value = home(value, plane, column)
        returned.append(value)
        blocks.append(2 * plane + column)
    out_hidden = combine(residual, scores, route_flat, slots, capacity, blocks, returned)
    return (out_hidden.reshape(requests, per, width), decode_cache)


def solution(mesh):
    return jax.shard_map(
        body,
        mesh=mesh,
        in_specs=(
            P("blk", "tok", None),
            P(),
            P(),
            P(),
            P("blk", "tok", None, None),
            P("blk"),
            P(),
            P(),
            P("tok", "blk", None, None),
            P("blk", None, None, "tok"),
            P("blk", "tok", None),
        ),
        out_specs=(P("blk", "tok", None), P("blk", None, None, "tok")),
        check_vma=False,
    )
```
